256 devices in a mesh: seq: 32 (over z, x_hi, core), mp: 8 (over y, x_lo).
Axes of the slice: x: 4 (x_hi: 2, x_lo: 2; x = x_hi * 2 + x_lo), y: 4, z: 8, core: 2. Of those that a mesh axis runs over, the one named last changes fastest.
Arguments:
- anchor: bfloat16 [8192, 4608], P('seq', 'mp'), may hold values from -6 to 6
- augment: bfloat16 [8192, 2304], P('seq', 'mp'), may hold values from -6 to 6
- proj_weight: bfloat16 [2304, 4608], P(None, 'mp'), may hold values from -0.125 to 0.125
- q_weight: bfloat16 [4608, 2048], P(None, 'mp'), may hold values from -0.09375 to 0.09375
- kv_weight: bfloat16 [4608, 8, 2, 128], P(None, 'mp'), may hold values from -0.09375 to 0.09375
- doc_ids: int32 [8192], P('seq'), may hold values from 0 to 1, never falling along the last dimension, each value on 1 to 6144 neighbouring positions
- d_out: bfloat16 [8192, 2048], P('seq', 'mp'), may hold values from -6 to 6
Outputs:
- attended: bfloat16 [8192, 2048], P('seq', 'mp')
- grad_query: float32 [4608, 2048], P('seq', 'mp')
- grad_kv: float32 [4608, 8, 2, 128], P('seq', 'mp')
- grad_kv_rows: bfloat16 [8192, 8, 2, 128], P('seq', 'mp')
The draws below stay inside these ranges and needn't reach their ends.
Inputs may be any that keep to these rules, and one draw needn't show every extreme that they name: `doc_ids`: document numbers never fall along the sequence; every document has 1 to 6144 tokens.
All inputs are finite; a program needn't handle non-finite values.
Results may differ from the reference program's by a relative error of at most 0.025.
Values may be sent and summed in bfloat16 or wider, within the bound.
A program may use at most 128 MiB of HBM per device.

```python
import math
import jax
import jax.numpy as jnp
import numpy as np
from jax import lax

D = 4608
D_AUG = 2304
HEADS = 16
KVH = 8
HD = 128
DOCS = 2
TOK_DEV = 256
TOKENS = 8192
DOC_MOST = 6144
N_SEQ = 32


def spiked(result, stream_key, source, target, blocks, factor):
    owner, partner = [(jnp.arange(result.shape[position]) // (result.shape[position] // blocks)).reshape([-1 if axis == position else 1 for axis in range(result.ndim)]) for position in (source, target)]
    chosen = jax.random.permutation(stream_key, blocks)[partner]
    strong = (owner == chosen) | (owner == (partner + blocks // 2) % blocks)
    return jnp.where(strong, factor * result, result)


def block_scale(own_key, dims, cuts, least, largest):
    def one(dim, blocks):
        steps = jax.random.uniform(jax.random.fold_in(jax.random.fold_in(own_key, 6), dim), (blocks,), jnp.float32, least / len(cuts), largest / len(cuts))
        return jnp.repeat(jnp.exp(steps), dims[dim] // blocks).reshape((-1,) + (1,) * (len(dims) - dim - 1))

    factor_of = one(*cuts[0])
    for cut in cuts[1:]:
        factor_of = factor_of * one(*cut)
    return factor_of


def split_up(number_of, total, bound, lean):
    portions = [(1 << 20) // math.isqrt(standing ** lean) + 1 for standing in range(2, number_of + 1)]
    surplus, holding = total - bound - (number_of - 1), [1] * (number_of - 1)
    while surplus > 0:
        movable = [i for i in range(number_of - 1) if holding[i] < bound]
        mass, left = sum([portions[i] for i in movable]), surplus
        for i in movable:
            extra = min(bound - holding[i], max(1, left * portions[i] // mass), surplus)
            holding[i] = holding[i] + extra
            surplus = surplus - extra
    return np.array([bound] + holding)


def uneven(stream_key, amount, total, limit, skew):
    if amount == 2:
        one = jax.random.randint(stream_key, (), max(1, total - limit), min(limit, total - 1) + 1)
        return jnp.stack([one, total - one])
    sizes = jnp.asarray(split_up(amount, total, limit, skew), jnp.int32)
    twos = (amount - 1) // 2
    source_of, receiver = sizes[1:1 + 2 * twos:2], sizes[2:2 + 2 * twos:2]
    slack = jnp.minimum(source_of - 1, limit - receiver)
    shifted = jax.random.randint(jax.random.fold_in(stream_key, 1), (twos,), 0, 1 << 20) % (slack + 1)
    sizes = sizes.at[1:1 + 2 * twos:2].set(source_of - shifted).at[2:2 + 2 * twos:2].set(receiver + shifted)
    return sizes[jax.random.permutation(jax.random.fold_in(stream_key, 2), amount)]


def gaussian(own_key, shape, width, reach, pieces=(), kind=jnp.bfloat16):
    gain = block_scale(own_key, shape, pieces, -0.22, 0.18) if pieces else 1.0
    result = jax.random.normal(own_key, shape, jnp.float32) * width * gain
    return jnp.minimum(jnp.maximum(result, -reach), reach).astype(kind)


def noise_with(own_key, dims, scale, limit, pieces, heavy, held_as=jnp.bfloat16):
    entries = scale * jax.random.normal(own_key, dims, jnp.float32)
    if pieces:
        entries = entries * block_scale(own_key, dims, pieces, -0.22, 0.18)
    return jnp.clip(spiked(entries, jax.random.fold_in(own_key, 3), *heavy), -limit, limit).astype(held_as)


def setup_inputs(seed: int = 0) -> dict:
    streams_of = jax.random.split(jax.random.key(seed), 8)
    anchor = noise_with(streams_of[0], (TOKENS, D), 1.0, 6.0, ((0, 32), (1, 8)), (0, 1, 32, 2.75))
    augment = gaussian(streams_of[1], (TOKENS, D_AUG), 1.0, 6.0, ((0, 32), (1, 8)))
    proj_weight = gaussian(streams_of[2], (D_AUG, D), D_AUG ** -0.5, 0.125, ((1, 8),))
    q_weight = gaussian(streams_of[3], (D, HEADS * HD), D ** -0.5, 0.09375, ((1, 8),))
    kv_weight = gaussian(streams_of[4], (D, KVH, 2, HD), D ** -0.5, 0.09375, ((1, 8),))
    doc_ids = jnp.searchsorted(jnp.cumsum(uneven(streams_of[5], DOCS, TOKENS, DOC_MOST, 0)), jnp.arange(TOKENS), side="right").astype(jnp.int32)
    d_out = gaussian(streams_of[6], (TOKENS, HEADS * HD), 1.0, 6.0, ((0, 32), (1, 8)))
    return {"anchor": anchor, "augment": augment, "proj_weight": proj_weight, "q_weight": q_weight, "kv_weight": kv_weight, "doc_ids": doc_ids, "d_out": d_out}


softcap_limit = 50.0
score_scale = 144.0 ** -0.5


def rounded(values_in):
    return lax.optimization_barrier(values_in.astype(jnp.bfloat16)).astype(jnp.float32)


def reference(anchor, augment, proj_weight, q_weight, kv_weight, doc_ids, d_out):
    projected = jnp.dot(augment, proj_weight, preferred_element_type=jnp.float32).astype(jnp.bfloat16)
    query = jnp.dot(anchor, q_weight, preferred_element_type=jnp.float32).astype(jnp.bfloat16)
    kv_flat = kv_weight.reshape(D, KVH * 2 * HD)
    key_value = jnp.dot(projected, kv_flat, preferred_element_type=jnp.float32).astype(jnp.bfloat16)
    key_value = key_value.reshape(TOKENS, KVH, 2, HD)
    all_keys = key_value[:, :, 0].astype(jnp.float32)
    all_values = key_value[:, :, 1].astype(jnp.float32)
    group = HEADS // KVH
    key_pos = jnp.arange(TOKENS, dtype=jnp.int32)
    query_blocks = query.reshape(N_SEQ, TOK_DEV, KVH, group, HD)
    grad_blocks = d_out.reshape(N_SEQ, TOK_DEV, KVH, group, HD)
    doc_blocks = doc_ids.reshape(N_SEQ, TOK_DEV)
    anchor_blocks = anchor.reshape(N_SEQ, TOK_DEV, D)

    def per_block(carry, inputs):
        kv_total, query_total = carry
        query_heads, grad_heads, block_docs, block_anchor, index = inputs
        query_pos = index * TOK_DEV + jnp.arange(TOK_DEV, dtype=jnp.int32)
        query_f = query_heads.astype(jnp.float32)
        grad_f = grad_heads.astype(jnp.float32)
        raw = jnp.einsum("tkgd,ukd->kgtu", query_f, all_keys) * score_scale
        capped = softcap_limit * jnp.tanh(raw / softcap_limit)
        allowed = (key_pos[None, :] <= query_pos[:, None]) & (doc_ids[None, :] == block_docs[:, None])
        weights = jnp.where(allowed, jnp.exp(capped), 0.0)
        denom = jnp.sum(weights, axis=-1)
        numer = jnp.einsum("kgtu,ukd->tkgd", rounded(weights), all_values)
        attended = (numer / jnp.transpose(denom, (2, 0, 1))[..., None]).astype(jnp.bfloat16)
        delta = jnp.sum(grad_f * attended.astype(jnp.float32), axis=-1)
        prob = weights / denom[..., None]
        grad_prob = jnp.einsum("tkgd,ukd->kgtu", grad_f, all_values)
        grad_soft = prob * (grad_prob - jnp.transpose(delta, (1, 2, 0))[..., None])
        grad_raw = rounded(grad_soft * (1.0 - (capped / softcap_limit) ** 2) * score_scale)
        grad_q = jnp.einsum("kgtu,ukd->tkgd", grad_raw, all_keys).astype(jnp.bfloat16)
        grad_q = grad_q.reshape(TOK_DEV, HEADS * HD)
        grad_key = jnp.einsum("kgtu,tkgd->ukd", grad_raw, query_f)
        grad_value = jnp.einsum("kgtu,tkgd->ukd", rounded(prob), grad_f)
        kv_total = kv_total + jnp.stack([grad_key, grad_value], axis=2)
        query_total = query_total + rounded(jnp.dot(block_anchor.T, grad_q, preferred_element_type=jnp.float32))
        return (kv_total, query_total), attended.reshape(TOK_DEV, HEADS * HD)

    start = (jnp.zeros((TOKENS, KVH, 2, HD), jnp.float32), jnp.zeros((D, HEADS * HD), jnp.float32))
    block_ids = jnp.arange(N_SEQ, dtype=jnp.int32)
    (kv_total, grad_query), attended_blocks = lax.scan(per_block, start, (query_blocks, grad_blocks, doc_blocks, anchor_blocks, block_ids))
    grad_kv_rows = kv_total.astype(jnp.bfloat16)
    kv_rows = grad_kv_rows.reshape(N_SEQ, TOK_DEV, KVH * 2 * HD)
    projected_blocks = projected.reshape(N_SEQ, TOK_DEV, D)

    def kv_block(total, inputs):
        block_projected, block_grad = inputs
        return total + rounded(jnp.dot(block_projected.T, block_grad, preferred_element_type=jnp.float32)), None

    grad_kv, _ = lax.scan(kv_block, jnp.zeros((D, KVH * 2 * HD), jnp.float32), (projected_blocks, kv_rows))
    return attended_blocks.reshape(TOKENS, HEADS * HD), grad_query, grad_kv.reshape(D, KVH, 2, HD), grad_kv_rows
```

```python
import functools

import jax
import jax.numpy as jnp
from jax import lax
from jax.experimental import pallas as pl
from jax.experimental.pallas import tpu as pltpu
from jax.sharding import PartitionSpec as P

BF = jnp.bfloat16
F32 = jnp.float32
TOK = 256
HD = 128
MESH = pl.DeviceIdType.MESH
LOG2E = 1.4426950408889634
TN = (((0,), (0,)), ((), ()))


def remote(src, dst, send, recv, where):
    return pltpu.make_async_remote_copy(
        src_ref=src, dst_ref=dst, send_sem=send, recv_sem=recv, device_id=where, device_id_type=MESH
    )


def dot(a, b):
    return jnp.dot(a, b, preferred_element_type=F32)


def dot_tn(a, b):
    return lax.dot_general(a, b, TN, preferred_element_type=F32)


def rows_of(ref, start, size):
    return ref.at[pl.ds(pl.multiple_of(start, 16), size)]


def greet(partners):
    barrier = pltpu.get_barrier_semaphore()
    for where in partners:
        pl.semaphore_signal(barrier, inc=1, device_id=where, device_id_type=MESH)
    pl.semaphore_wait(barrier, len(partners))


class FeatureGather:
    def __init__(self, own, buf, rows, send, recv, m):
        self.own, self.buf, self.rows, self.send, self.recv = own, buf, rows, send, recv
        self.m = m
        self.p = m + 1 - 2 * lax.rem(m, 2)
        self.up, self.dn = lax.rem(m + 2, 8), lax.rem(m + 6, 8)

    def part(self, block, half=None):
        if half is None:
            return rows_of(self.buf, block * self.rows, self.rows)
        n = self.rows // 2
        return rows_of(self.buf, block * self.rows + half * n, n)

    def copy(self, i, src, dst, to):
        return remote(src, dst, self.send.at[i], self.recv.at[i], {"mp": to})

    def sent(self, i):
        m, p = self.m, self.p
        a, b = lax.rem(m + 6, 8), lax.rem(m + 2, 8)
        pa, pb = lax.rem(p + 6, 8), lax.rem(p + 2, 8)
        table = [
            (m, None, p), (m, None, self.up), (m, None, self.dn),
            (p, None, self.up), (p, None, self.dn),
            (a, 0, self.up), (b, 1, self.dn),
            (pa, 0, self.up), (pb, 1, self.dn),
        ]
        block, half, to = table[i]
        dst = self.part(block, half)
        return self.copy(i, self.own if i < 3 else dst, dst, to)

    def arrived(self, i):
        m, p = self.m, self.p
        o, po = lax.rem(m + 4, 8), lax.rem(p + 4, 8)
        table = [
            (p, None), (self.dn, None), (self.up, None),
            (lax.rem(p + 6, 8), None), (lax.rem(p + 2, 8), None),
            (o, 0), (o, 1), (po, 0), (po, 1),
        ]
        block, half = table[i]
        dst = self.part(block, half)
        return self.copy(i, dst, dst, p)

    def start(self):
        for i in range(3):
            self.sent(i).start()

    def relay(self, stage):
        if stage == 0:
            self.arrived(0).wait_recv()
            self.sent(3).start()
            self.sent(4).start()
        elif stage == 1:
            self.arrived(1).wait_recv()
            self.sent(5).start()
            self.arrived(2).wait_recv()
            self.sent(6).start()
        elif stage == 2:
            self.arrived(3).wait_recv()
            self.sent(7).start()
            self.arrived(4).wait_recv()
            self.sent(8).start()
        elif stage == 3:
            self.arrived(5).wait_recv()
            self.arrived(6).wait_recv()
        else:
            self.arrived(7).wait_recv()
            self.arrived(8).wait_recv()

    def blocks(self, stage):
        m, p = self.m, self.p
        return [
            [p], [self.dn, self.up], [lax.rem(p + 6, 8), lax.rem(p + 2, 8)],
            [lax.rem(m + 4, 8)], [lax.rem(p + 4, 8)],
        ][stage]

    def drain(self):
        for i in range(9):
            self.sent(i).wait_send()


def feature_kernel(
    aug_ref, anc_ref, pw_hbm, qw_hbm, kw_hbm, doc_ref,
    query_ref, kv_ref, first_ref, anchor_ref, projected_ref,
    augment, pw, qw, kw, acc, cnt_out, cnt_in,
    wsem, asend, arecv, nsend, nrecv, psend, precv, csend, crecv,
):
    s, m = lax.axis_index("seq"), lax.axis_index("mp")
    hyper = []
    for k in range(5):
        bit = lax.rem(s // (1 << k), 2)
        hyper.append(s + (1 << k) * (1 - 2 * bit))
    loads = [
        pltpu.make_async_copy(src, dst, wsem.at[i])
        for i, (src, dst) in enumerate([(pw_hbm, pw), (qw_hbm, qw), (kw_hbm, kw)])
    ]
    for load in loads:
        load.start()
    aug = FeatureGather(aug_ref, augment, 288, asend, arecv, m)
    anc = FeatureGather(anc_ref, anchor_ref, 576, nsend, nrecv, m)
    own_projected = rows_of(projected_ref, m * 576, 576)
    pro = FeatureGather(own_projected, projected_ref, 576, psend, precv, m)
    greet([{"mp": aug.p}, {"mp": aug.up}, {"mp": aug.dn}] + [{"seq": h} for h in hyper])
    aug.start()
    doc = doc_ref[...]
    zeros = jnp.sum((1 - doc).astype(F32), axis=1, keepdims=True)
    cnt_out[0] = jnp.broadcast_to(zeros, (8, 128)).astype(jnp.int32)
    step = lambda k: remote(cnt_out.at[k], cnt_in.at[k], csend.at[k], crecv.at[k], {"seq": hyper[k]})

    def count(k):
        step(k).wait_recv()
        cnt_out[k + 1] = cnt_out[k] + cnt_in[k]
        if k < 4:
            step(k + 1).start()

    step(0).start()
    anc.start()
    rows_of(augment, m * 288, 288)[...] = aug_ref[...]
    rows_of(anchor_ref, m * 576, 576)[...] = anc_ref[...]
    for stage in range(5):
        aug.relay(stage)
        count(stage)
    first_ref[...] = doc * cnt_out[5, 0:1, 0:1]
    loads[0].wait()
    own_projected[...] = dot(pw[...], augment[...]).astype(BF)
    pro.start()
    loads[1].wait()

    def add(buf, weight, block):
        acc[...] += dot_tn(rows_of(buf, block * 576, 576)[...], rows_of(weight, block * 576, 576)[...])

    acc[...] = jnp.zeros_like(acc)
    add(anchor_ref, qw, m)
    for stage in range(5):
        anc.relay(stage)
        if stage == 1:
            pro.relay(0)
        if stage == 3:
            pro.relay(1)
        for block in anc.blocks(stage):
            add(anchor_ref, qw, block)
    query_ref[...] = acc[...].astype(BF)
    loads[2].wait()
    acc[...] = jnp.zeros_like(acc)
    add(projected_ref, kw, m)
    for stage in range(5):
        if stage > 1:
            pro.relay(stage)
        for block in pro.blocks(stage):
            add(projected_ref, kw, block)
    kv_ref[...] = acc[...].astype(BF)
    aug.drain()
    anc.drain()
    pro.drain()
    for k in range(5):
        step(k).wait_send()


def feature_call(aug_t, anc_t, pw_t, q_weight, kv_flat, doc):
    dma = pltpu.SemaphoreType.DMA
    vmem = pl.BlockSpec(memory_space=pltpu.VMEM)
    hbm = pl.BlockSpec(memory_space=pl.ANY)
    return pl.pallas_call(
        feature_kernel,
        out_shape=[
            jax.ShapeDtypeStruct((TOK, 256), BF),
            jax.ShapeDtypeStruct((TOK, 256), BF),
            jax.ShapeDtypeStruct((1, TOK), jnp.int32),
            jax.ShapeDtypeStruct((4608, TOK), BF),
            jax.ShapeDtypeStruct((4608, TOK), BF),
        ],
        in_specs=[vmem, vmem, hbm, hbm, hbm, vmem],
        out_specs=[vmem] * 5,
        scratch_shapes=[
            pltpu.VMEM((2304, TOK), BF),
            pltpu.VMEM((576, 2304), BF),
            pltpu.VMEM((4608, 256), BF),
            pltpu.VMEM((4608, 256), BF),
            pltpu.VMEM((TOK, 256), F32),
            pltpu.VMEM((6, 8, 128), jnp.int32),
            pltpu.VMEM((5, 8, 128), jnp.int32),
            dma((3,)), dma((9,)), dma((9,)), dma((9,)), dma((9,)), dma((9,)), dma((9,)),
            dma((5,)), dma((5,)),
        ],
        compiler_params=pltpu.CompilerParams(
            collective_id=1, has_side_effects=True, vmem_limit_bytes=40 * 1024 * 1024
        ),
    )(aug_t, anc_t, pw_t, q_weight, kv_flat, doc)


def needed(t, z):
    return (t >= 0) & (z <= 7) & ((t >= 2) | (z <= 5))


def sequence_kernel(
    query_ref, kv_ref, dout_ref, first_ref, anchor_ref, projected_ref,
    att_ref, gq_ref, gkv_ref, rows_ref,
    kvs, q_n, q_t, do_n, do_t, num, den, first, place, delta, dq_t,
    mine, tosib, fromsib, ringout, ringin, xout, xin, grads,
    wsib_out, wsib_in, wd_out, wd_in, wu_out, wu_in, wx_out, wx_in, wacc,
    up_s, up_r, sb_s, sb_r, xp_s, xp_r, gs_s, gs_r, rg_s, rg_r, xg_s, xg_r,
    ws_s, ws_r, wd_s, wd_r, wu_s, wu_r, wx_s, wx_r,
):
    s = lax.axis_index("seq")
    z, xh, c = s // 4, lax.rem(s // 2, 2), lax.rem(s, 2)
    sib = {"seq": s + 1 - 2 * c}
    xp_id = s + 2 - 4 * xh
    xp = {"seq": xp_id}
    up, dn = {"seq": lax.rem(s + 4, 32)}, {"seq": lax.rem(s + 28, 32)}
    greet([sib, xp, up, dn])

    def block_copy(src, block, send, recv, where):
        return remote(src, kvs.at[block], send, recv, where)

    def lane(t, j):
        return 4 * t + 2 * j + c

    def to_up(g, j, src=None):
        b = lane(z - g, j)
        return block_copy(kvs.at[b] if src is None else src, b, up_s.at[g, j], up_r.at[g, j], up)

    def to_sib(g, j, src=None):
        b = lane(z - g, j)
        return block_copy(kvs.at[b] if src is None else src, b, sb_s.at[g, j], sb_r.at[g, j], sib)

    def from_sib(g, j):
        b = 4 * (z - g) + 2 * j + 1 - c
        return block_copy(kvs.at[b], b, sb_s.at[g, j], sb_r.at[g, j], sib)

    def from_dn(g, j):
        b = lane(z - g, j)
        return block_copy(kvs.at[b], b, up_s.at[g - 1, j], up_r.at[g - 1, j], dn)

    def up_needs(g):
        return needed(z - g, z + 1)

    to_xp = block_copy(kv_ref, s, xp_s, xp_r, xp)
    from_xp = block_copy(kvs.at[xp_id], xp_id, xp_s, xp_r, xp)
    to_xp.start()

    @pl.when(up_needs(0))
    def _():
        to_up(0, xh, kv_ref).start()

    to_sib(0, xh, kv_ref).start()
    kvs[s] = kv_ref[...]
    lanes = lax.broadcasted_iota(jnp.int32, (1, 2 * TOK), 1)
    place[...] = lax.rem(lanes, TOK) + s * TOK
    for h in range(2):
        cut = slice(h * TOK, (h + 1) * TOK)
        head = slice(h * HD, (h + 1) * HD)
        first[:, cut] = first_ref[...]
        q_n[cut, :] = query_ref[:, head]
        do_n[cut, :] = dout_ref[:, head]
        q_t[:, cut] = query_ref[:, head].T
        do_t[:, cut] = dout_ref[:, head].T
    num[...] = jnp.zeros_like(num)
    den[...] = jnp.zeros_like(den)
    dq_t[...] = jnp.zeros_like(dq_t)
    from_xp.wait_recv()

    @pl.when(up_needs(0))
    def _():
        to_up(0, 1 - xh).start()

    to_sib(0, 1 - xh).start()

    def scores(block):
        k, v = kvs[block, :, :HD], kvs[block, :, HD:]
        th = jnp.tanh(dot(k, q_t[...]) * (1.0 / 600.0))
        pos = block * TOK + lax.broadcasted_iota(jnp.int32, (TOK, 2 * TOK), 0)
        allowed = (pos >= first[...]) & (pos <= place[...])
        return k, v, th, jnp.where(allowed, jnp.exp2(th * (50.0 * LOG2E)), 0.0)

    def forward(g):
        def one(b, carry):
            block = 4 * (z - g) + b

            @pl.when(block <= s)
            def _():
                _, v, _, w = scores(block)
                den[...] += jnp.sum(w, axis=0, keepdims=True)
                num[...] += dot_tn(v, w.astype(BF))

            return carry

        lax.fori_loop(0, 4, one, 0)

    def forward_step(g, carry):
        @pl.when(needed(z - g, z))
        def _():
            @pl.when(g > 0)
            def _():
                for j in range(2):
                    from_dn(g, j).wait_recv()

                    @pl.when(up_needs(g))
                    def _():
                        to_up(g, j).start()

                    to_sib(g, j).start()

            for j in range(2):
                from_sib(g, j).wait_recv()
            forward(g)

        return carry

    lax.fori_loop(0, 6, forward_step, 0)

    attended = (num[...] * (1.0 / den[...])).astype(BF)
    delta[...] = jnp.sum(do_t[...].astype(F32) * attended.astype(F32), axis=0, keepdims=True)
    den[...] = 1.0 / den[...]
    for h in range(2):
        att_ref[:, h * HD:(h + 1) * HD] = attended[:, h * TOK:(h + 1) * TOK].T

    def ring_out(g, j):
        return remote(ringout.at[g - 1, j], ringin.at[g - 1, j], rg_s.at[g - 1, j], rg_r.at[g - 1, j], dn)

    def ring_in(g, j):
        return remote(ringout.at[g, j], ringin.at[g, j], rg_s.at[g, j], rg_r.at[g, j], up)

    def sib_grad(g, j):
        return remote(tosib.at[g, j], fromsib.at[g, j], gs_s.at[g, j], gs_r.at[g, j], sib)

    def backward(block, write):
        k, v, th, w = scores(block)
        prob = w * den[...]
        soft = prob * (dot(v, do_t[...]) - delta[...])
        raw = (soft * ((1.0 - th * th) * (1.0 / 12.0))).astype(BF)
        write(dot(raw, q_n[...]), dot(prob.astype(BF), do_n[...]))
        dq_t[...] += dot_tn(k, raw)

    def contributions(g):
        def for_sib(j, carry):
            block = 4 * (z - g) + 2 * j + 1 - c

            @pl.when(block <= s)
            def _():
                def write(gk, gv):
                    tosib[g, j, :, :HD] = gk.astype(BF)
                    tosib[g, j, :, HD:] = gv.astype(BF)

                backward(block, write)

            @pl.when(block > s)
            def _():
                tosib[g, j] = jnp.zeros((TOK, 256), BF)

            sib_grad(g, j).start()
            return carry

        def for_me(j, carry):
            block = lane(z - g, j)

            @pl.when(block <= s)
            def _():
                def write(gk, gv):
                    mine[j, :, :HD] = gk
                    mine[j, :, HD:] = gv

                backward(block, write)

            @pl.when(block > s)
            def _():
                mine[j] = jnp.zeros((TOK, 256), F32)

            return carry

        lax.fori_loop(0, 2, for_sib, 0)
        lax.fori_loop(0, 2, for_me, 0)

    def sum_up(g, j):
        sib_grad(g, j).wait_recv()
        mine[j] += fromsib[g, j].astype(F32)

        @pl.when(up_needs(g))
        def _():
            ring_in(g, j).wait_recv()
            mine[j] += ringin[g, j].astype(F32)

    def backward_step(i, carry):
        g = 5 - i

        @pl.when(needed(z - g, z))
        def _():
            contributions(g)
            for j in range(2):
                sum_up(g, j)
                ringout[g - 1, j] = mine[j].astype(BF)
                ring_out(g, j).start()

        return carry

    lax.fori_loop(0, 5, backward_step, 0)
    contributions(0)

    def weight(n, act):
        grad = grads.at[n]

        def partial(t, j, core):
            return dot(rows_of(act, t * 576 + j * 288 + core * 144, 144)[...], grad[...])

        def sib_copy(t):
            return remote(wsib_out.at[n, t], wsib_in.at[n, t], ws_s.at[n, t], ws_r.at[n, t], sib)

        def target(k, way):
            return lax.rem(z + 4 + k, 8) if way == 0 else lax.rem(z + 11 - k, 8)

        def send_all():
            def one(i, carry):
                t = lax.rem(z + 4 + 7 * lax.rem(i, 2) * (i // 2 + 1) + (1 - lax.rem(i, 2)) * (i // 2), 8)
                for j in range(2):
                    wsib_out[n, t, j] = partial(t, j, 1 - c).astype(BF)
                sib_copy(t).start()
                return carry

            lax.fori_loop(0, 8, one, 0)

        def hop(k, way):
            out, into = (wd_out, wd_in) if way == 0 else (wu_out, wu_in)
            ss, rr = (wd_s, wd_r) if way == 0 else (wu_s, wu_r)
            return remote(out.at[n, k], into.at[n, k], ss.at[n, k], rr.at[n, k], dn if way == 0 else up)

        def hop_step(k, way):
            out, into = (wd_out, wd_in) if way == 0 else (wu_out, wu_in)
            t = target(k, way)
            sib_copy(t).wait_recv()
            for j in range(2):
                wacc[j] = partial(t, j, c) + wsib_in[n, t, j].astype(F32)

            @pl.when(k > 0)
            def _():
                hop(k - 1, way).wait_recv()
                for j in range(2):
                    wacc[j] += into[n, k - 1, j].astype(F32)

            for j in range(2):
                out[n, k, j] = wacc[j].astype(BF)
            hop(k, way).start()

        def step(k):
            hop_step(k, 0)

            @pl.when(k < 3)
            def _():
                hop_step(k, 1)

        def x_copy():
            return remote(wx_out.at[n], wx_in.at[n], wx_s.at[n], wx_r.at[n], xp)

        def meet():
            sib_copy(z).wait_recv()
            hop(3, 0).wait_recv()
            hop(2, 1).wait_recv()
            for j in range(2):
                wacc[j] = (
                    partial(z, j, c) + wsib_in[n, z, j].astype(F32)
                    + wd_in[n, 3, j].astype(F32) + wu_in[n, 2, j].astype(F32)
                )
            wx_out[n] = wacc[1 - xh].astype(BF)
            x_copy().start()
            return wacc[xh]

        def drain():
            for t in range(8):
                sib_copy(t).wait_send()
            for k in range(4):
                hop(k, 0).wait_send()
            for k in range(3):
                hop(k, 1).wait_send()
            x_copy().wait_send()

        return send_all, step, meet, x_copy, drain

    wq = weight(0, anchor_ref)
    wkv = weight(1, projected_ref)
    for h in range(2):
        grads[0, :, h * HD:(h + 1) * HD] = dq_t[:, h * TOK:(h + 1) * TOK].T.astype(BF)
    wq[0]()
    wq[1](0)
    for j in range(2):
        sum_up(0, j)
    xout[...] = mine[1 - xh].astype(BF)
    x_rows = remote(xout, xin, xg_s, xg_r, xp)
    x_rows.start()
    wq[1](1)
    x_rows.wait_recv()
    grads[1] = (mine[xh] + xin[...].astype(F32)).astype(BF)
    rows_ref[...] = grads[1]
    wkv[0]()

    def both(k, carry):
        wkv[1](k)
        wq[1](k + 2)
        return carry

    lax.fori_loop(0, 2, both, 0)
    own_q = wq[2]()
    gq_ref[...] = own_q
    wkv[1](2)
    wkv[1](3)
    own_kv = wkv[2]()
    gkv_ref[...] = own_kv
    wq[3]().wait_recv()
    gq_ref[...] += wx_in[0].astype(F32)
    wkv[3]().wait_recv()
    gkv_ref[...] += wx_in[1].astype(F32)

    to_xp.wait_send()
    x_rows.wait_send()
    wq[4]()
    wkv[4]()

    def drained(g, carry):
        @pl.when(needed(z - g, z))
        def _():
            for j in range(2):
                to_sib(g, j).wait_send()
                sib_grad(g, j).wait_send()

                @pl.when(up_needs(g))
                def _():
                    to_up(g, j).wait_send()

                @pl.when(g > 0)
                def _():
                    ring_out(g, j).wait_send()

        return carry

    lax.fori_loop(0, 6, drained, 0)


def sequence_call(query, kv, d_out, first, anchor, projected):
    dma = pltpu.SemaphoreType.DMA
    vmem = pl.BlockSpec(memory_space=pltpu.VMEM)
    two = lambda n: [dma(n), dma(n)]
    return pl.pallas_call(
        sequence_kernel,
        out_shape=[
            jax.ShapeDtypeStruct((TOK, 256), BF),
            jax.ShapeDtypeStruct((144, 256), F32),
            jax.ShapeDtypeStruct((144, 256), F32),
            jax.ShapeDtypeStruct((TOK, 256), BF),
        ],
        in_specs=[vmem] * 6,
        out_specs=[vmem] * 4,
        scratch_shapes=[
            pltpu.VMEM((32, TOK, 256), BF),
            pltpu.VMEM((512, HD), BF), pltpu.VMEM((HD, 512), BF),
            pltpu.VMEM((512, HD), BF), pltpu.VMEM((HD, 512), BF),
            pltpu.VMEM((HD, 512), F32), pltpu.VMEM((1, 512), F32),
            pltpu.VMEM((1, 512), jnp.int32), pltpu.VMEM((1, 512), jnp.int32),
            pltpu.VMEM((1, 512), F32), pltpu.VMEM((HD, 512), F32),
            pltpu.VMEM((2, TOK, 256), F32),
            pltpu.VMEM((6, 2, TOK, 256), BF), pltpu.VMEM((6, 2, TOK, 256), BF),
            pltpu.VMEM((5, 2, TOK, 256), BF), pltpu.VMEM((5, 2, TOK, 256), BF),
            pltpu.VMEM((TOK, 256), BF), pltpu.VMEM((TOK, 256), BF),
            pltpu.VMEM((2, TOK, 256), BF),
            pltpu.VMEM((2, 8, 2, 144, 256), BF), pltpu.VMEM((2, 8, 2, 144, 256), BF),
            pltpu.VMEM((2, 4, 2, 144, 256), BF), pltpu.VMEM((2, 4, 2, 144, 256), BF),
            pltpu.VMEM((2, 3, 2, 144, 256), BF), pltpu.VMEM((2, 3, 2, 144, 256), BF),
            pltpu.VMEM((2, 144, 256), BF), pltpu.VMEM((2, 144, 256), BF),
            pltpu.VMEM((2, 144, 256), F32),
            *two((5, 2)), *two((6, 2)), *two(()), *two((6, 2)), *two((5, 2)), *two(()),
            *two((2, 8)), *two((2, 4)), *two((2, 3)), *two((2,)),
        ],
        compiler_params=pltpu.CompilerParams(
            collective_id=2, has_side_effects=True, vmem_limit_bytes=56 * 1024 * 1024
        ),
    )(query, kv, d_out, first, anchor, projected)


def body(anchor, augment, proj_weight, q_weight, kv_weight, doc_ids, d_out):
    query, kv, first, anchor_t, projected_t = feature_call(
        augment.T, anchor.T, proj_weight.T, q_weight,
        kv_weight.reshape(kv_weight.shape[0], -1), doc_ids.reshape(1, -1),
    )
    attended, grad_q, grad_kv, rows = sequence_call(query, kv, d_out, first, anchor_t, projected_t)
    return attended, grad_q, grad_kv.reshape(144, 1, 2, HD), rows.reshape(TOK, 1, 2, HD)


def solution(mesh):
    placed = (
        P("seq", "mp"), P("seq", "mp"), P(None, "mp"), P(None, "mp"),
        P(None, "mp", None, None), P("seq"), P("seq", "mp"),
    )
    return jax.shard_map(
        body,
        mesh=mesh,
        in_specs=placed,
        out_specs=(
            P("seq", "mp"), P("seq", "mp"),
            P("seq", "mp", None, None), P("seq", "mp", None, None),
        ),
        check_vma=False,
    )
```

```python
import functools

import jax
import jax.numpy as jnp
from jax import lax
from jax.experimental import pallas as pl
from jax.experimental.pallas import tpu as pltpu
from jax.sharding import PartitionSpec as P

BF = jnp.bfloat16
F32 = jnp.float32
TOK = 256
HD = 128
MESH = pl.DeviceIdType.MESH
LOG2E = 1.4426950408889634
TN = (((0,), (0,)), ((), ()))


def remote(src, dst, send, recv, where):
    return pltpu.make_async_remote_copy(
        src_ref=src, dst_ref=dst, send_sem=send, recv_sem=recv, device_id=where, device_id_type=MESH
    )


def dot(a, b):
    return jnp.dot(a, b, preferred_element_type=F32)


def dot_tn(a, b):
    return lax.dot_general(a, b, TN, preferred_element_type=F32)


def rows_of(ref, start, size):
    return ref.at[pl.ds(pl.multiple_of(start, 16), size)]


def greet(partners):
    barrier = pltpu.get_barrier_semaphore()
    for where in partners:
        pl.semaphore_signal(barrier, inc=1, device_id=where, device_id_type=MESH)
    pl.semaphore_wait(barrier, len(partners))


class FeatureGather:
    def __init__(self, own, buf, rows, send, recv, m):
        self.own, self.buf, self.rows, self.send, self.recv = own, buf, rows, send, recv
        self.m = m
        self.p = m + 1 - 2 * lax.rem(m, 2)
        self.up, self.dn = lax.rem(m + 2, 8), lax.rem(m + 6, 8)

    def part(self, block, half=None):
        if half is None:
            return rows_of(self.buf, block * self.rows, self.rows)
        n = self.rows // 2
        return rows_of(self.buf, block * self.rows + half * n, n)

    def copy(self, i, src, dst, to):
        return remote(src, dst, self.send.at[i], self.recv.at[i], {"mp": to})

    def sent(self, i):
        m, p = self.m, self.p
        a, b = lax.rem(m + 6, 8), lax.rem(m + 2, 8)
        pa, pb = lax.rem(p + 6, 8), lax.rem(p + 2, 8)
        table = [
            (m, None, p), (m, None, self.up), (m, None, self.dn),
            (p, None, self.up), (p, None, self.dn),
            (a, 0, self.up), (b, 1, self.dn),
            (pa, 0, self.up), (pb, 1, self.dn),
        ]
        block, half, to = table[i]
        dst = self.part(block, half)
        return self.copy(i, self.own if i < 3 else dst, dst, to)

    def arrived(self, i):
        m, p = self.m, self.p
        o, po = lax.rem(m + 4, 8), lax.rem(p + 4, 8)
        table = [
            (p, None), (self.dn, None), (self.up, None),
            (lax.rem(p + 6, 8), None), (lax.rem(p + 2, 8), None),
            (o, 0), (o, 1), (po, 0), (po, 1),
        ]
        block, half = table[i]
        dst = self.part(block, half)
        return self.copy(i, dst, dst, p)

    def start(self):
        for i in range(3):
            self.sent(i).start()

    def relay(self, stage):
        if stage == 0:
            self.arrived(0).wait_recv()
            self.sent(3).start()
            self.sent(4).start()
        elif stage == 1:
            self.arrived(1).wait_recv()
            self.sent(5).start()
            self.arrived(2).wait_recv()
            self.sent(6).start()
        elif stage == 2:
            self.arrived(3).wait_recv()
            self.sent(7).start()
            self.arrived(4).wait_recv()
            self.sent(8).start()
        elif stage == 3:
            self.arrived(5).wait_recv()
            self.arrived(6).wait_recv()
        else:
            self.arrived(7).wait_recv()
            self.arrived(8).wait_recv()

    def blocks(self, stage):
        m, p = self.m, self.p
        return [
            [p], [self.dn, self.up], [lax.rem(p + 6, 8), lax.rem(p + 2, 8)],
            [lax.rem(m + 4, 8)], [lax.rem(p + 4, 8)],
        ][stage]

    def drain(self):
        for i in range(9):
            self.sent(i).wait_send()


def needed(t, z):
    return (t >= 0) & (z <= 7) & ((t >= 2) | (z <= 5))


def step_kernel(
    aug_ref, anc_ref, pw_hbm, qw_hbm, kw_hbm, doc_ref, dout_ref,
    att_ref, gq_ref, gkv_ref, rows_ref,
    augment, anchor, projected, pw, qw, kw, kw_pairs, pairs, acc, kv_ref, cnt_out, cnt_in,
    kvs, q_n, q_t, do_n, do_t, num, den, first, place, delta, dq_t,
    mine, tosib, fromsib, ringout, ringin, xout, xin, grads,
    wsib_out, wsib_in, wd_out, wd_in, wu_out, wu_in, wx_out, wx_in, wacc,
    wsem, asend, arecv, nsend, nrecv, psend, precv, csend, crecv,
    up_s, up_r, sb_s, sb_r, xp_s, xp_r, gs_s, gs_r, rg_s, rg_r, xg_s, xg_r,
    ws_s, ws_r, wd_s, wd_r, wu_s, wu_r, wx_s, wx_r,
):
    s, m = lax.axis_index("seq"), lax.axis_index("mp")
    z, xh, c = s // 4, lax.rem(s // 2, 2), lax.rem(s, 2)
    sib = {"seq": s + 1 - 2 * c}
    xp_id = s + 2 - 4 * xh
    xp = {"seq": xp_id}
    up, dn = {"seq": lax.rem(s + 4, 32)}, {"seq": lax.rem(s + 28, 32)}
    hyper = []
    for k in range(5):
        bit = lax.rem(s // (1 << k), 2)
        hyper.append(s + (1 << k) * (1 - 2 * bit))
    loads = [
        pltpu.make_async_copy(src, dst, wsem.at[i])
        for i, (src, dst) in enumerate([(pw_hbm, pw), (qw_hbm, qw), (kw_hbm, kw_pairs)])
    ]
    for load in loads:
        load.start()
    aug = FeatureGather(aug_ref, augment, 288, asend, arecv, m)
    anc = FeatureGather(anc_ref, anchor, 576, nsend, nrecv, m)
    own_projected = rows_of(projected, m * 576, 576)
    pro = FeatureGather(own_projected, projected, 576, psend, precv, m)
    greet([{"mp": aug.p}, {"mp": aug.up}, {"mp": aug.dn}, up, dn] + [{"seq": h} for h in hyper])

    aug.start()
    doc = doc_ref[...]
    zeros = jnp.sum((1 - doc).astype(F32), axis=1, keepdims=True)
    cnt_out[0] = jnp.broadcast_to(zeros, (8, 128)).astype(jnp.int32)

    def step(k):
        return remote(cnt_out.at[k], cnt_in.at[k], csend.at[k], crecv.at[k], {"seq": hyper[k]})

    def count(k):
        step(k).wait_recv()
        cnt_out[k + 1] = cnt_out[k] + cnt_in[k]
        if k < 4:
            step(k + 1).start()

    step(0).start()
    rows_of(augment, m * 288, 288)[...] = aug_ref[...]
    rows_of(anchor, m * 576, 576)[...] = anc_ref[...]
    loads[2].wait()

    def unpair(i, carry):
        pairs[...] = kw_pairs[pl.ds(pl.multiple_of(i * 1152, 1152), 1152), :].astype(F32)
        for half in range(2):
            out = pairs[pl.ds(half, 576, stride=2), :].astype(BF)
            kw[pl.ds(pl.multiple_of(i * 576, 576), 576), half * HD:(half + 1) * HD] = out
        return carry

    for stage in range(5):
        aug.relay(stage)
        count(stage)
        lax.fori_loop(2 * stage, min(2 * stage + 2, 8), unpair, 0)
    here = doc * cnt_out[5, 0:1, 0:1]
    lanes = lax.broadcasted_iota(jnp.int32, (1, 2 * TOK), 1)
    place[...] = lax.rem(lanes, TOK) + s * TOK
    for h in range(2):
        cut = slice(h * TOK, (h + 1) * TOK)
        head = slice(h * HD, (h + 1) * HD)
        first[:, cut] = here
        do_n[cut, :] = dout_ref[:, head]
        do_t[:, cut] = dout_ref[:, head].T
    loads[0].wait()
    loads[1].wait()
    own_projected[...] = dot(pw[...], augment[...]).astype(BF)
    pro.start()

    def add(buf, weight, block):
        acc[...] += dot_tn(rows_of(buf, block * 576, 576)[...], rows_of(weight, block * 576, 576)[...])

    acc[...] = jnp.zeros_like(acc)
    add(projected, kw, m)
    for stage in range(5):
        pro.relay(stage)
        if stage == 2:
            anc.start()
        for block in pro.blocks(stage):
            add(projected, kw, block)
    kv_ref[...] = acc[...].astype(BF)

    def block_copy(src, block, send, recv, where):
        return remote(src, kvs.at[block], send, recv, where)

    def lane(t, j):
        return 4 * t + 2 * j + c

    def to_up(g, j, src=None):
        b = lane(z - g, j)
        return block_copy(kvs.at[b] if src is None else src, b, up_s.at[g, j], up_r.at[g, j], up)

    def to_sib(g, j, src=None):
        b = lane(z - g, j)
        return block_copy(kvs.at[b] if src is None else src, b, sb_s.at[g, j], sb_r.at[g, j], sib)

    def from_sib(g, j):
        b = 4 * (z - g) + 2 * j + 1 - c
        return block_copy(kvs.at[b], b, sb_s.at[g, j], sb_r.at[g, j], sib)

    def from_dn(g, j):
        b = lane(z - g, j)
        return block_copy(kvs.at[b], b, up_s.at[g - 1, j], up_r.at[g - 1, j], dn)

    def up_needs(g):
        return needed(z - g, z + 1)

    to_xp = block_copy(kv_ref, s, xp_s, xp_r, xp)
    from_xp = block_copy(kvs.at[xp_id], xp_id, xp_s, xp_r, xp)
    to_xp.start()

    @pl.when(up_needs(0))
    def _():
        to_up(0, xh, kv_ref).start()

    to_sib(0, xh, kv_ref).start()
    kvs[s] = kv_ref[...]
    num[...] = jnp.zeros_like(num)
    den[...] = jnp.zeros_like(den)
    dq_t[...] = jnp.zeros_like(dq_t)
    from_xp.wait_recv()

    @pl.when(up_needs(0))
    def _():
        to_up(0, 1 - xh).start()

    to_sib(0, 1 - xh).start()

    def scores(block):
        k, v = kvs[block, :, :HD], kvs[block, :, HD:]
        th = jnp.tanh(dot(k, q_t[...]) * (1.0 / 600.0))
        pos = block * TOK + lax.broadcasted_iota(jnp.int32, (TOK, 2 * TOK), 0)
        allowed = (pos >= first[...]) & (pos <= place[...])
        return k, v, th, jnp.where(allowed, jnp.exp2(th * (50.0 * LOG2E)), 0.0)

    def forward(g):
        def one(b, carry):
            block = 4 * (z - g) + b

            @pl.when(block <= s)
            def _():
                _, v, _, w = scores(block)
                den[...] += jnp.sum(w, axis=0, keepdims=True)
                num[...] += dot_tn(v, w.astype(BF))

            return carry

        lax.fori_loop(0, 4, one, 0)

    def pass_on(g):
        for j in range(2):
            from_dn(g, j).wait_recv()

            @pl.when(up_needs(g))
            def _():
                to_up(g, j).start()

            to_sib(g, j).start()

    acc[...] = jnp.zeros_like(acc)
    add(anchor, qw, m)
    for stage in range(5):
        anc.relay(stage)
        for block in anc.blocks(stage):
            add(anchor, qw, block)
        if stage in (1, 2):
            @pl.when(needed(z - stage, z))
            def _():
                pass_on(stage)

    query = acc[...].astype(BF)
    for h in range(2):
        cut = slice(h * TOK, (h + 1) * TOK)
        head = slice(h * HD, (h + 1) * HD)
        q_n[cut, :] = query[:, head]
        q_t[:, cut] = query[:, head].T

    def forward_step(g, carry):
        @pl.when(needed(z - g, z))
        def _():
            @pl.when(g > 2)
            def _():
                pass_on(g)

            for j in range(2):
                from_sib(g, j).wait_recv()
            forward(g)

        return carry

    lax.fori_loop(0, 6, forward_step, 0)

    attended = (num[...] * (1.0 / den[...])).astype(BF)
    delta[...] = jnp.sum(do_t[...].astype(F32) * attended.astype(F32), axis=0, keepdims=True)
    den[...] = 1.0 / den[...]
    for h in range(2):
        att_ref[:, h * HD:(h + 1) * HD] = attended[:, h * TOK:(h + 1) * TOK].T

    def ring_out(g, j):
        return remote(ringout.at[g - 1, j], ringin.at[g - 1, j], rg_s.at[g - 1, j], rg_r.at[g - 1, j], dn)

    def ring_in(g, j):
        return remote(ringout.at[g, j], ringin.at[g, j], rg_s.at[g, j], rg_r.at[g, j], up)

    def sib_grad(g, j):
        return remote(tosib.at[g, j], fromsib.at[g, j], gs_s.at[g, j], gs_r.at[g, j], sib)

    def backward(block, write):
        k, v, th, w = scores(block)
        prob = w * den[...]
        soft = prob * (dot(v, do_t[...]) - delta[...])
        raw = (soft * ((1.0 - th * th) * (1.0 / 12.0))).astype(BF)
        write(dot(raw, q_n[...]), dot(prob.astype(BF), do_n[...]))
        dq_t[...] += dot_tn(k, raw)

    def contributions(g):
        def for_sib(j, carry):
            block = 4 * (z - g) + 2 * j + 1 - c

            @pl.when(block <= s)
            def _():
                def write(gk, gv):
                    tosib[g, j, :, :HD] = gk.astype(BF)
                    tosib[g, j, :, HD:] = gv.astype(BF)

                backward(block, write)

            @pl.when(block > s)
            def _():
                tosib[g, j] = jnp.zeros((TOK, 256), BF)

            sib_grad(g, j).start()
            return carry

        def for_me(j, carry):
            block = lane(z - g, j)

            @pl.when(block <= s)
            def _():
                def write(gk, gv):
                    mine[j, :, :HD] = gk
                    mine[j, :, HD:] = gv

                backward(block, write)

            @pl.when(block > s)
            def _():
                mine[j] = jnp.zeros((TOK, 256), F32)

            return carry

        lax.fori_loop(0, 2, for_sib, 0)
        lax.fori_loop(0, 2, for_me, 0)

    def sum_up(g, j):
        sib_grad(g, j).wait_recv()
        mine[j] += fromsib[g, j].astype(F32)

        @pl.when(up_needs(g))
        def _():
            ring_in(g, j).wait_recv()
            mine[j] += ringin[g, j].astype(F32)

    def backward_step(i, carry):
        g = 5 - i

        @pl.when(needed(z - g, z))
        def _():
            contributions(g)
            for j in range(2):
                sum_up(g, j)
                ringout[g - 1, j] = mine[j].astype(BF)
                ring_out(g, j).start()

        return carry

    lax.fori_loop(0, 5, backward_step, 0)
    contributions(0)

    def weight(n, act):
        grad = grads.at[n]

        def partial(t, j, core):
            return dot(rows_of(act, t * 576 + j * 288 + core * 144, 144)[...], grad[...])

        def sib_copy(t):
            return remote(wsib_out.at[n, t], wsib_in.at[n, t], ws_s.at[n, t], ws_r.at[n, t], sib)

        def target(k, way):
            return lax.rem(z + 4 + k, 8) if way == 0 else lax.rem(z + 11 - k, 8)

        def send_all():
            def one(i, carry):
                t = lax.rem(z + 4 + 7 * lax.rem(i, 2) * (i // 2 + 1) + (1 - lax.rem(i, 2)) * (i // 2), 8)
                for j in range(2):
                    wsib_out[n, t, j] = partial(t, j, 1 - c).astype(BF)
                sib_copy(t).start()
                return carry

            lax.fori_loop(0, 8, one, 0)

        def hop(k, way):
            out, into = (wd_out, wd_in) if way == 0 else (wu_out, wu_in)
            ss, rr = (wd_s, wd_r) if way == 0 else (wu_s, wu_r)
            return remote(out.at[n, k], into.at[n, k], ss.at[n, k], rr.at[n, k], dn if way == 0 else up)

        def hop_step(k, way):
            out, into = (wd_out, wd_in) if way == 0 else (wu_out, wu_in)
            t = target(k, way)
            sib_copy(t).wait_recv()
            for j in range(2):
                wacc[j] = partial(t, j, c) + wsib_in[n, t, j].astype(F32)

            @pl.when(k > 0)
            def _():
                hop(k - 1, way).wait_recv()
                for j in range(2):
                    wacc[j] += into[n, k - 1, j].astype(F32)

            for j in range(2):
                out[n, k, j] = wacc[j].astype(BF)
            hop(k, way).start()

        def step(k):
            hop_step(k, 0)

            @pl.when(k < 3)
            def _():
                hop_step(k, 1)

        def x_copy():
            return remote(wx_out.at[n], wx_in.at[n], wx_s.at[n], wx_r.at[n], xp)

        def meet():
            sib_copy(z).wait_recv()
            hop(3, 0).wait_recv()
            hop(2, 1).wait_recv()
            for j in range(2):
                wacc[j] = (
                    partial(z, j, c) + wsib_in[n, z, j].astype(F32)
                    + wd_in[n, 3, j].astype(F32) + wu_in[n, 2, j].astype(F32)
                )
            wx_out[n] = wacc[1 - xh].astype(BF)
            x_copy().start()
            return wacc[xh]

        def drain():
            for t in range(8):
                sib_copy(t).wait_send()
            for k in range(4):
                hop(k, 0).wait_send()
            for k in range(3):
                hop(k, 1).wait_send()
            x_copy().wait_send()

        return send_all, step, meet, x_copy, drain

    wq = weight(0, anchor)
    wkv = weight(1, projected)
    for h in range(2):
        grads[0, :, h * HD:(h + 1) * HD] = dq_t[:, h * TOK:(h + 1) * TOK].T.astype(BF)
    wq[0]()
    wq[1](0)
    for j in range(2):
        sum_up(0, j)
    xout[...] = mine[1 - xh].astype(BF)
    x_rows = remote(xout, xin, xg_s, xg_r, xp)
    x_rows.start()
    wq[1](1)
    x_rows.wait_recv()
    grads[1] = (mine[xh] + xin[...].astype(F32)).astype(BF)
    for half in range(2):
        pairs[pl.ds(half, TOK, stride=2), :] = grads[1, :, half * HD:(half + 1) * HD].astype(F32)
    rows_ref[...] = pairs[:2 * TOK, :].astype(BF)
    wkv[0]()

    def both(k, carry):
        wkv[1](k)
        wq[1](k + 2)
        return carry

    lax.fori_loop(0, 2, both, 0)
    own_q = wq[2]()
    gq_ref[...] = own_q
    wkv[1](2)
    wkv[1](3)
    own_kv = wkv[2]()
    wacc[0] = own_kv
    wq[3]().wait_recv()
    gq_ref[...] += wx_in[0].astype(F32)
    wkv[3]().wait_recv()
    wacc[0] += wx_in[1].astype(F32)
    for half in range(2):
        gkv_ref[pl.ds(half, 144, stride=2), :] = wacc[0, :, half * HD:(half + 1) * HD]

    to_xp.wait_send()
    x_rows.wait_send()
    wq[4]()
    wkv[4]()
    aug.drain()
    anc.drain()
    pro.drain()
    for k in range(5):
        step(k).wait_send()

    def drained(g, carry):
        @pl.when(needed(z - g, z))
        def _():
            for j in range(2):
                to_sib(g, j).wait_send()
                sib_grad(g, j).wait_send()

                @pl.when(up_needs(g))
                def _():
                    to_up(g, j).wait_send()

                @pl.when(g > 0)
                def _():
                    ring_out(g, j).wait_send()

        return carry

    lax.fori_loop(0, 6, drained, 0)


def step_call(aug_t, anc_t, pw_t, q_weight, kv_pairs, doc, d_out):
    dma = pltpu.SemaphoreType.DMA
    vmem = pl.BlockSpec(memory_space=pltpu.VMEM)
    hbm = pl.BlockSpec(memory_space=pl.ANY)
    two = lambda n: [dma(n), dma(n)]
    return pl.pallas_call(
        step_kernel,
        out_shape=[
            jax.ShapeDtypeStruct((TOK, 256), BF),
            jax.ShapeDtypeStruct((144, 256), F32),
            jax.ShapeDtypeStruct((288, HD), F32),
            jax.ShapeDtypeStruct((2 * TOK, HD), BF),
        ],
        in_specs=[vmem, vmem, hbm, hbm, hbm, vmem, vmem],
        out_specs=[vmem] * 4,
        scratch_shapes=[
            pltpu.VMEM((2304, TOK), BF), pltpu.VMEM((4608, TOK), BF), pltpu.VMEM((4608, TOK), BF),
            pltpu.VMEM((576, 2304), BF), pltpu.VMEM((4608, 256), BF), pltpu.VMEM((4608, 256), BF),
            pltpu.VMEM((9216, HD), BF), pltpu.VMEM((1152, HD), F32),
            pltpu.VMEM((TOK, 256), F32), pltpu.VMEM((TOK, 256), BF),
            pltpu.VMEM((6, 8, 128), jnp.int32), pltpu.VMEM((5, 8, 128), jnp.int32),
            pltpu.VMEM((32, TOK, 256), BF),
            pltpu.VMEM((512, HD), BF), pltpu.VMEM((HD, 512), BF),
            pltpu.VMEM((512, HD), BF), pltpu.VMEM((HD, 512), BF),
            pltpu.VMEM((HD, 512), F32), pltpu.VMEM((1, 512), F32),
            pltpu.VMEM((1, 512), jnp.int32), pltpu.VMEM((1, 512), jnp.int32),
            pltpu.VMEM((1, 512), F32), pltpu.VMEM((HD, 512), F32),
            pltpu.VMEM((2, TOK, 256), F32),
            pltpu.VMEM((6, 2, TOK, 256), BF), pltpu.VMEM((6, 2, TOK, 256), BF),
            pltpu.VMEM((5, 2, TOK, 256), BF), pltpu.VMEM((5, 2, TOK, 256), BF),
            pltpu.VMEM((TOK, 256), BF), pltpu.VMEM((TOK, 256), BF),
            pltpu.VMEM((2, TOK, 256), BF),
            pltpu.VMEM((2, 8, 2, 144, 256), BF), pltpu.VMEM((2, 8, 2, 144, 256), BF),
            pltpu.VMEM((2, 4, 2, 144, 256), BF), pltpu.VMEM((2, 4, 2, 144, 256), BF),
            pltpu.VMEM((2, 3, 2, 144, 256), BF), pltpu.VMEM((2, 3, 2, 144, 256), BF),
            pltpu.VMEM((2, 144, 256), BF), pltpu.VMEM((2, 144, 256), BF),
            pltpu.VMEM((2, 144, 256), F32),
            dma((3,)), *two((9,)), *two((9,)), *two((9,)), *two((5,)),
            *two((5, 2)), *two((6, 2)), *two(()), *two((6, 2)), *two((5, 2)), *two(()),
            *two((2, 8)), *two((2, 4)), *two((2, 3)), *two((2,)),
        ],
        compiler_params=pltpu.CompilerParams(
            collective_id=1, has_side_effects=True, vmem_limit_bytes=60 * 1024 * 1024
        ),
    )(aug_t, anc_t, pw_t, q_weight, kv_pairs, doc, d_out)


def hand_over(*refs):
    n = len(refs) // 2
    for src, dst in zip(refs[:n], refs[n:]):
        dst[...] = src[...]


def body(anchor, augment, proj_weight, q_weight, kv_weight, doc_ids, d_out):
    results = step_call(
        augment.T, anchor.T, proj_weight.T, q_weight,
        kv_weight.reshape(-1, HD), doc_ids.reshape(1, -1), d_out,
    )
    attended, grad_q, grad_kv, rows = pl.pallas_call(
        hand_over,
        out_shape=[jax.ShapeDtypeStruct(r.shape, r.dtype) for r in results],
        in_specs=[pl.BlockSpec(memory_space=pltpu.VMEM)] * 4,
        out_specs=[pl.BlockSpec(memory_space=pltpu.VMEM)] * 4,
    )(*results)
    return attended, grad_q, grad_kv.reshape(144, 1, 2, HD), rows.reshape(TOK, 1, 2, HD)


def solution(mesh):
    placed = (
        P("seq", "mp"), P("seq", "mp"), P(None, "mp"), P(None, "mp"),
        P(None, "mp", None, None), P("seq"), P("seq", "mp"),
    )
    return jax.shard_map(
        body,
        mesh=mesh,
        in_specs=placed,
        out_specs=(
            P("seq", "mp"), P("seq", "mp"),
            P("seq", "mp", None, None), P("seq", "mp", None, None),
        ),
        check_vma=False,
    )
```

```python
import functools

import jax
import jax.numpy as jnp
from jax import lax
from jax.experimental import pallas as pl
from jax.experimental.pallas import tpu as pltpu
from jax.sharding import PartitionSpec as P

BF = jnp.bfloat16
F32 = jnp.float32
TOK = 256
HALF = 128
HD = 128
MESH = pl.DeviceIdType.MESH
LOG2E = 1.4426950408889634
TN = (((0,), (0,)), ((), ()))


def remote(src, dst, send, recv, where):
    return pltpu.make_async_remote_copy(
        src_ref=src, dst_ref=dst, send_sem=send, recv_sem=recv, device_id=where, device_id_type=MESH
    )


def dot(a, b):
    return jnp.dot(a, b, preferred_element_type=F32)


def dot_tn(a, b):
    return lax.dot_general(a, b, TN, preferred_element_type=F32)


def rows_of(ref, start, size):
    return ref.at[pl.ds(pl.multiple_of(start, 16), size)]


def greet(partners):
    barrier = pltpu.get_barrier_semaphore()
    for where in partners:
        pl.semaphore_signal(barrier, inc=1, device_id=where, device_id_type=MESH)
    pl.semaphore_wait(barrier, len(partners))


class FeatureGather:
    def __init__(self, own, buf, rows, send, recv, m, lanes=pl.ds(0, TOK)):
        self.own, self.buf, self.rows, self.send, self.recv = own, buf, rows, send, recv
        self.lanes = lanes
        self.m = m
        self.p = m + 1 - 2 * lax.rem(m, 2)
        self.up, self.dn = lax.rem(m + 2, 8), lax.rem(m + 6, 8)

    def part(self, block, half=None):
        n = self.rows if half is None else self.rows // 2
        start = block * self.rows + (half or 0) * n
        return self.buf.at[pl.ds(pl.multiple_of(start, 16), n), self.lanes]

    def copy(self, i, src, dst, to):
        return remote(src, dst, self.send.at[i], self.recv.at[i], {"mp": to})

    def sent(self, i):
        m, p = self.m, self.p
        a, b = lax.rem(m + 6, 8), lax.rem(m + 2, 8)
        pa, pb = lax.rem(p + 6, 8), lax.rem(p + 2, 8)
        table = [
            (m, None, p), (m, None, self.up), (m, None, self.dn),
            (p, None, self.up), (p, None, self.dn),
            (a, 0, self.up), (b, 1, self.dn),
            (pa, 0, self.up), (pb, 1, self.dn),
        ]
        block, half, to = table[i]
        dst = self.part(block, half)
        return self.copy(i, self.own if i < 3 else dst, dst, to)

    def arrived(self, i):
        m, p = self.m, self.p
        o, po = lax.rem(m + 4, 8), lax.rem(p + 4, 8)
        table = [
            (p, None), (self.dn, None), (self.up, None),
            (lax.rem(p + 6, 8), None), (lax.rem(p + 2, 8), None),
            (o, 0), (o, 1), (po, 0), (po, 1),
        ]
        block, half = table[i]
        dst = self.part(block, half)
        return self.copy(i, dst, dst, p)

    def start(self):
        for i in range(3):
            self.sent(i).start()

    def relay(self, stage):
        if stage == 0:
            self.arrived(0).wait_recv()
            self.sent(3).start()
            self.sent(4).start()
        elif stage == 1:
            self.arrived(1).wait_recv()
            self.sent(5).start()
            self.arrived(2).wait_recv()
            self.sent(6).start()
        elif stage == 2:
            self.arrived(3).wait_recv()
            self.sent(7).start()
            self.arrived(4).wait_recv()
            self.sent(8).start()
        elif stage == 3:
            self.arrived(5).wait_recv()
            self.arrived(6).wait_recv()
        else:
            self.arrived(7).wait_recv()
            self.arrived(8).wait_recv()

    def blocks(self, stage):
        m, p = self.m, self.p
        return [
            [p], [self.dn, self.up], [lax.rem(p + 6, 8), lax.rem(p + 2, 8)],
            [lax.rem(m + 4, 8)], [lax.rem(p + 4, 8)],
        ][stage]

    def drain(self):
        for i in range(9):
            self.sent(i).wait_send()


def needed(t, z):
    return (t >= 0) & (z <= 7) & ((t >= 2) | (z <= 5))


def step_kernel(
    aug_ref, anc_ref, pw_hbm, qw_hbm, kw_hbm, doc_ref, dout_ref,
    att_ref, gq_ref, gkv_ref, rows_ref,
    augment, anchor, projected, pw, qw, kw, kw_pairs, pairs, acc, kv_ref, cnt_out, cnt_in,
    kvs, q_n, q_t, do_n, do_t, num, den, first, place, delta, dq_t,
    mine, tosib, fromsib, ringout, ringin, xout, xin, grads,
    wsib_out, wsib_in, wd_out, wd_in, wu_out, wu_in, wx_out, wx_in, wacc,
    wsem, asend, arecv, nsend, nrecv, psend, precv, csend, crecv,
    up_s, up_r, sb_s, sb_r, xp_s, xp_r, gs_s, gs_r, rg_s, rg_r, xg_s, xg_r,
    ws_s, ws_r, wd_s, wd_r, wu_s, wu_r, wx_s, wx_r,
):
    s, m = lax.axis_index("seq"), lax.axis_index("mp")
    z, xh, c = s // 4, lax.rem(s // 2, 2), lax.rem(s, 2)
    sib = {"seq": s + 1 - 2 * c}
    xp_id = s + 2 - 4 * xh
    xp = {"seq": xp_id}
    up, dn = {"seq": lax.rem(s + 4, 32)}, {"seq": lax.rem(s + 28, 32)}
    hyper = []
    for k in range(5):
        bit = lax.rem(s // (1 << k), 2)
        hyper.append(s + (1 << k) * (1 - 2 * bit))
    loads = [
        pltpu.make_async_copy(src, dst, wsem.at[i])
        for i, (src, dst) in enumerate([(pw_hbm, pw), (qw_hbm, qw), (kw_hbm, kw_pairs)])
    ]
    for load in loads:
        load.start()
    aug = FeatureGather(aug_ref, augment, 288, asend, arecv, m)
    anc = FeatureGather(anc_ref, anchor, 576, nsend, nrecv, m)
    own_projected = rows_of(projected, m * 576, 576)
    halves = [pl.ds(h * HALF, HALF) for h in range(2)]
    pros = [
        FeatureGather(own_projected.at[:, half], projected, 576, psend.at[h], precv.at[h], m, half)
        for h, half in enumerate(halves)
    ]
    far, near = {"seq": lax.rem(s + 20, 32)}, {"seq": lax.rem(s + 12, 32)}
    greet(
        [{"mp": aug.p}, {"mp": aug.up}, {"mp": aug.dn}, up, dn, far, near]
        + [{"seq": h} for h in hyper]
    )

    aug.start()
    doc = doc_ref[...]
    zeros = jnp.sum((1 - doc).astype(F32), axis=1, keepdims=True)
    cnt_out[0] = jnp.broadcast_to(zeros, (8, 128)).astype(jnp.int32)

    def step(k):
        return remote(cnt_out.at[k], cnt_in.at[k], csend.at[k], crecv.at[k], {"seq": hyper[k]})

    def count(k):
        step(k).wait_recv()
        cnt_out[k + 1] = cnt_out[k] + cnt_in[k]
        if k < 4:
            step(k + 1).start()

    step(0).start()
    rows_of(augment, m * 288, 288)[...] = aug_ref[...]
    rows_of(anchor, m * 576, 576)[...] = anc_ref[...]
    loads[2].wait()

    def unpair(i, carry):
        pairs[...] = kw_pairs[pl.ds(pl.multiple_of(i * 1152, 1152), 1152), :].astype(F32)
        for half in range(2):
            out = pairs[pl.ds(half, 576, stride=2), :].astype(BF)
            kw[pl.ds(pl.multiple_of(i * 576, 576), 576), half * HD:(half + 1) * HD] = out
        return carry

    for stage in range(5):
        aug.relay(stage)
        count(stage)
        lax.fori_loop(2 * stage, min(2 * stage + 2, 8), unpair, 0)
    here = doc * cnt_out[5, 0:1, 0:1]
    lanes = lax.broadcasted_iota(jnp.int32, (1, 2 * TOK), 1)
    place[...] = lax.rem(lanes, TOK) + s * TOK
    for h in range(2):
        cut = slice(h * TOK, (h + 1) * TOK)
        head = slice(h * HD, (h + 1) * HD)
        first[:, cut] = here
        do_n[cut, :] = dout_ref[:, head]
        do_t[:, cut] = dout_ref[:, head].T
    loads[0].wait()
    loads[1].wait()
    for h, half in enumerate(halves):
        own_projected[:, half] = dot(pw[...], augment[:, half]).astype(BF)
        if h == 0:
            pros[0].start()

    def add(block):
        acc[...] += dot_tn(rows_of(anchor, block * 576, 576)[...], rows_of(qw, block * 576, 576)[...])

    def add_kv(h, block):
        piece = projected[pl.ds(pl.multiple_of(block * 576, 16), 576), halves[h]]
        acc[halves[h]] += dot_tn(piece, rows_of(kw, block * 576, 576)[...])

    def half_copy(src, block, h, send, recv, where):
        dst = kvs.at[block, halves[h]]
        return remote(dst if src is None else src.at[halves[h]], dst, send, recv, where)

    def lane(t, j):
        return 4 * t + 2 * j + c

    def to_up(g, j, h, src=None):
        return half_copy(src, lane(z - g, j), h, up_s.at[g, j, h], up_r.at[g, j, h], up)

    def to_far(j, h, src=None):
        return half_copy(src, lane(z, j), h, up_s.at[4, j, h], up_r.at[4, j, h], far)

    def to_sib(g, j, h, src=None):
        return half_copy(src, lane(z - g, j), h, sb_s.at[g, j, h], sb_r.at[g, j, h], sib)

    def from_sib(g, j, h):
        b = 4 * (z - g) + 2 * j + 1 - c
        return half_copy(None, b, h, sb_s.at[g, j, h], sb_r.at[g, j, h], sib)

    def from_dn(g, j, h):
        return half_copy(None, lane(z - g, j), h, up_s.at[g - 1, j, h], up_r.at[g - 1, j, h], dn)

    def up_needs(g):
        return (g < 4) & needed(z - g, z + 1)

    far_needs = needed(z, z + 5)

    def to_xp(h):
        return half_copy(kv_ref, s, h, xp_s.at[h], xp_r.at[h], xp)

    def from_xp(h):
        return half_copy(None, xp_id, h, xp_s.at[h], xp_r.at[h], xp)

    def spread(j, h, src=None):
        @pl.when(up_needs(0))
        def _():
            to_up(0, j, h, src).start()

        @pl.when(far_needs)
        def _():
            to_far(j, h, src).start()

        to_sib(0, j, h, src).start()

    def launch(h):
        kv_ref[halves[h]] = acc[halves[h]].astype(BF)
        to_xp(h).start()
        spread(xh, h, kv_ref)
        kvs[s, halves[h]] = kv_ref[halves[h]]

    def second(h):
        from_xp(h).wait_recv()
        spread(1 - xh, h)

    def pass_on(g, h):
        @pl.when(needed(z - g, z))
        def _():
            for j in range(2):
                from_dn(g, j, h).wait_recv()

                @pl.when(up_needs(g))
                def _():
                    to_up(g, j, h).start()

                to_sib(g, j, h).start()

    acc[...] = jnp.zeros_like(acc)
    for h in range(2):
        add_kv(h, m)
        for stage in range(5):
            pros[h].relay(stage)
            if stage == 2:
                if h == 0:
                    pros[1].start()
                else:
                    anc.start()
                    second(0)
            for block in pros[h].blocks(stage):
                add_kv(h, block)
        launch(h)
    pass_on(1, 0)
    num[...] = jnp.zeros_like(num)
    den[...] = jnp.zeros_like(den)
    dq_t[...] = jnp.zeros_like(dq_t)
    second(1)

    def scores(block):
        k, v = kvs[block, :, :HD], kvs[block, :, HD:]
        th = jnp.tanh(dot(k, q_t[...]) * (1.0 / 600.0))
        pos = block * TOK + lax.broadcasted_iota(jnp.int32, (TOK, 2 * TOK), 0)
        allowed = (pos >= first[...]) & (pos <= place[...])
        return k, v, th, jnp.where(allowed, jnp.exp2(th * (50.0 * LOG2E)), 0.0)

    def forward(g):
        def one(b, carry):
            block = 4 * (z - g) + b

            @pl.when(block <= s)
            def _():
                _, v, _, w = scores(block)
                den[...] += jnp.sum(w, axis=0, keepdims=True)
                num[...] += dot_tn(v, w.astype(BF))

            return carry

        lax.fori_loop(0, 4, one, 0)

    acc[...] = jnp.zeros_like(acc)
    add(m)
    for stage in range(5):
        anc.relay(stage)
        for block in anc.blocks(stage):
            add(block)
        if stage < 3:
            pass_on((stage + 3) // 2, (stage + 1) % 2)

    query = acc[...].astype(BF)
    for h in range(2):
        cut = slice(h * TOK, (h + 1) * TOK)
        head = slice(h * HD, (h + 1) * HD)
        q_n[cut, :] = query[:, head]
        q_t[:, cut] = query[:, head].T

    def forward_step(g, carry):
        @pl.when(needed(z - g, z))
        def _():
            @pl.when(g > 2)
            def _():
                for h in range(2):
                    pass_on(g, h)

            for h in range(2):
                for j in range(2):
                    from_sib(g, j, h).wait_recv()
            forward(g)

        return carry

    lax.fori_loop(0, 6, forward_step, 0)

    attended = (num[...] * (1.0 / den[...])).astype(BF)
    delta[...] = jnp.sum(do_t[...].astype(F32) * attended.astype(F32), axis=0, keepdims=True)
    den[...] = 1.0 / den[...]
    for h in range(2):
        att_ref[:, h * HD:(h + 1) * HD] = attended[:, h * TOK:(h + 1) * TOK].T

    def ring_out(g, j, where=dn):
        return remote(ringout.at[g - 1, j], ringin.at[g - 1, j], rg_s.at[g - 1, j], rg_r.at[g - 1, j], where)

    def ring_in(g, j):
        return remote(ringout.at[g, j], ringin.at[g, j], rg_s.at[g, j], rg_r.at[g, j], up)

    def sib_grad(g, j):
        return remote(tosib.at[g, j], fromsib.at[g, j], gs_s.at[g, j], gs_r.at[g, j], sib)

    def backward(block, write):
        k, v, th, w = scores(block)
        prob = w * den[...]
        soft = prob * (dot(v, do_t[...]) - delta[...])
        raw = (soft * ((1.0 - th * th) * (1.0 / 12.0))).astype(BF)
        write(dot(raw, q_n[...]), dot(prob.astype(BF), do_n[...]))
        dq_t[...] += dot_tn(k, raw)

    def contributions(g):
        def for_sib(j, carry):
            block = 4 * (z - g) + 2 * j + 1 - c

            @pl.when(block <= s)
            def _():
                def write(gk, gv):
                    tosib[g, j, :, :HD] = gk.astype(BF)
                    tosib[g, j, :, HD:] = gv.astype(BF)

                backward(block, write)

            @pl.when(block > s)
            def _():
                tosib[g, j] = jnp.zeros((TOK, 256), BF)

            sib_grad(g, j).start()
            return carry

        def for_me(j, carry):
            block = lane(z - g, j)

            @pl.when(block <= s)
            def _():
                def write(gk, gv):
                    mine[g, j, :, :HD] = gk
                    mine[g, j, :, HD:] = gv

                backward(block, write)

            @pl.when(block > s)
            def _():
                mine[g, j] = jnp.zeros((TOK, 256), F32)

            return carry

        lax.fori_loop(0, 2, for_sib, 0)
        lax.fori_loop(0, 2, for_me, 0)

    def sum_up(g, j):
        sib_grad(g, j).wait_recv()
        mine[g, j] += fromsib[g, j].astype(F32)

        @pl.when(up_needs(g))
        def _():
            ring_in(g, j).wait_recv()
            mine[g, j] += ringin[g, j].astype(F32)

    def contribute(g):
        @pl.when(needed(z - g, z))
        def _():
            contributions(g)

    def send_sum(g):
        @pl.when(needed(z - g, z))
        def _():
            for j in range(2):
                sum_up(g, j)
                ringout[g - 1, j] = mine[g, j].astype(BF)
                ring_out(g, j, near if g == 5 else dn).start()

    contribute(5)
    contribute(4)
    send_sum(5)
    contribute(3)
    contribute(2)
    send_sum(4)
    contribute(1)
    contribute(0)

    def weight(n, act, lengths):
        grad = grads.at[n]

        def partial(t, j, core):
            return dot(rows_of(act, t * 576 + j * 288 + core * 144, 144)[...], grad[...])

        def sib_copy(t):
            return remote(wsib_out.at[n, t], wsib_in.at[n, t], ws_s.at[n, t], ws_r.at[n, t], sib)

        def target(k, way):
            return lax.rem(z + 8 - lengths[0] + k, 8) if way == 0 else lax.rem(z + 8 + lengths[1] - k, 8)

        def send_all():
            def one(i, carry):
                t = lax.rem(z + 4 + 7 * lax.rem(i, 2) * (i // 2 + 1) + (1 - lax.rem(i, 2)) * (i // 2), 8)
                for j in range(2):
                    wsib_out[n, t, j] = partial(t, j, 1 - c).astype(BF)
                sib_copy(t).start()
                return carry

            lax.fori_loop(0, 8, one, 0)

        def hop(k, way, j):
            out, into = (wd_out, wd_in) if way == 0 else (wu_out, wu_in)
            ss, rr = (wd_s, wd_r) if way == 0 else (wu_s, wu_r)
            return remote(
                out.at[n, k, j], into.at[n, k, j], ss.at[n, k, j], rr.at[n, k, j], dn if way == 0 else up
            )

        def hop_step(k, way):
            out, into = (wd_out, wd_in) if way == 0 else (wu_out, wu_in)
            t = target(k, way)
            sib_copy(t).wait_recv()
            for j in range(2):
                total = partial(t, j, c) + wsib_in[n, t, j].astype(F32)
                if k > 0:
                    hop(k - 1, way, j).wait_recv()
                    total += into[n, k - 1, j].astype(F32)
                out[n, k, j] = total.astype(BF)
                hop(k, way, j).start()

        def step(k):
            for way in range(2):
                if k < lengths[way]:
                    hop_step(k, way)

        def x_copy():
            return remote(wx_out.at[n], wx_in.at[n], wx_s.at[n], wx_r.at[n], xp)

        def meet():
            sib_copy(z).wait_recv()
            for j in range(2):
                for way in range(2):
                    hop(lengths[way] - 1, way, j).wait_recv()
                wacc[j] = (
                    partial(z, j, c) + wsib_in[n, z, j].astype(F32)
                    + wd_in[n, lengths[0] - 1, j].astype(F32) + wu_in[n, lengths[1] - 1, j].astype(F32)
                )
            wx_out[n] = wacc[1 - xh].astype(BF)
            x_copy().start()
            return wacc[xh]

        def drain():
            for t in range(8):
                sib_copy(t).wait_send()
            for way in range(2):
                for k in range(lengths[way]):
                    for j in range(2):
                        hop(k, way, j).wait_send()
            x_copy().wait_send()

        return send_all, step, meet, x_copy, drain

    wq = weight(0, anchor, (3, 4))
    wkv = weight(1, projected, (4, 3))
    for h in range(2):
        grads[0, :, h * HD:(h + 1) * HD] = dq_t[:, h * TOK:(h + 1) * TOK].T.astype(BF)
    send_sum(3)
    wq[0]()
    send_sum(2)
    wq[1](0)
    send_sum(1)
    wq[1](1)
    for j in range(2):
        sum_up(0, j)

        @pl.when(far_needs)
        def _():
            ring_in(4, j).wait_recv()
            mine[0, j] += ringin[4, j].astype(F32)

    xout[...] = mine[0, 1 - xh].astype(BF)
    x_rows = remote(xout, xin, xg_s, xg_r, xp)
    x_rows.start()
    wq[1](2)
    x_rows.wait_recv()
    grads[1] = (mine[0, xh] + xin[...].astype(F32)).astype(BF)
    wkv[0]()
    wkv[1](0)
    wq[1](3)
    for half in range(2):
        pairs[pl.ds(half, TOK, stride=2), :] = grads[1, :, half * HD:(half + 1) * HD].astype(F32)
    rows_ref[...] = pairs[:2 * TOK, :].astype(BF)
    wkv[1](1)
    own_q = wq[2]()
    gq_ref[...] = own_q
    wkv[1](2)
    wkv[1](3)
    own_kv = wkv[2]()
    wacc[0] = own_kv
    wq[3]().wait_recv()
    gq_ref[...] += wx_in[0].astype(F32)
    wkv[3]().wait_recv()
    wacc[0] += wx_in[1].astype(F32)
    for half in range(2):
        gkv_ref[pl.ds(half, 144, stride=2), :] = wacc[0, :, half * HD:(half + 1) * HD]

    for h in range(2):
        to_xp(h).wait_send()
        for j in range(2):
            @pl.when(far_needs)
            def _():
                to_far(j, h).wait_send()

    x_rows.wait_send()
    wq[4]()
    wkv[4]()
    aug.drain()
    anc.drain()
    pros[0].drain()
    pros[1].drain()
    for k in range(5):
        step(k).wait_send()

    def drained(g, carry):
        @pl.when(needed(z - g, z))
        def _():
            for j in range(2):
                sib_grad(g, j).wait_send()
                for h in range(2):
                    to_sib(g, j, h).wait_send()

                    @pl.when(up_needs(g))
                    def _():
                        to_up(g, j, h).wait_send()

                @pl.when(g > 0)
                def _():
                    ring_out(g, j).wait_send()

        return carry

    lax.fori_loop(0, 6, drained, 0)


def step_call(aug_t, anc_t, pw_t, q_weight, kv_pairs, doc, d_out):
    dma = pltpu.SemaphoreType.DMA
    vmem = pl.BlockSpec(memory_space=pltpu.VMEM)
    hbm = pl.BlockSpec(memory_space=pl.ANY)
    two = lambda n: [dma(n), dma(n)]
    return pl.pallas_call(
        step_kernel,
        out_shape=[
            jax.ShapeDtypeStruct((TOK, 256), BF),
            jax.ShapeDtypeStruct((144, 256), F32),
            jax.ShapeDtypeStruct((288, HD), F32),
            jax.ShapeDtypeStruct((2 * TOK, HD), BF),
        ],
        in_specs=[vmem, vmem, hbm, hbm, hbm, vmem, vmem],
        out_specs=[vmem] * 4,
        scratch_shapes=[
            pltpu.VMEM((2304, TOK), BF), pltpu.VMEM((4608, TOK), BF), pltpu.VMEM((4608, TOK), BF),
            pltpu.VMEM((576, 2304), BF), pltpu.VMEM((4608, 256), BF), pltpu.VMEM((4608, 256), BF),
            pltpu.VMEM((9216, HD), BF), pltpu.VMEM((1152, HD), F32),
            pltpu.VMEM((TOK, 256), F32), pltpu.VMEM((TOK, 256), BF),
            pltpu.VMEM((6, 8, 128), jnp.int32), pltpu.VMEM((5, 8, 128), jnp.int32),
            pltpu.VMEM((32, TOK, 256), BF),
            pltpu.VMEM((512, HD), BF), pltpu.VMEM((HD, 512), BF),
            pltpu.VMEM((512, HD), BF), pltpu.VMEM((HD, 512), BF),
            pltpu.VMEM((HD, 512), F32), pltpu.VMEM((1, 512), F32),
            pltpu.VMEM((1, 512), jnp.int32), pltpu.VMEM((1, 512), jnp.int32),
            pltpu.VMEM((1, 512), F32), pltpu.VMEM((HD, 512), F32),
            pltpu.VMEM((6, 2, TOK, 256), F32),
            pltpu.VMEM((6, 2, TOK, 256), BF), pltpu.VMEM((6, 2, TOK, 256), BF),
            pltpu.VMEM((5, 2, TOK, 256), BF), pltpu.VMEM((5, 2, TOK, 256), BF),
            pltpu.VMEM((TOK, 256), BF), pltpu.VMEM((TOK, 256), BF),
            pltpu.VMEM((2, TOK, 256), BF),
            pltpu.VMEM((2, 8, 2, 144, 256), BF), pltpu.VMEM((2, 8, 2, 144, 256), BF),
            pltpu.VMEM((2, 4, 2, 144, 256), BF), pltpu.VMEM((2, 4, 2, 144, 256), BF),
            pltpu.VMEM((2, 4, 2, 144, 256), BF), pltpu.VMEM((2, 4, 2, 144, 256), BF),
            pltpu.VMEM((2, 144, 256), BF), pltpu.VMEM((2, 144, 256), BF),
            pltpu.VMEM((2, 144, 256), F32),
            dma((3,)), *two((9,)), *two((9,)), *two((2, 9)), *two((5,)),
            *two((5, 2, 2)), *two((6, 2, 2)), *two((2,)), *two((6, 2)), *two((5, 2)), *two(()),
            *two((2, 8)), *two((2, 4, 2)), *two((2, 4, 2)), *two((2,)),
        ],
        compiler_params=pltpu.CompilerParams(
            collective_id=1, has_side_effects=True, vmem_limit_bytes=60 * 1024 * 1024
        ),
    )(aug_t, anc_t, pw_t, q_weight, kv_pairs, doc, d_out)


def hand_over(*refs):
    n = len(refs) // 2
    for src, dst in zip(refs[:n], refs[n:]):
        dst[...] = src[...]


def body(anchor, augment, proj_weight, q_weight, kv_weight, doc_ids, d_out):
    results = step_call(
        augment.T, anchor.T, proj_weight.T, q_weight,
        kv_weight.reshape(-1, HD), doc_ids.reshape(1, -1), d_out,
    )
    attended, grad_q, grad_kv, rows = pl.pallas_call(
        hand_over,
        out_shape=[jax.ShapeDtypeStruct(r.shape, r.dtype) for r in results],
        in_specs=[pl.BlockSpec(memory_space=pltpu.VMEM)] * 4,
        out_specs=[pl.BlockSpec(memory_space=pltpu.VMEM)] * 4,
    )(*results)
    return attended, grad_q, grad_kv.reshape(144, 1, 2, HD), rows.reshape(TOK, 1, 2, HD)


def solution(mesh):
    placed = (
        P("seq", "mp"), P("seq", "mp"), P(None, "mp"), P(None, "mp"),
        P(None, "mp", None, None), P("seq"), P("seq", "mp"),
    )
    return jax.shard_map(
        body,
        mesh=mesh,
        in_specs=placed,
        out_specs=(
            P("seq", "mp"), P("seq", "mp"),
            P("seq", "mp", None, None), P("seq", "mp", None, None),
        ),
        check_vma=False,
    )
```

```python
import functools

import jax
import jax.numpy as jnp
from jax import lax
from jax.experimental import pallas as pl
from jax.experimental.pallas import tpu as pltpu
from jax.sharding import PartitionSpec as P

BF = jnp.bfloat16
F32 = jnp.float32
TOK = 256
HALF = 128
HD = 128
MESH = pl.DeviceIdType.MESH
LOG2E = 1.4426950408889634
TN = (((0,), (0,)), ((), ()))


def remote(src, dst, send, recv, where):
    return pltpu.make_async_remote_copy(
        src_ref=src, dst_ref=dst, send_sem=send, recv_sem=recv, device_id=where, device_id_type=MESH
    )


def dot(a, b):
    return jnp.dot(a, b, preferred_element_type=F32)


def dot_tn(a, b):
    return lax.dot_general(a, b, TN, preferred_element_type=F32)


def rows_of(ref, start, size):
    return ref.at[pl.ds(pl.multiple_of(start, 16), size)]


def greet(partners):
    barrier = pltpu.get_barrier_semaphore()
    for where in partners:
        pl.semaphore_signal(barrier, inc=1, device_id=where, device_id_type=MESH)
    pl.semaphore_wait(barrier, len(partners))


class FeatureGather:
    def __init__(self, own, buf, rows, send, recv, m, lanes=pl.ds(0, TOK)):
        self.own, self.buf, self.rows, self.send, self.recv = own, buf, rows, send, recv
        self.lanes, self.m = lanes, m
        self.p = m + 1 - 2 * lax.rem(m, 2)
        self.up, self.dn = lax.rem(m + 2, 8), lax.rem(m + 6, 8)
        self.o = lax.rem(m + 4, 8)
        p = self.p
        self.p_up, self.p_dn, self.p_o = lax.rem(p + 2, 8), lax.rem(p + 6, 8), lax.rem(p + 4, 8)
        n = rows // 9
        whole, left, right = (0, 9 * n), (0, 5 * n), (5 * n, 4 * n)
        top, bottom = (0, rows // 2), (rows // 2, rows // 2)
        left0, left1 = (0, 5 * n // 2), (5 * n // 2, 5 * n // 2)
        m, p, up, dn = self.m, self.p, self.up, self.dn
        self.out = [
            (m, left, p), (m, whole, up), (m, whole, dn), (p, left, up), (p, left, dn),
            (dn, top, up), (up, bottom, dn), (self.p_dn, left0, up), (self.p_up, left1, dn),
            (m, right, p), (dn, right, p), (up, right, p), (self.o, right, p),
        ]
        self.into = [
            (p, left), (dn, whole), (up, whole), (self.p_dn, left), (self.p_up, left),
            (self.o, top), (self.o, bottom), (self.p_o, left0), (self.p_o, left1),
            (p, right), (self.p_dn, right), (self.p_up, right), (self.p_o, right),
        ]

    def part(self, block, rows):
        start = block * self.rows + rows[0]
        return self.buf.at[pl.ds(pl.multiple_of(start, 16), rows[1]), self.lanes]

    def sent(self, i):
        block, rows, to = self.out[i]
        dst = self.part(block, rows)
        src = self.own.at[pl.ds(*rows)] if i in (0, 1, 2, 9) else dst
        return remote(src, dst, self.send.at[i], self.recv.at[i], {"mp": to})

    def arrived(self, i):
        dst = self.part(*self.into[i])
        return remote(dst, dst, self.send.at[i], self.recv.at[i], {"mp": self.p})

    def start(self):
        for i in (0, 1, 2, 9):
            self.sent(i).start()

    def relay(self, stage):
        waits, sends = [
            ((0,), (3, 4)), ((1,), (5, 10)), ((2,), (6, 11)), ((3,), (7,)), ((4,), (8,)),
            ((6,), (12,)), ((5,), ()), ((9, 10, 11), ()), ((7, 8, 12), ()),
        ][stage]
        for i in waits:
            self.arrived(i).wait_recv()
        for i in sends:
            self.sent(i).start()

    def blocks(self, stage):
        return {
            1: [self.dn], 2: [self.up], 6: [self.o],
            7: [self.p, self.p_dn, self.p_up], 8: [self.p_o],
        }.get(stage, [])

    def drain(self):
        for i in range(13):
            self.sent(i).wait_send()


def needed(t, z):
    return (t >= 0) & (z <= 7) & ((t >= 2) | (z <= 5))


def step_kernel(
    aug_ref, anc_ref, pw_hbm, qw_hbm, kw_hbm, doc_ref, dout_ref,
    att_ref, gq_ref, gkv_ref, rows_ref,
    augment, anchor, projected, pw, qw, kw, kw_pairs, pairs, acc, kv_ref, cnt_out, cnt_in,
    kvs, q_n, q_t, do_n, do_t, num, den, first, place, delta, dq_t,
    mine, tosib, fromsib, ringout, ringin, xout, xin, grads,
    wsib_out, wsib_in, wd_out, wd_in, wu_out, wu_in, wx_out, wx_in, wacc,
    wsem, asend, arecv, nsend, nrecv, psend, precv, csend, crecv,
    up_s, up_r, sb_s, sb_r, xp_s, xp_r, gs_s, gs_r, rg_s, rg_r, xg_s, xg_r,
    ws_s, ws_r, wd_s, wd_r, wu_s, wu_r, wx_s, wx_r,
):
    s, m = lax.axis_index("seq"), lax.axis_index("mp")
    z, xh, c = s // 4, lax.rem(s // 2, 2), lax.rem(s, 2)
    sib = {"seq": s + 1 - 2 * c}
    xp_id = s + 2 - 4 * xh
    xp = {"seq": xp_id}
    up, dn = {"seq": lax.rem(s + 4, 32)}, {"seq": lax.rem(s + 28, 32)}
    hyper = []
    for k in range(5):
        bit = lax.rem(s // (1 << k), 2)
        hyper.append(s + (1 << k) * (1 - 2 * bit))
    loads = [
        pltpu.make_async_copy(src, dst, wsem.at[i])
        for i, (src, dst) in enumerate([(pw_hbm, pw), (qw_hbm, qw), (kw_hbm, kw_pairs)])
    ]
    for load in loads:
        load.start()
    aug = FeatureGather(aug_ref, augment, 288, asend, arecv, m)
    anc = FeatureGather(anc_ref, anchor, 576, nsend, nrecv, m)
    own_projected = rows_of(projected, m * 576, 576)
    halves = [pl.ds(h * HALF, HALF) for h in range(2)]
    pros = [
        FeatureGather(own_projected.at[:, half], projected, 576, psend.at[h], precv.at[h], m, half)
        for h, half in enumerate(halves)
    ]
    far, near = {"seq": lax.rem(s + 20, 32)}, {"seq": lax.rem(s + 12, 32)}
    across = 2 - 4 * xh
    ring = [up, dn, far, near]
    greet(
        [{"mp": aug.p}, {"mp": aug.up}, {"mp": aug.dn}] + ring
        + [{"seq": one["seq"] + across} for one in ring] + [{"seq": h} for h in hyper]
    )

    aug.start()
    doc = doc_ref[...]
    zeros = jnp.sum((1 - doc).astype(F32), axis=1, keepdims=True)
    cnt_out[0] = jnp.broadcast_to(zeros, (8, 128)).astype(jnp.int32)

    def step(k):
        return remote(cnt_out.at[k], cnt_in.at[k], csend.at[k], crecv.at[k], {"seq": hyper[k]})

    def count(k):
        step(k).wait_recv()
        cnt_out[k + 1] = cnt_out[k] + cnt_in[k]
        if k < 4:
            step(k + 1).start()

    step(0).start()
    rows_of(augment, m * 288, 288)[...] = aug_ref[...]
    rows_of(anchor, m * 576, 576)[...] = anc_ref[...]
    loads[2].wait()

    def unpair(i, carry):
        pairs[...] = kw_pairs[pl.ds(pl.multiple_of(i * 1152, 1152), 1152), :].astype(F32)
        for half in range(2):
            out = pairs[pl.ds(half, 576, stride=2), :].astype(BF)
            kw[pl.ds(pl.multiple_of(i * 576, 576), 576), half * HD:(half + 1) * HD] = out
        return carry

    for stage in range(9):
        aug.relay(stage)
        if stage < 5:
            count(stage)
            lax.fori_loop(2 * stage, min(2 * stage + 2, 8), unpair, 0)
        if stage == 5:
            anc.start()
    here = doc * cnt_out[5, 0:1, 0:1]
    lanes = lax.broadcasted_iota(jnp.int32, (1, 2 * TOK), 1)
    place[...] = lax.rem(lanes, TOK) + s * TOK
    for h in range(2):
        cut = slice(h * TOK, (h + 1) * TOK)
        head = slice(h * HD, (h + 1) * HD)
        first[:, cut] = here
        do_n[cut, :] = dout_ref[:, head]
        do_t[:, cut] = dout_ref[:, head].T
    loads[0].wait()
    loads[1].wait()
    for h, half in enumerate(halves):
        own_projected[:, half] = dot(pw[...], augment[:, half]).astype(BF)
        if h == 0:
            pros[0].start()

    def add(block):
        acc[...] += dot_tn(rows_of(anchor, block * 576, 576)[...], rows_of(qw, block * 576, 576)[...])

    def add_kv(h, block):
        piece = projected[pl.ds(pl.multiple_of(block * 576, 16), 576), halves[h]]
        acc[halves[h]] += dot_tn(piece, rows_of(kw, block * 576, 576)[...])

    def half_copy(src, block, h, send, recv, where):
        dst = kvs.at[block, halves[h]]
        return remote(dst if src is None else src.at[halves[h]], dst, send, recv, where)

    def lane(t, j):
        return 4 * t + 2 * j + c

    def to_up(g, j, h, src=None):
        return half_copy(src, lane(z - g, j), h, up_s.at[g, j, h], up_r.at[g, j, h], up)

    def to_far(j, h, src=None):
        return half_copy(src, lane(z, j), h, up_s.at[4, j, h], up_r.at[4, j, h], far)

    def to_sib(g, j, h, src=None):
        return half_copy(src, lane(z - g, j), h, sb_s.at[g, j, h], sb_r.at[g, j, h], sib)

    def from_sib(g, j, h):
        b = 4 * (z - g) + 2 * j + 1 - c
        return half_copy(None, b, h, sb_s.at[g, j, h], sb_r.at[g, j, h], sib)

    def from_dn(g, j, h):
        return half_copy(None, lane(z - g, j), h, up_s.at[g - 1, j, h], up_r.at[g - 1, j, h], dn)

    def up_needs(g):
        return (g < 4) & needed(z - g, z + 1)

    far_needs = needed(z, z + 5)

    def to_xp(h):
        return half_copy(kv_ref, s, h, xp_s.at[h], xp_r.at[h], xp)

    def from_xp(h):
        return half_copy(None, xp_id, h, xp_s.at[h], xp_r.at[h], xp)

    def spread(j, h, src=None):
        @pl.when(up_needs(0))
        def _():
            to_up(0, j, h, src).start()

        @pl.when(far_needs)
        def _():
            to_far(j, h, src).start()

        to_sib(0, j, h, src).start()

    def launch(h):
        kv_ref[halves[h]] = acc[halves[h]].astype(BF)
        to_xp(h).start()
        spread(xh, h, kv_ref)
        kvs[s, halves[h]] = kv_ref[halves[h]]

    def second(h):
        from_xp(h).wait_recv()
        spread(1 - xh, h)

    def pass_on(g, h):
        @pl.when(needed(z - g, z))
        def _():
            for j in range(2):
                from_dn(g, j, h).wait_recv()

                @pl.when(up_needs(g))
                def _():
                    to_up(g, j, h).start()

                to_sib(g, j, h).start()

    acc[...] = jnp.zeros_like(acc)
    for h in range(2):
        add_kv(h, m)
        for stage in range(9):
            pros[h].relay(stage)
            if stage == 4 and h == 0:
                pros[1].start()
            if stage == 5 and h == 1:
                second(0)
                for early in range(3):
                    anc.relay(early)
            for block in pros[h].blocks(stage):
                add_kv(h, block)
        launch(h)
    pass_on(1, 0)
    num[...] = jnp.zeros_like(num)
    den[...] = jnp.zeros_like(den)
    dq_t[...] = jnp.zeros_like(dq_t)
    second(1)

    def scores(block):
        k, v = kvs[block, :, :HD], kvs[block, :, HD:]
        th = jnp.tanh(dot(k, q_t[...]) * (1.0 / 600.0))
        pos = block * TOK + lax.broadcasted_iota(jnp.int32, (TOK, 2 * TOK), 0)
        allowed = (pos >= first[...]) & (pos <= place[...])
        return k, v, th, jnp.where(allowed, jnp.exp2(th * (50.0 * LOG2E)), 0.0)

    def forward(g):
        def one(b, carry):
            block = 4 * (z - g) + b

            @pl.when(block <= s)
            def _():
                _, v, _, w = scores(block)
                den[...] += jnp.sum(w, axis=0, keepdims=True)
                num[...] += dot_tn(v, w.astype(BF))

            return carry

        lax.fori_loop(0, 4, one, 0)

    acc[...] = jnp.zeros_like(acc)
    add(m)
    for stage in range(9):
        if stage > 2:
            anc.relay(stage)
        for block in anc.blocks(stage):
            add(block)
        if stage in (4, 5, 6):
            pass_on((stage - 1) // 2, (stage + 1) % 2)

    query = acc[...].astype(BF)
    for h in range(2):
        cut = slice(h * TOK, (h + 1) * TOK)
        head = slice(h * HD, (h + 1) * HD)
        q_n[cut, :] = query[:, head]
        q_t[:, cut] = query[:, head].T

    def forward_step(g, carry):
        @pl.when(needed(z - g, z))
        def _():
            @pl.when(g > 2)
            def _():
                for h in range(2):
                    pass_on(g, h)

            for h in range(2):
                for j in range(2):
                    from_sib(g, j, h).wait_recv()
            forward(g)

        return carry

    lax.fori_loop(0, 6, forward_step, 0)

    attended = (num[...] * (1.0 / den[...])).astype(BF)
    delta[...] = jnp.sum(do_t[...].astype(F32) * attended.astype(F32), axis=0, keepdims=True)
    den[...] = 1.0 / den[...]
    for h in range(2):
        att_ref[:, h * HD:(h + 1) * HD] = attended[:, h * TOK:(h + 1) * TOK].T

    def piece(k):
        return lax.rem(xh + k, 2)

    def there(where, k):
        return {"seq": where["seq"] + k * across}

    def ring_out(g, k, last=False):
        where = there(near if g == 5 else dn, k) if last else dn
        return remote(ringout.at[g - 1, k], ringin.at[g - 1, k], rg_s.at[g - 1, k], rg_r.at[g - 1, k], where)

    def ring_in(g, k):
        return remote(ringout.at[g, k], ringin.at[g, k], rg_s.at[g, k], rg_r.at[g, k], up)

    def sib_grad(g, j):
        return remote(tosib.at[g, j], fromsib.at[g, j], gs_s.at[g, j], gs_r.at[g, j], sib)

    def backward(block, write):
        k, v, th, w = scores(block)
        prob = w * den[...]
        soft = prob * (dot(v, do_t[...]) - delta[...])
        raw = (soft * ((1.0 - th * th) * (1.0 / 12.0))).astype(BF)
        write(dot(raw, q_n[...]), dot(prob.astype(BF), do_n[...]))
        dq_t[...] += dot_tn(k, raw)

    def contributions(g):
        def for_sib(j, carry):
            block = 4 * (z - g) + 2 * j + 1 - c

            @pl.when(block <= s)
            def _():
                def write(gk, gv):
                    tosib[g, j, :, :HD] = gk.astype(BF)
                    tosib[g, j, :, HD:] = gv.astype(BF)

                backward(block, write)

            @pl.when(block > s)
            def _():
                tosib[g, j] = jnp.zeros((TOK, 256), BF)

            sib_grad(g, j).start()
            return carry

        def for_me(j, carry):
            block = lane(z - g, j)

            @pl.when(block <= s)
            def _():
                def write(gk, gv):
                    mine[g, j, :, :HD] = gk
                    mine[g, j, :, HD:] = gv

                backward(block, write)

            @pl.when(block > s)
            def _():
                mine[g, j] = jnp.zeros((TOK, 256), F32)

            return carry

        lax.fori_loop(0, 2, for_sib, 0)
        lax.fori_loop(0, 2, for_me, 0)

    def contribute(g):
        @pl.when(needed(z - g, z))
        def _():
            contributions(g)

    def send_sum(g):
        @pl.when(needed(z - g, z))
        def _():
            for k in (1, 0):
                j = piece(k)
                sib_grad(g, j).wait_recv()
                mine[g, j] += fromsib[g, j].astype(F32)

                @pl.when(up_needs(g))
                def _():
                    ring_in(g, k).wait_recv()
                    mine[g, j] += ringin[g, k].astype(F32)

                ringout[g - 1, k] = mine[g, j].astype(BF)
                ring_out(g, k, g in (1, 5)).start()

    contribute(4)
    send_sum(4)
    contribute(3)
    contribute(5)
    send_sum(5)
    send_sum(3)
    contribute(2)
    send_sum(2)
    contribute(1)
    send_sum(1)
    contribute(0)

    def weight(n, act, lengths):
        grad = grads.at[n]

        def partial(t, j, core):
            return dot(rows_of(act, t * 576 + j * 288 + core * 144, 144)[...], grad[...])

        def sib_copy(t):
            return remote(wsib_out.at[n, t], wsib_in.at[n, t], ws_s.at[n, t], ws_r.at[n, t], sib)

        def target(k, way):
            return lax.rem(z + 8 - lengths[0] + k, 8) if way == 0 else lax.rem(z + 8 + lengths[1] - k, 8)

        def push(*targets):
            for t in targets:
                for j in range(2):
                    wsib_out[n, t, j] = partial(t, j, 1 - c).astype(BF)
                sib_copy(t).start()

        def push_for(k):
            push(*[target(k, way) for way in range(2) if k < lengths[way]])

        def hop(k, way, q):
            out, into = (wd_out, wd_in) if way == 0 else (wu_out, wu_in)
            ss, rr = (wd_s, wd_r) if way == 0 else (wu_s, wu_r)
            where = dn if way == 0 else up
            if k == lengths[way] - 1:
                where = there(where, q)
            return remote(out.at[n, k, q], into.at[n, k, q], ss.at[n, k, q], rr.at[n, k, q], where)

        def hop_step(k, way):
            out, into = (wd_out, wd_in) if way == 0 else (wu_out, wu_in)
            t = target(k, way)
            sib_copy(t).wait_recv()
            for q in (1, 0):
                total = partial(t, piece(q), c) + wsib_in[n, t, piece(q)].astype(F32)
                if k > 0:
                    hop(k - 1, way, q).wait_recv()
                    total += into[n, k - 1, q].astype(F32)
                out[n, k, q] = total.astype(BF)
                hop(k, way, q).start()

        def step(k):
            for way in range(2):
                if k < lengths[way]:
                    hop_step(k, way)

        def x_copy():
            return remote(wx_out.at[n], wx_in.at[n], wx_s.at[n], wx_r.at[n], xp)

        def cross():
            sib_copy(z).wait_recv()
            for q in (1, 0):
                wacc[n, q] = partial(z, piece(q), c) + wsib_in[n, z, piece(q)].astype(F32)
            wx_out[n] = wacc[n, 1].astype(BF)
            x_copy().start()

        def meet():
            x_copy().wait_recv()
            total = wacc[n, 0] + wx_in[n].astype(F32)
            for way, into in enumerate((wd_in, wu_in)):
                for q in range(2):
                    hop(lengths[way] - 1, way, q).wait_recv()
                    total += into[n, lengths[way] - 1, q].astype(F32)
            return total

        def drain():
            for t in range(8):
                sib_copy(t).wait_send()
            for way in range(2):
                for k in range(lengths[way]):
                    for q in range(2):
                        hop(k, way, q).wait_send()
            x_copy().wait_send()

        return push, push_for, step, cross, meet, drain

    push_q, push_q_for, step_q, cross_q, meet_q, drain_q = weight(0, anchor, (3, 4))
    push_kv, push_kv_for, step_kv, cross_kv, meet_kv, drain_kv = weight(1, projected, (4, 3))
    for k in (1, 0):
        sib_grad(0, piece(k)).wait_recv()
        mine[0, piece(k)] += fromsib[0, piece(k)].astype(F32)
        if k == 1:
            xout[...] = mine[0, piece(1)].astype(BF)
            x_rows = remote(xout, xin, xg_s, xg_r, xp)
            x_rows.start()
    for h in range(2):
        grads[0, :, h * HD:(h + 1) * HD] = dq_t[:, h * TOK:(h + 1) * TOK].T.astype(BF)
    push_q_for(0)
    push_q_for(1)
    step_q(0)
    push_q_for(2)
    push_q_for(3)
    push_q(z)
    x_rows.wait_recv()
    own = mine[0, xh] + xin[...].astype(F32)
    mine[0, xh] = own
    for k in range(2):
        @pl.when(far_needs)
        def _():
            ring_in(4, k).wait_recv()
            mine[0, xh] += ringin[4, k].astype(F32)

    for k in range(2):
        @pl.when(up_needs(0))
        def _():
            ring_in(0, k).wait_recv()
            mine[0, xh] += ringin[0, k].astype(F32)

    grads[1] = mine[0, xh].astype(BF)
    push_kv_for(0)
    push_kv_for(1)
    step_kv(0)
    step_q(1)
    push_kv_for(2)
    step_kv(1)
    step_q(2)
    push_kv_for(3)
    push_kv(z)
    step_kv(2)
    cross_kv()
    cross_q()
    step_kv(3)
    step_q(3)
    for half in range(2):
        pairs[pl.ds(half, TOK, stride=2), :] = grads[1, :, half * HD:(half + 1) * HD].astype(F32)
    rows_ref[...] = pairs[:2 * TOK, :].astype(BF)
    gq_ref[...] = meet_q()
    wacc[1, 0] = meet_kv()
    for half in range(2):
        gkv_ref[pl.ds(half, 144, stride=2), :] = wacc[1, 0, :, half * HD:(half + 1) * HD]

    for h in range(2):
        to_xp(h).wait_send()
        for j in range(2):
            @pl.when(far_needs)
            def _():
                to_far(j, h).wait_send()

    x_rows.wait_send()
    drain_q()
    drain_kv()
    aug.drain()
    anc.drain()
    pros[0].drain()
    pros[1].drain()
    for k in range(5):
        step(k).wait_send()

    def drained(g, carry):
        @pl.when(needed(z - g, z))
        def _():
            for j in range(2):
                sib_grad(g, j).wait_send()
                for h in range(2):
                    to_sib(g, j, h).wait_send()

                    @pl.when(up_needs(g))
                    def _():
                        to_up(g, j, h).wait_send()

                @pl.when(g > 0)
                def _():
                    ring_out(g, j).wait_send()

        return carry

    lax.fori_loop(0, 6, drained, 0)


def step_call(aug_t, anc_t, pw_t, q_weight, kv_pairs, doc, d_out):
    dma = pltpu.SemaphoreType.DMA
    vmem = pl.BlockSpec(memory_space=pltpu.VMEM)
    hbm = pl.BlockSpec(memory_space=pl.ANY)
    two = lambda n: [dma(n), dma(n)]
    return pl.pallas_call(
        step_kernel,
        out_shape=[
            jax.ShapeDtypeStruct((TOK, 256), BF),
            jax.ShapeDtypeStruct((144, 256), F32),
            jax.ShapeDtypeStruct((288, HD), F32),
            jax.ShapeDtypeStruct((2 * TOK, HD), BF),
        ],
        in_specs=[vmem, vmem, hbm, hbm, hbm, vmem, vmem],
        out_specs=[vmem] * 4,
        scratch_shapes=[
            pltpu.VMEM((2304, TOK), BF), pltpu.VMEM((4608, TOK), BF), pltpu.VMEM((4608, TOK), BF),
            pltpu.VMEM((576, 2304), BF), pltpu.VMEM((4608, 256), BF), pltpu.VMEM((4608, 256), BF),
            pltpu.VMEM((9216, HD), BF), pltpu.VMEM((1152, HD), F32),
            pltpu.VMEM((TOK, 256), F32), pltpu.VMEM((TOK, 256), BF),
            pltpu.VMEM((6, 8, 128), jnp.int32), pltpu.VMEM((5, 8, 128), jnp.int32),
            pltpu.VMEM((32, TOK, 256), BF),
            pltpu.VMEM((512, HD), BF), pltpu.VMEM((HD, 512), BF),
            pltpu.VMEM((512, HD), BF), pltpu.VMEM((HD, 512), BF),
            pltpu.VMEM((HD, 512), F32), pltpu.VMEM((1, 512), F32),
            pltpu.VMEM((1, 512), jnp.int32), pltpu.VMEM((1, 512), jnp.int32),
            pltpu.VMEM((1, 512), F32), pltpu.VMEM((HD, 512), F32),
            pltpu.VMEM((6, 2, TOK, 256), F32),
            pltpu.VMEM((6, 2, TOK, 256), BF), pltpu.VMEM((6, 2, TOK, 256), BF),
            pltpu.VMEM((5, 2, TOK, 256), BF), pltpu.VMEM((5, 2, TOK, 256), BF),
            pltpu.VMEM((TOK, 256), BF), pltpu.VMEM((TOK, 256), BF),
            pltpu.VMEM((2, TOK, 256), BF),
            pltpu.VMEM((2, 8, 2, 144, 256), BF), pltpu.VMEM((2, 8, 2, 144, 256), BF),
            pltpu.VMEM((2, 4, 2, 144, 256), BF), pltpu.VMEM((2, 4, 2, 144, 256), BF),
            pltpu.VMEM((2, 4, 2, 144, 256), BF), pltpu.VMEM((2, 4, 2, 144, 256), BF),
            pltpu.VMEM((2, 144, 256), BF), pltpu.VMEM((2, 144, 256), BF),
            pltpu.VMEM((2, 2, 144, 256), F32),
            dma((3,)), *two((13,)), *two((13,)), *two((2, 13)), *two((5,)),
            *two((5, 2, 2)), *two((6, 2, 2)), *two((2,)), *two((6, 2)), *two((5, 2)), *two(()),
            *two((2, 8)), *two((2, 4, 2)), *two((2, 4, 2)), *two((2,)),
        ],
        compiler_params=pltpu.CompilerParams(
            collective_id=1, has_side_effects=True, vmem_limit_bytes=60 * 1024 * 1024
        ),
    )(aug_t, anc_t, pw_t, q_weight, kv_pairs, doc, d_out)


def hand_over(*refs):
    n = len(refs) // 2
    for src, dst in zip(refs[:n], refs[n:]):
        dst[...] = src[...]


def body(anchor, augment, proj_weight, q_weight, kv_weight, doc_ids, d_out):
    results = step_call(
        augment.T, anchor.T, proj_weight.T, q_weight,
        kv_weight.reshape(-1, HD), doc_ids.reshape(1, -1), d_out,
    )
    attended, grad_q, grad_kv, rows = pl.pallas_call(
        hand_over,
        out_shape=[jax.ShapeDtypeStruct(r.shape, r.dtype) for r in results],
        in_specs=[pl.BlockSpec(memory_space=pltpu.VMEM)] * 4,
        out_specs=[pl.BlockSpec(memory_space=pltpu.VMEM)] * 4,
    )(*results)
    return attended, grad_q, grad_kv.reshape(144, 1, 2, HD), rows.reshape(TOK, 1, 2, HD)


def solution(mesh):
    placed = (
        P("seq", "mp"), P("seq", "mp"), P(None, "mp"), P(None, "mp"),
        P(None, "mp", None, None), P("seq"), P("seq", "mp"),
    )
    return jax.shard_map(
        body,
        mesh=mesh,
        in_specs=placed,
        out_specs=(
            P("seq", "mp"), P("seq", "mp"),
            P("seq", "mp", None, None), P("seq", "mp", None, None),
        ),
        check_vma=False,
    )
```

```python
import functools

import jax
import jax.numpy as jnp
from jax import lax
from jax.experimental import pallas as pl
from jax.experimental.pallas import tpu as pltpu
from jax.sharding import PartitionSpec as P

BF = jnp.bfloat16
F32 = jnp.float32
TOK = 256
HALF = 128
HD = 128
MESH = pl.DeviceIdType.MESH
LOG2E = 1.4426950408889634
TN = (((0,), (0,)), ((), ()))


def remote(src, dst, send, recv, where):
    return pltpu.make_async_remote_copy(
        src_ref=src, dst_ref=dst, send_sem=send, recv_sem=recv, device_id=where, device_id_type=MESH
    )


def dot(a, b):
    return jnp.dot(a, b, preferred_element_type=F32)


def dot_tn(a, b):
    return lax.dot_general(a, b, TN, preferred_element_type=F32)


def rows_of(ref, start, size):
    return ref.at[pl.ds(pl.multiple_of(start, 16), size)]


def greet(partners):
    barrier = pltpu.get_barrier_semaphore()
    for where in partners:
        pl.semaphore_signal(barrier, inc=1, device_id=where, device_id_type=MESH)
    pl.semaphore_wait(barrier, len(partners))


class FeatureGather:
    def __init__(self, own, buf, rows, send, recv, m, lanes=pl.ds(0, TOK)):
        self.own, self.buf, self.rows, self.send, self.recv = own, buf, rows, send, recv
        self.lanes, self.m = lanes, m
        self.p = m + 1 - 2 * lax.rem(m, 2)
        self.up, self.dn = lax.rem(m + 2, 8), lax.rem(m + 6, 8)
        self.o = lax.rem(m + 4, 8)
        p = self.p
        self.p_up, self.p_dn, self.p_o = lax.rem(p + 2, 8), lax.rem(p + 6, 8), lax.rem(p + 4, 8)
        n = rows // 9
        whole, left, right = (0, 9 * n), (0, 5 * n), (5 * n, 4 * n)
        top, bottom = (0, rows // 2), (rows // 2, rows // 2)
        left0, left1 = (0, 5 * n // 2), (5 * n // 2, 5 * n // 2)
        m, p, up, dn = self.m, self.p, self.up, self.dn
        self.out = [
            (m, left, p), (m, whole, up), (m, whole, dn), (p, left, up), (p, left, dn),
            (dn, top, up), (up, bottom, dn), (self.p_dn, left0, up), (self.p_up, left1, dn),
            (m, right, p), (dn, right, p), (up, right, p), (self.o, right, p),
        ]
        self.into = [
            (p, left), (dn, whole), (up, whole), (self.p_dn, left), (self.p_up, left),
            (self.o, top), (self.o, bottom), (self.p_o, left0), (self.p_o, left1),
            (p, right), (self.p_dn, right), (self.p_up, right), (self.p_o, right),
        ]

    def part(self, block, rows):
        start = block * self.rows + rows[0]
        return self.buf.at[pl.ds(pl.multiple_of(start, 16), rows[1]), self.lanes]

    def sent(self, i):
        block, rows, to = self.out[i]
        dst = self.part(block, rows)
        src = self.own.at[pl.ds(*rows)] if i in (0, 1, 2, 9) else dst
        return remote(src, dst, self.send.at[i], self.recv.at[i], {"mp": to})

    def arrived(self, i):
        dst = self.part(*self.into[i])
        return remote(dst, dst, self.send.at[i], self.recv.at[i], {"mp": self.p})

    def start(self):
        for i in (0, 1, 2, 9):
            self.sent(i).start()

    def relay(self, stage):
        waits, sends = [
            ((0,), (3, 4)), ((1,), (5, 10)), ((2,), (6, 11)), ((3,), (7,)), ((4,), (8,)),
            ((6,), (12,)), ((5,), ()), ((9, 10, 11), ()), ((7, 8, 12), ()),
        ][stage]
        for i in waits:
            self.arrived(i).wait_recv()
        for i in sends:
            self.sent(i).start()

    def blocks(self, stage):
        return {
            1: [self.dn], 2: [self.up], 6: [self.o],
            7: [self.p, self.p_dn, self.p_up], 8: [self.p_o],
        }.get(stage, [])

    def drain(self):
        for i in range(13):
            self.sent(i).wait_send()


def needed(t, z):
    return (t >= 0) & (z <= 7) & ((t >= 2) | (z <= 5))


def step_kernel(
    aug_ref, anc_ref, pw_hbm, qw_hbm, kw_hbm, doc_ref, dout_ref,
    att_ref, gq_ref, gkv_ref, rows_ref,
    augment, anchor, projected, pw, qw, kw, kw_pairs, pairs, acc, kv_ref, cnt_out, cnt_in,
    kvs, q_n, q_t, do_n, do_t, num, den, first, place, delta, dq_t,
    mine, tosib, fromsib, ringout, ringin, xout, xin, grads,
    wsib_out, wsib_in, wd_out, wd_in, wu_out, wu_in, wx_out, wx_in, wacc,
    wsem, asend, arecv, nsend, nrecv, psend, precv, csend, crecv,
    up_s, up_r, sb_s, sb_r, xp_s, xp_r, gs_s, gs_r, rg_s, rg_r, xg_s, xg_r,
    ws_s, ws_r, wd_s, wd_r, wu_s, wu_r, wx_s, wx_r,
):
    s, m = lax.axis_index("seq"), lax.axis_index("mp")
    z, xh, c = s // 4, lax.rem(s // 2, 2), lax.rem(s, 2)
    sib = {"seq": s + 1 - 2 * c}
    xp_id = s + 2 - 4 * xh
    xp = {"seq": xp_id}
    up, dn = {"seq": lax.rem(s + 4, 32)}, {"seq": lax.rem(s + 28, 32)}
    hyper = []
    for k in range(5):
        bit = lax.rem(s // (1 << k), 2)
        hyper.append(s + (1 << k) * (1 - 2 * bit))
    loads = [
        pltpu.make_async_copy(src, dst, wsem.at[i])
        for i, (src, dst) in enumerate([(pw_hbm, pw), (qw_hbm, qw), (kw_hbm, kw_pairs)])
    ]
    for load in loads:
        load.start()
    aug = FeatureGather(aug_ref, augment, 288, asend, arecv, m)
    anc = FeatureGather(anc_ref, anchor, 576, nsend, nrecv, m)
    own_projected = rows_of(projected, m * 576, 576)
    halves = [pl.ds(h * HALF, HALF) for h in range(2)]
    pros = [
        FeatureGather(own_projected.at[:, half], projected, 576, psend.at[h], precv.at[h], m, half)
        for h, half in enumerate(halves)
    ]
    far, near = {"seq": lax.rem(s + 20, 32)}, {"seq": lax.rem(s + 12, 32)}
    across = 2 - 4 * xh
    ring = [up, dn, far, near]
    greet(
        [{"mp": aug.p}, {"mp": aug.up}, {"mp": aug.dn}] + ring
        + [{"seq": one["seq"] + across} for one in ring[:2]] + [{"seq": h} for h in hyper]
    )

    aug.start()
    doc = doc_ref[...]
    zeros = jnp.sum((1 - doc).astype(F32), axis=1, keepdims=True)
    cnt_out[0] = jnp.broadcast_to(zeros, (8, 128)).astype(jnp.int32)

    def step(k):
        return remote(cnt_out.at[k], cnt_in.at[k], csend.at[k], crecv.at[k], {"seq": hyper[k]})

    def count(k):
        step(k).wait_recv()
        cnt_out[k + 1] = cnt_out[k] + cnt_in[k]
        if k < 4:
            step(k + 1).start()

    step(0).start()
    rows_of(augment, m * 288, 288)[...] = aug_ref[...]
    rows_of(anchor, m * 576, 576)[...] = anc_ref[...]
    loads[2].wait()

    def unpair(i, carry):
        pairs[...] = kw_pairs[pl.ds(pl.multiple_of(i * 1152, 1152), 1152), :].astype(F32)
        for half in range(2):
            out = pairs[pl.ds(half, 576, stride=2), :].astype(BF)
            kw[pl.ds(pl.multiple_of(i * 576, 576), 576), half * HD:(half + 1) * HD] = out
        return carry

    lax.fori_loop(0, 2, unpair, 0)
    lanes = lax.broadcasted_iota(jnp.int32, (1, 2 * TOK), 1)
    place[...] = lax.rem(lanes, TOK) + s * TOK
    for h in range(2):
        cut = slice(h * TOK, (h + 1) * TOK)
        head = slice(h * HD, (h + 1) * HD)
        do_n[cut, :] = dout_ref[:, head]
        do_t[:, cut] = dout_ref[:, head].T
    loads[0].wait()
    loads[1].wait()
    for stage in range(9):
        aug.relay(stage)
        if stage == 4:
            anc.start()
            lax.fori_loop(2, 6, unpair, 0)
    own_projected[...] = dot(pw[...], augment[...]).astype(BF)
    pros[0].start()
    count(0)
    lax.fori_loop(6, 8, unpair, 0)

    def add(block):
        acc[...] += dot_tn(rows_of(anchor, block * 576, 576)[...], rows_of(qw, block * 576, 576)[...])

    def add_kv(h, block):
        piece = projected[pl.ds(pl.multiple_of(block * 576, 16), 576), halves[h]]
        acc[halves[h]] += dot_tn(piece, rows_of(kw, block * 576, 576)[...])

    def half_copy(src, block, h, send, recv, where):
        dst = kvs.at[block, halves[h]]
        return remote(dst if src is None else src.at[halves[h]], dst, send, recv, where)

    def lane(t, j):
        return 4 * t + 2 * j + c

    def piece(k):
        return lax.rem(xh + k, 2)

    def to_up(g, h, src=None):
        return half_copy(src, lane(z - g, xh), h, up_s.at[g, h], up_r.at[g, h], up)

    def to_far(h, src=None):
        return half_copy(src, lane(z, xh), h, up_s.at[4, h], up_r.at[4, h], far)

    def to_xp(g, h, src=None):
        return half_copy(src, lane(z - g, xh), h, xp_s.at[g, h], xp_r.at[g, h], xp)

    def to_sib(g, k, h, src=None):
        return half_copy(src, lane(z - g, piece(k)), h, sb_s.at[g, k, h], sb_r.at[g, k, h], sib)

    def from_sib(g, k, h):
        b = 4 * (z - g) + 2 * piece(k) + 1 - c
        return half_copy(None, b, h, sb_s.at[g, k, h], sb_r.at[g, k, h], sib)

    def from_dn(g, h):
        return half_copy(None, lane(z - g, xh), h, up_s.at[g - 1, h], up_r.at[g - 1, h], dn)

    def from_xp(g, h):
        return half_copy(None, lane(z - g, 1 - xh), h, xp_s.at[g, h], xp_r.at[g, h], xp)

    def up_needs(g):
        return (g < 4) & needed(z - g, z + 1)

    far_needs = needed(z, z + 5)

    def launch(h):
        kv_ref[halves[h]] = acc[halves[h]].astype(BF)

        @pl.when(up_needs(0))
        def _():
            to_up(0, h, kv_ref).start()

        to_xp(0, h, kv_ref).start()
        to_sib(0, 0, h, kv_ref).start()

        @pl.when(far_needs)
        def _():
            to_far(h, kv_ref).start()

        kvs[s, halves[h]] = kv_ref[halves[h]]

    def pass_on(g, h):
        @pl.when(needed(z - g, z))
        def _():
            from_dn(g, h).wait_recv()

            @pl.when(up_needs(g))
            def _():
                to_up(g, h).start()

            to_xp(g, h).start()
            to_sib(g, 0, h).start()

    def crossed(g, h):
        @pl.when(needed(z - g, z))
        def _():
            from_xp(g, h).wait_recv()
            to_sib(g, 1, h).start()

    acc[...] = jnp.zeros_like(acc)
    def gather(h, *stages):
        for stage in stages:
            pros[h].relay(stage)
            for block in pros[h].blocks(stage):
                add_kv(h, block)

    add_kv(0, m)
    gather(0, 0, 1, 2, 3, 4)
    pros[1].start()
    for stage in range(3):
        anc.relay(stage)
    count(1)
    add_kv(1, m)
    gather(0, 5, 6, 7)
    pros[1].relay(0)
    gather(0, 8)
    launch(0)
    count(2)
    gather(1, 1, 2, 3, 4)
    pass_on(1, 0)
    for stage in range(3, 6):
        anc.relay(stage)
    count(3)
    gather(1, 5, 6)
    pass_on(2, 0)
    gather(1, 7, 8)
    launch(1)
    pass_on(3, 0)
    count(4)
    for h in range(2):
        first[:, h * TOK:(h + 1) * TOK] = doc * cnt_out[5, 0:1, 0:1]
    num[...] = jnp.zeros_like(num)
    den[...] = jnp.zeros_like(den)
    dq_t[...] = jnp.zeros_like(dq_t)
    crossed(0, 0)

    def scores(block):
        k, v = kvs[block, :, :HD], kvs[block, :, HD:]
        th = jnp.tanh(dot(k, q_t[...]) * (1.0 / 600.0))
        pos = block * TOK + lax.broadcasted_iota(jnp.int32, (TOK, 2 * TOK), 0)
        allowed = (pos >= first[...]) & (pos <= place[...])
        return k, v, th, jnp.where(allowed, jnp.exp2(th * (50.0 * LOG2E)), 0.0)

    def forward(g):
        def one(b, carry):
            block = 4 * (z - g) + b

            @pl.when(block <= s)
            def _():
                _, v, _, w = scores(block)
                den[...] += jnp.sum(w, axis=0, keepdims=True)
                num[...] += dot_tn(v, w.astype(BF))

            return carry

        lax.fori_loop(0, 4, one, 0)

    acc[...] = jnp.zeros_like(acc)
    for block in (m, anc.dn, anc.up):
        add(block)
    for stage in range(6, 9):
        anc.relay(stage)
        for block in anc.blocks(stage):
            add(block)
    pass_on(1, 1)
    pass_on(4, 0)
    crossed(1, 0)
    crossed(0, 1)

    query = acc[...].astype(BF)
    for h in range(2):
        cut = slice(h * TOK, (h + 1) * TOK)
        head = slice(h * HD, (h + 1) * HD)
        q_n[cut, :] = query[:, head]
        q_t[:, cut] = query[:, head].T

    def forward_step(g):
        @pl.when(needed(z - g, z))
        def _():
            for h in range(2):
                for k in range(2):
                    from_sib(g, k, h).wait_recv()
            forward(g)

    pass_on(2, 1)
    crossed(1, 1)
    forward_step(0)
    pass_on(3, 1)
    crossed(2, 0)
    crossed(2, 1)
    forward_step(1)
    pass_on(4, 1)
    crossed(3, 0)
    crossed(3, 1)
    pass_on(5, 0)
    pass_on(5, 1)
    forward_step(2)
    for g in (4, 5):
        for h in range(2):
            crossed(g, h)
    forward_step(3)
    forward_step(5)
    forward_step(4)

    attended = (num[...] * (1.0 / den[...])).astype(BF)
    delta[...] = jnp.sum(do_t[...].astype(F32) * attended.astype(F32), axis=0, keepdims=True)
    den[...] = 1.0 / den[...]
    for h in range(2):
        att_ref[:, h * HD:(h + 1) * HD] = attended[:, h * TOK:(h + 1) * TOK].T

    def there(where, k):
        return {"seq": where["seq"] + k * across}

    def ring_out(g, h, where=dn):
        return remote(ringout.at[g - 1, h], ringin.at[g - 1, h], rg_s.at[g - 1, h], rg_r.at[g - 1, h], where)

    def ring_in(g, h):
        return remote(ringout.at[g, h], ringin.at[g, h], rg_s.at[g, h], rg_r.at[g, h], up)

    def sib_grad(g, k):
        return remote(tosib.at[g, k], fromsib.at[g, k], gs_s.at[g, k], gs_r.at[g, k], sib)

    def x_grad(g, h):
        return remote(xout.at[g, h], xin.at[g, h], xg_s.at[g, h], xg_r.at[g, h], xp)

    def backward(block, write):
        k, v, th, w = scores(block)
        prob = w * den[...]
        soft = prob * (dot(v, do_t[...]) - delta[...])
        raw = (soft * ((1.0 - th * th) * (1.0 / 12.0))).astype(BF)
        write(dot(raw, q_n[...]), dot(prob.astype(BF), do_n[...]))
        dq_t[...] += dot_tn(k, raw)

    def contributions(g):
        def for_sib(i, carry):
            k = 1 - i
            block = 4 * (z - g) + 2 * piece(k) + 1 - c

            @pl.when(block <= s)
            def _():
                def write(gk, gv):
                    tosib[g, k, :, :HD] = gk.astype(BF)
                    tosib[g, k, :, HD:] = gv.astype(BF)

                backward(block, write)

            @pl.when(block > s)
            def _():
                tosib[g, k] = jnp.zeros((TOK, 256), BF)

            sib_grad(g, k).start()
            return carry

        def for_me(i, carry):
            k = 1 - i
            block = lane(z - g, piece(k))

            @pl.when(block <= s)
            def _():
                def write(gk, gv):
                    mine[g, k, :, :HD] = gk
                    mine[g, k, :, HD:] = gv

                backward(block, write)

            @pl.when(block > s)
            def _():
                mine[g, k] = jnp.zeros((TOK, 256), F32)

            @pl.when(k == 1)
            def _():
                sib_grad(g, 1).wait_recv()
                for h in range(2):
                    xout[g, h] = (mine[g, 1, halves[h]] + fromsib[g, 1, halves[h]].astype(F32)).astype(BF)
                    x_grad(g, h).start()

            return carry

        lax.fori_loop(0, 2, for_sib, 0)
        lax.fori_loop(0, 2, for_me, 0)

    def contribute(g):
        @pl.when(needed(z - g, z))
        def _():
            contributions(g)

    def collect(g, h):
        if h == 0:
            sib_grad(g, 0).wait_recv()
        x_grad(g, h).wait_recv()
        half = halves[h]
        mine[g, 0, half] += fromsib[g, 0, half].astype(F32) + xin[g, h].astype(F32)

        @pl.when(up_needs(g))
        def _():
            ring_in(g, h).wait_recv()
            mine[g, 0, half] += ringin[g, h].astype(F32)

    def send_sum(g):
        @pl.when(needed(z - g, z))
        def _():
            for h in range(2):
                collect(g, h)
                ringout[g - 1, h] = mine[g, 0, halves[h]].astype(BF)
                ring_out(g, h, near if g == 5 else dn).start()

    contribute(4)
    send_sum(4)
    contribute(3)
    contribute(2)
    send_sum(3)
    contribute(5)
    send_sum(5)
    send_sum(2)
    contribute(1)
    send_sum(1)
    contribute(0)

    def weight(n, act, lengths):
        grad = grads.at[n]

        def partial(t, j, core):
            return dot(rows_of(act, t * 576 + j * 288 + core * 144, 144)[...], grad[...])

        def sib_copy(t):
            return remote(wsib_out.at[n, t], wsib_in.at[n, t], ws_s.at[n, t], ws_r.at[n, t], sib)

        def target(k, way):
            return lax.rem(z + 8 - lengths[0] + k, 8) if way == 0 else lax.rem(z + 8 + lengths[1] - k, 8)

        def push(*targets):
            for t in targets:
                for j in range(2):
                    wsib_out[n, t, j] = partial(t, j, 1 - c).astype(BF)
                sib_copy(t).start()

        def push_for(k):
            push(*[target(k, way) for way in range(2) if k < lengths[way]])

        def hop(k, way, q):
            out, into = (wd_out, wd_in) if way == 0 else (wu_out, wu_in)
            ss, rr = (wd_s, wd_r) if way == 0 else (wu_s, wu_r)
            where = dn if way == 0 else up
            if k == lengths[way] - 1:
                where = there(where, q)
            return remote(out.at[n, k, q], into.at[n, k, q], ss.at[n, k, q], rr.at[n, k, q], where)

        def hop_step(k, way):
            out, into = (wd_out, wd_in) if way == 0 else (wu_out, wu_in)
            t = target(k, way)
            sib_copy(t).wait_recv()
            for q in (1, 0):
                total = partial(t, piece(q), c) + wsib_in[n, t, piece(q)].astype(F32)
                if k > 0:
                    hop(k - 1, way, q).wait_recv()
                    total += into[n, k - 1, q].astype(F32)
                out[n, k, q] = total.astype(BF)
                hop(k, way, q).start()

        def step(k):
            for way in range(2):
                if k < lengths[way]:
                    hop_step(k, way)

        def x_copy():
            return remote(wx_out.at[n], wx_in.at[n], wx_s.at[n], wx_r.at[n], xp)

        def cross():
            sib_copy(z).wait_recv()
            for q in (1, 0):
                wacc[n, q] = partial(z, piece(q), c) + wsib_in[n, z, piece(q)].astype(F32)
            wx_out[n] = wacc[n, 1].astype(BF)
            x_copy().start()

        def meet():
            x_copy().wait_recv()
            total = wacc[n, 0] + wx_in[n].astype(F32)
            for way, into in enumerate((wd_in, wu_in)):
                for q in range(2):
                    hop(lengths[way] - 1, way, q).wait_recv()
                    total += into[n, lengths[way] - 1, q].astype(F32)
            return total

        def drain():
            for t in range(8):
                sib_copy(t).wait_send()
            for way in range(2):
                for k in range(lengths[way]):
                    for q in range(2):
                        hop(k, way, q).wait_send()
            x_copy().wait_send()

        return push, push_for, step, cross, meet, drain

    push_q, push_q_for, step_q, cross_q, meet_q, drain_q = weight(0, anchor, (3, 4))
    push_kv, push_kv_for, step_kv, cross_kv, meet_kv, drain_kv = weight(1, projected, (4, 3))
    for h in range(2):
        grads[0, :, h * HD:(h + 1) * HD] = dq_t[:, h * TOK:(h + 1) * TOK].T.astype(BF)
    push_q_for(0)
    push_q_for(1)
    step_q(0)
    push_q_for(2)
    push_q_for(3)
    push_q(z)
    for h in range(2):
        @pl.when(far_needs)
        def _():
            ring_in(4, h).wait_recv()
            mine[0, 0, halves[h]] += ringin[4, h].astype(F32)

        collect(0, h)
        grads[1, halves[h]] = mine[0, 0, halves[h]].astype(BF)

    push_kv_for(0)
    step_kv(0)
    push_kv_for(1)
    step_q(1)
    push_kv_for(2)
    step_kv(1)
    step_q(2)
    push_kv_for(3)
    push_kv(z)
    step_kv(2)
    cross_kv()
    cross_q()
    step_kv(3)
    step_q(3)
    for half in range(2):
        pairs[pl.ds(half, TOK, stride=2), :] = grads[1, :, half * HD:(half + 1) * HD].astype(F32)
    rows_ref[...] = pairs[:2 * TOK, :].astype(BF)
    gq_ref[...] = meet_q()
    wacc[1, 0] = meet_kv()
    for half in range(2):
        gkv_ref[pl.ds(half, 144, stride=2), :] = wacc[1, 0, :, half * HD:(half + 1) * HD]

    for h in range(2):
        @pl.when(far_needs)
        def _():
            to_far(h).wait_send()

    drain_q()
    drain_kv()
    aug.drain()
    anc.drain()
    pros[0].drain()
    pros[1].drain()
    for k in range(5):
        step(k).wait_send()

    def drained(g, carry):
        @pl.when(needed(z - g, z))
        def _():
            for h in range(2):
                sib_grad(g, h).wait_send()
                x_grad(g, h).wait_send()
                to_xp(g, h).wait_send()
                for k in range(2):
                    to_sib(g, k, h).wait_send()

                @pl.when(up_needs(g))
                def _():
                    to_up(g, h).wait_send()

                @pl.when(g > 0)
                def _():
                    ring_out(g, h).wait_send()

        return carry

    lax.fori_loop(0, 6, drained, 0)


def step_call(aug_t, anc_t, pw_t, q_weight, kv_pairs, doc, d_out):
    dma = pltpu.SemaphoreType.DMA
    vmem = pl.BlockSpec(memory_space=pltpu.VMEM)
    hbm = pl.BlockSpec(memory_space=pl.ANY)
    two = lambda n: [dma(n), dma(n)]
    return pl.pallas_call(
        step_kernel,
        out_shape=[
            jax.ShapeDtypeStruct((TOK, 256), BF),
            jax.ShapeDtypeStruct((144, 256), F32),
            jax.ShapeDtypeStruct((288, HD), F32),
            jax.ShapeDtypeStruct((2 * TOK, HD), BF),
        ],
        in_specs=[vmem, vmem, hbm, hbm, hbm, vmem, vmem],
        out_specs=[vmem] * 4,
        scratch_shapes=[
            pltpu.VMEM((2304, TOK), BF), pltpu.VMEM((4608, TOK), BF), pltpu.VMEM((4608, TOK), BF),
            pltpu.VMEM((576, 2304), BF), pltpu.VMEM((4608, 256), BF), pltpu.VMEM((4608, 256), BF),
            pltpu.VMEM((9216, HD), BF), pltpu.VMEM((1152, HD), F32),
            pltpu.VMEM((TOK, 256), F32), pltpu.VMEM((TOK, 256), BF),
            pltpu.VMEM((6, 8, 128), jnp.int32), pltpu.VMEM((5, 8, 128), jnp.int32),
            pltpu.VMEM((32, TOK, 256), BF),
            pltpu.VMEM((512, HD), BF), pltpu.VMEM((HD, 512), BF),
            pltpu.VMEM((512, HD), BF), pltpu.VMEM((HD, 512), BF),
            pltpu.VMEM((HD, 512), F32), pltpu.VMEM((1, 512), F32),
            pltpu.VMEM((1, 512), jnp.int32), pltpu.VMEM((1, 512), jnp.int32),
            pltpu.VMEM((1, 512), F32), pltpu.VMEM((HD, 512), F32),
            pltpu.VMEM((6, 2, TOK, 256), F32),
            pltpu.VMEM((6, 2, TOK, 256), BF), pltpu.VMEM((6, 2, TOK, 256), BF),
            pltpu.VMEM((5, 2, HALF, 256), BF), pltpu.VMEM((5, 2, HALF, 256), BF),
            pltpu.VMEM((6, 2, HALF, 256), BF), pltpu.VMEM((6, 2, HALF, 256), BF),
            pltpu.VMEM((2, TOK, 256), BF),
            pltpu.VMEM((2, 8, 2, 144, 256), BF), pltpu.VMEM((2, 8, 2, 144, 256), BF),
            pltpu.VMEM((2, 4, 2, 144, 256), BF), pltpu.VMEM((2, 4, 2, 144, 256), BF),
            pltpu.VMEM((2, 4, 2, 144, 256), BF), pltpu.VMEM((2, 4, 2, 144, 256), BF),
            pltpu.VMEM((2, 144, 256), BF), pltpu.VMEM((2, 144, 256), BF),
            pltpu.VMEM((2, 2, 144, 256), F32),
            dma((3,)), *two((13,)), *two((13,)), *two((2, 13)), *two((5,)),
            *two((5, 2)), *two((6, 2, 2)), *two((6, 2)), *two((6, 2)), *two((5, 2)), *two((6, 2)),
            *two((2, 8)), *two((2, 4, 2)), *two((2, 4, 2)), *two((2,)),
        ],
        compiler_params=pltpu.CompilerParams(
            collective_id=1, has_side_effects=True, vmem_limit_bytes=60 * 1024 * 1024
        ),
    )(aug_t, anc_t, pw_t, q_weight, kv_pairs, doc, d_out)


def hand_over(*refs):
    n = len(refs) // 2
    for src, dst in zip(refs[:n], refs[n:]):
        dst[...] = src[...]


def body(anchor, augment, proj_weight, q_weight, kv_weight, doc_ids, d_out):
    results = step_call(
        augment.T, anchor.T, proj_weight.T, q_weight,
        kv_weight.reshape(-1, HD), doc_ids.reshape(1, -1), d_out,
    )
    attended, grad_q, grad_kv, rows = pl.pallas_call(
        hand_over,
        out_shape=[jax.ShapeDtypeStruct(r.shape, r.dtype) for r in results],
        in_specs=[pl.BlockSpec(memory_space=pltpu.VMEM)] * 4,
        out_specs=[pl.BlockSpec(memory_space=pltpu.VMEM)] * 4,
    )(*results)
    return attended, grad_q, grad_kv.reshape(144, 1, 2, HD), rows.reshape(TOK, 1, 2, HD)


def solution(mesh):
    placed = (
        P("seq", "mp"), P("seq", "mp"), P(None, "mp"), P(None, "mp"),
        P(None, "mp", None, None), P("seq"), P("seq", "mp"),
    )
    return jax.shard_map(
        body,
        mesh=mesh,
        in_specs=placed,
        out_specs=(
            P("seq", "mp"), P("seq", "mp"),
            P("seq", "mp", None, None), P("seq", "mp", None, None),
        ),
        check_vma=False,
    )
```

```python
import functools

import jax
import jax.numpy as jnp
from jax import lax
from jax.experimental import pallas as pl
from jax.experimental.pallas import tpu as pltpu
from jax.sharding import PartitionSpec as P

BF = jnp.bfloat16
F32 = jnp.float32
TOK = 256
HALF = 128
GROUP = 1024
HD = 128
MESH = pl.DeviceIdType.MESH
LOG2E = 1.4426950408889634
TN = (((0,), (0,)), ((), ()))


def remote(src, dst, send, recv, where):
    return pltpu.make_async_remote_copy(
        src_ref=src, dst_ref=dst, send_sem=send, recv_sem=recv, device_id=where, device_id_type=MESH
    )


def dot(a, b):
    return jnp.dot(a, b, preferred_element_type=F32)


def dot_tn(a, b):
    return lax.dot_general(a, b, TN, preferred_element_type=F32)


def rows_of(ref, start, size):
    return ref.at[pl.ds(pl.multiple_of(start, 16), size)]


def greet(partners):
    barrier = pltpu.get_barrier_semaphore()
    for where in partners:
        pl.semaphore_signal(barrier, inc=1, device_id=where, device_id_type=MESH)
    pl.semaphore_wait(barrier, len(partners))


class FeatureGather:
    def __init__(self, own, buf, rows, send, recv, m, lanes=pl.ds(0, TOK)):
        self.own, self.buf, self.rows, self.send, self.recv = own, buf, rows, send, recv
        self.lanes, self.m = lanes, m
        self.p = m + 1 - 2 * lax.rem(m, 2)
        self.up, self.dn = lax.rem(m + 2, 8), lax.rem(m + 6, 8)
        self.o = lax.rem(m + 4, 8)
        p = self.p
        self.p_up, self.p_dn, self.p_o = lax.rem(p + 2, 8), lax.rem(p + 6, 8), lax.rem(p + 4, 8)
        n = rows // 9
        whole, left, right = (0, 9 * n), (0, 5 * n), (5 * n, 4 * n)
        top, bottom = (0, rows // 2), (rows // 2, rows // 2)
        left0, left1 = (0, 5 * n // 2), (5 * n // 2, 5 * n // 2)
        m, p, up, dn = self.m, self.p, self.up, self.dn
        self.out = [
            (m, left, p), (m, whole, up), (m, whole, dn), (p, left, up), (p, left, dn),
            (dn, top, up), (up, bottom, dn), (self.p_dn, left0, up), (self.p_up, left1, dn),
            (m, right, p), (dn, right, p), (up, right, p), (self.o, right, p),
        ]
        self.into = [
            (p, left), (dn, whole), (up, whole), (self.p_dn, left), (self.p_up, left),
            (self.o, top), (self.o, bottom), (self.p_o, left0), (self.p_o, left1),
            (p, right), (self.p_dn, right), (self.p_up, right), (self.p_o, right),
        ]

    def part(self, block, rows):
        start = block * self.rows + rows[0]
        return self.buf.at[pl.ds(pl.multiple_of(start, 16), rows[1]), self.lanes]

    def sent(self, i):
        block, rows, to = self.out[i]
        dst = self.part(block, rows)
        src = self.own.at[pl.ds(*rows)] if i in (0, 1, 2, 9) else dst
        return remote(src, dst, self.send.at[i], self.recv.at[i], {"mp": to})

    def arrived(self, i):
        dst = self.part(*self.into[i])
        return remote(dst, dst, self.send.at[i], self.recv.at[i], {"mp": self.p})

    def start(self):
        for i in (0, 1, 2, 9):
            self.sent(i).start()

    def relay(self, stage):
        waits, sends = [
            ((0,), (3, 4)), ((1,), (5, 10)), ((2,), (6, 11)), ((3,), (7,)), ((4,), (8,)),
            ((6,), (12,)), ((5,), ()), ((9, 10, 11), ()), ((7, 8, 12), ()),
        ][stage]
        for i in waits:
            self.arrived(i).wait_recv()
        for i in sends:
            self.sent(i).start()

    def blocks(self, stage):
        return {
            1: [self.dn], 2: [self.up], 6: [self.o],
            7: [self.p, self.p_dn, self.p_up], 8: [self.p_o],
        }.get(stage, [])

    def drain(self):
        for i in range(13):
            self.sent(i).wait_send()


def needed(t, z):
    return (t >= 0) & (z <= 7) & ((t >= 2) | (z <= 5))


def step_kernel(
    aug_ref, anc_ref, pw_hbm, qw_hbm, kw_hbm, doc_ref, dout_ref,
    att_ref, gq_ref, gkv_ref, rows_ref,
    augment, anchor, projected, pw, qw, kw, kw_pairs, pairs, acc, kv_ref, cnt_out, cnt_in,
    kvs, q_n, q_t, do_n, do_t, num, den, first, place, delta, dq_t,
    mine, parts, tosib, fromsib, ringout, ringin, xout, xin, grads,
    wsib_out, wsib_in, wd_out, wd_in, wu_out, wu_in, wx_out, wx_in, wacc,
    wsem, asend, arecv, nsend, nrecv, psend, precv, csend, crecv,
    up_s, up_r, sb_s, sb_r, xp_s, xp_r, gs_s, gs_r, rg_s, rg_r, xg_s, xg_r,
    ws_s, ws_r, wd_s, wd_r, wu_s, wu_r, wx_s, wx_r,
):
    s, m = lax.axis_index("seq"), lax.axis_index("mp")
    z, xh, c = s // 4, lax.rem(s // 2, 2), lax.rem(s, 2)
    sib = {"seq": s + 1 - 2 * c}
    xp_id = s + 2 - 4 * xh
    xp = {"seq": xp_id}
    up, dn = {"seq": lax.rem(s + 4, 32)}, {"seq": lax.rem(s + 28, 32)}
    hyper = []
    for k in range(5):
        bit = lax.rem(s // (1 << k), 2)
        hyper.append(s + (1 << k) * (1 - 2 * bit))
    loads = [
        pltpu.make_async_copy(src, dst, wsem.at[i])
        for i, (src, dst) in enumerate([(pw_hbm, pw), (qw_hbm, qw), (kw_hbm, kw_pairs)])
    ]
    for load in loads:
        load.start()
    aug = FeatureGather(aug_ref, augment, 288, asend, arecv, m)
    anc = FeatureGather(anc_ref, anchor, 576, nsend, nrecv, m)
    own_projected = rows_of(projected, m * 576, 576)
    halves = [pl.ds(h * HALF, HALF) for h in range(2)]
    pros = [
        FeatureGather(own_projected.at[:, half], projected, 576, psend.at[h], precv.at[h], m, half)
        for h, half in enumerate(halves)
    ]
    far, near = {"seq": lax.rem(s + 20, 32)}, {"seq": lax.rem(s + 12, 32)}
    across = 2 - 4 * xh
    ring = [up, dn, far, near]
    greet(
        [{"mp": aug.p}, {"mp": aug.up}, {"mp": aug.dn}] + ring
        + [{"seq": one["seq"] + across} for one in ring] + [{"seq": h} for h in hyper]
    )

    aug.start()
    doc = doc_ref[...]
    zeros = jnp.sum((1 - doc).astype(F32), axis=1, keepdims=True)
    cnt_out[0] = jnp.broadcast_to(zeros, (8, 128)).astype(jnp.int32)

    def step(k):
        return remote(cnt_out.at[k], cnt_in.at[k], csend.at[k], crecv.at[k], {"seq": hyper[k]})

    def count(k):
        step(k).wait_recv()
        cnt_out[k + 1] = cnt_out[k] + cnt_in[k]
        if k < 4:
            step(k + 1).start()

    step(0).start()
    rows_of(augment, m * 288, 288)[...] = aug_ref[...]
    rows_of(anchor, m * 576, 576)[...] = anc_ref[...]
    loads[2].wait()

    def unpair(i, carry):
        pairs[...] = kw_pairs[pl.ds(pl.multiple_of(i * 1152, 1152), 1152), :].astype(F32)
        for half in range(2):
            out = pairs[pl.ds(half, 576, stride=2), :].astype(BF)
            kw[pl.ds(pl.multiple_of(i * 576, 576), 576), half * HD:(half + 1) * HD] = out
        return carry

    lax.fori_loop(0, 2, unpair, 0)
    lanes = lax.broadcasted_iota(jnp.int32, (1, 2 * TOK), 1)
    place[...] = lax.rem(lanes, TOK) + s * TOK
    for h in range(2):
        cut = slice(h * TOK, (h + 1) * TOK)
        head = slice(h * HD, (h + 1) * HD)
        do_n[cut, :] = dout_ref[:, head]
        do_t[:, cut] = dout_ref[:, head].T
    loads[0].wait()
    loads[1].wait()
    for stage in range(9):
        aug.relay(stage)
        if stage == 4:
            anc.start()
            lax.fori_loop(2, 6, unpair, 0)
    own_projected[...] = dot(pw[...], augment[...]).astype(BF)
    pros[0].start()
    count(0)
    lax.fori_loop(6, 8, unpair, 0)

    def add(block):
        acc[...] += dot_tn(rows_of(anchor, block * 576, 576)[...], rows_of(qw, block * 576, 576)[...])

    def add_kv(h, block):
        piece = projected[pl.ds(pl.multiple_of(block * 576, 16), 576), halves[h]]
        acc[halves[h]] += dot_tn(piece, rows_of(kw, block * 576, 576)[...])

    def half_copy(src, block, h, send, recv, where):
        dst = kvs.at[block, halves[h]]
        return remote(dst if src is None else src.at[halves[h]], dst, send, recv, where)

    def lane(t, j):
        return 4 * t + 2 * j + c

    def piece(k):
        return lax.rem(xh + k, 2)

    def to_up(g, h, src=None):
        return half_copy(src, lane(z - g, xh), h, up_s.at[g, h], up_r.at[g, h], up)

    def to_far(h, src=None):
        return half_copy(src, lane(z, xh), h, up_s.at[4, h], up_r.at[4, h], far)

    def to_xp(g, h, src=None):
        return half_copy(src, lane(z - g, xh), h, xp_s.at[g, h], xp_r.at[g, h], xp)

    def to_sib(g, k, h, src=None):
        return half_copy(src, lane(z - g, piece(k)), h, sb_s.at[g, k, h], sb_r.at[g, k, h], sib)

    def from_sib(g, k, h):
        b = 4 * (z - g) + 2 * piece(k) + 1 - c
        return half_copy(None, b, h, sb_s.at[g, k, h], sb_r.at[g, k, h], sib)

    def from_dn(g, h):
        return half_copy(None, lane(z - g, xh), h, up_s.at[g - 1, h], up_r.at[g - 1, h], dn)

    def from_xp(g, h):
        return half_copy(None, lane(z - g, 1 - xh), h, xp_s.at[g, h], xp_r.at[g, h], xp)

    def up_needs(g):
        return (g < 4) & needed(z - g, z + 1)

    far_needs = needed(z, z + 5)

    def launch(h):
        kv_ref[halves[h]] = acc[halves[h]].astype(BF)

        @pl.when(up_needs(0))
        def _():
            to_up(0, h, kv_ref).start()

        to_xp(0, h, kv_ref).start()
        to_sib(0, 0, h, kv_ref).start()

        @pl.when(far_needs)
        def _():
            to_far(h, kv_ref).start()

        kvs[s, halves[h]] = kv_ref[halves[h]]

    def pass_on(g, h):
        @pl.when(needed(z - g, z))
        def _():
            from_dn(g, h).wait_recv()

            @pl.when(up_needs(g))
            def _():
                to_up(g, h).start()

            to_xp(g, h).start()
            to_sib(g, 0, h).start()

    def crossed(g, h):
        @pl.when(needed(z - g, z))
        def _():
            from_xp(g, h).wait_recv()
            to_sib(g, 1, h).start()

    acc[...] = jnp.zeros_like(acc)
    def gather(h, *stages):
        for stage in stages:
            pros[h].relay(stage)
            for block in pros[h].blocks(stage):
                add_kv(h, block)

    add_kv(0, m)
    gather(0, 0, 1, 2, 3, 4)
    pros[1].start()
    for stage in range(3):
        anc.relay(stage)
    count(1)
    add_kv(1, m)
    gather(0, 5, 6, 7)
    pros[1].relay(0)
    gather(0, 8)
    launch(0)
    count(2)
    gather(1, 1, 2, 3, 4)
    pass_on(1, 0)
    for stage in range(3, 6):
        anc.relay(stage)
    count(3)
    gather(1, 5, 6)
    pass_on(2, 0)
    gather(1, 7, 8)
    launch(1)
    pass_on(3, 0)
    count(4)
    for h in range(2):
        first[:, h * TOK:(h + 1) * TOK] = doc * cnt_out[5, 0:1, 0:1]
    num[...] = jnp.zeros_like(num)
    den[...] = jnp.zeros_like(den)
    dq_t[...] = jnp.zeros_like(dq_t)
    crossed(0, 0)

    def scores(g):
        base = 4 * (z - g)
        kv = kvs[pl.ds(base, 4)].reshape(GROUP, 256)
        k, v = kv[:, :HD], kv[:, HD:]
        th = jnp.tanh(dot(k, q_t[...]) * (1.0 / 600.0))
        pos = lax.broadcasted_iota(jnp.int32, (GROUP, 2 * TOK), 0)
        allowed = (pos >= first[...] - base * TOK) & (pos <= place[...] - base * TOK)
        return k, v, th, jnp.where(allowed, jnp.exp2(th * (50.0 * LOG2E)), 0.0)

    def forward(g):
        _, v, _, w = scores(g)
        den[...] += jnp.sum(w, axis=0, keepdims=True)
        num[...] += dot_tn(v, w.astype(BF))

    acc[...] = jnp.zeros_like(acc)
    for block in (m, anc.dn, anc.up):
        add(block)
    for stage in range(6, 9):
        anc.relay(stage)
        for block in anc.blocks(stage):
            add(block)
    pass_on(1, 1)
    pass_on(4, 0)
    crossed(1, 0)
    crossed(0, 1)

    query = acc[...].astype(BF)
    for h in range(2):
        cut = slice(h * TOK, (h + 1) * TOK)
        head = slice(h * HD, (h + 1) * HD)
        q_n[cut, :] = query[:, head]
        q_t[:, cut] = query[:, head].T

    def forward_step(g):
        @pl.when(needed(z - g, z))
        def _():
            for h in range(2):
                for k in range(2):
                    from_sib(g, k, h).wait_recv()
            forward(g)

    pass_on(2, 1)
    crossed(1, 1)
    forward_step(0)
    pass_on(3, 1)
    crossed(2, 0)
    crossed(2, 1)
    forward_step(1)
    pass_on(4, 1)
    crossed(3, 0)
    crossed(3, 1)
    pass_on(5, 0)
    pass_on(5, 1)
    forward_step(2)
    for g in (4, 5):
        for h in range(2):
            crossed(g, h)
    forward_step(3)
    forward_step(5)
    forward_step(4)

    attended = (num[...] * (1.0 / den[...])).astype(BF)
    delta[...] = jnp.sum(do_t[...].astype(F32) * attended.astype(F32), axis=0, keepdims=True)
    den[...] = 1.0 / den[...]
    for h in range(2):
        att_ref[:, h * HD:(h + 1) * HD] = attended[:, h * TOK:(h + 1) * TOK].T

    def there(where, k):
        return {"seq": where["seq"] + k * across}

    def ring_out(g, k, h, last=False):
        where = there(near if g == 5 else dn, k) if last else dn
        return remote(
            ringout.at[g - 1, k, h], ringin.at[g - 1, k, h], rg_s.at[g - 1, k, h], rg_r.at[g - 1, k, h], where
        )

    def ring_in(g, k, h):
        return remote(ringout.at[g, k, h], ringin.at[g, k, h], rg_s.at[g, k, h], rg_r.at[g, k, h], up)

    def sib_grad(g, k):
        return remote(tosib.at[g, k], fromsib.at[g, k], gs_s.at[g, k], gs_r.at[g, k], sib)

    def contribute(g):
        @pl.when(needed(z - g, z))
        def _():
            k, v, th, w = scores(g)
            prob = w * den[...]
            soft = prob * (dot(v, do_t[...]) - delta[...])
            raw = (soft * ((1.0 - th * th) * (1.0 / 12.0))).astype(BF)
            parts[:, :HD] = dot(raw, q_n[...])
            parts[:, HD:] = dot(prob.astype(BF), do_n[...])
            for q in (1, 0):
                start = (2 * piece(q) + 1 - c) * TOK
                tosib[g, q] = parts[pl.ds(pl.multiple_of(start, TOK), TOK), :].astype(BF)
                sib_grad(g, q).start()
            for q in (1, 0):
                start = (2 * piece(q) + c) * TOK
                mine[g, q] = parts[pl.ds(pl.multiple_of(start, TOK), TOK), :]
            dq_t[...] += dot_tn(k, raw)

    def send_sum(g):
        @pl.when(needed(z - g, z))
        def _():
            for k in (1, 0):
                sib_grad(g, k).wait_recv()
                for h, half in enumerate(halves):
                    mine[g, k, half] += fromsib[g, k, half].astype(F32)

                    @pl.when(up_needs(g))
                    def _():
                        ring_in(g, k, h).wait_recv()
                        mine[g, k, half] += ringin[g, k, h].astype(F32)

                    ringout[g - 1, k, h] = mine[g, k, half].astype(BF)
                    ring_out(g, k, h, g in (1, 5)).start()

    contribute(4)
    send_sum(4)
    contribute(3)
    contribute(2)
    send_sum(3)
    contribute(1)
    contribute(5)
    send_sum(5)
    send_sum(2)
    contribute(0)

    def weight(n, act, lengths):
        grad = grads.at[n]

        def partial(t, j, core):
            return dot(rows_of(act, t * 576 + j * 288 + core * 144, 144)[...], grad[...])

        def sib_copy(t):
            return remote(wsib_out.at[n, t], wsib_in.at[n, t], ws_s.at[n, t], ws_r.at[n, t], sib)

        def target(k, way):
            return lax.rem(z + 8 - lengths[0] + k, 8) if way == 0 else lax.rem(z + 8 + lengths[1] - k, 8)

        def push(*targets):
            for t in targets:
                for j in range(2):
                    wsib_out[n, t, j] = partial(t, j, 1 - c).astype(BF)
                sib_copy(t).start()

        def push_for(k):
            push(*[target(k, way) for way in range(2) if k < lengths[way]])

        def hop(k, way, q):
            out, into = (wd_out, wd_in) if way == 0 else (wu_out, wu_in)
            ss, rr = (wd_s, wd_r) if way == 0 else (wu_s, wu_r)
            where = dn if way == 0 else up
            if k == lengths[way] - 1:
                where = there(where, q)
            return remote(out.at[n, k, q], into.at[n, k, q], ss.at[n, k, q], rr.at[n, k, q], where)

        def hop_step(k, way):
            out, into = (wd_out, wd_in) if way == 0 else (wu_out, wu_in)
            t = target(k, way)
            sib_copy(t).wait_recv()
            for q in (1, 0):
                total = partial(t, piece(q), c) + wsib_in[n, t, piece(q)].astype(F32)
                if k > 0:
                    hop(k - 1, way, q).wait_recv()
                    total += into[n, k - 1, q].astype(F32)
                out[n, k, q] = total.astype(BF)
                hop(k, way, q).start()

        def step(k):
            for way in range(2):
                if k < lengths[way]:
                    hop_step(k, way)

        def x_copy():
            return remote(wx_out.at[n], wx_in.at[n], wx_s.at[n], wx_r.at[n], xp)

        def cross():
            sib_copy(z).wait_recv()
            for q in (1, 0):
                wacc[n, q] = partial(z, piece(q), c) + wsib_in[n, z, piece(q)].astype(F32)
            wx_out[n] = wacc[n, 1].astype(BF)
            x_copy().start()

        def meet():
            x_copy().wait_recv()
            total = wacc[n, 0] + wx_in[n].astype(F32)
            for way, into in enumerate((wd_in, wu_in)):
                for q in range(2):
                    hop(lengths[way] - 1, way, q).wait_recv()
                    total += into[n, lengths[way] - 1, q].astype(F32)
            return total

        def drain():
            for t in range(8):
                sib_copy(t).wait_send()
            for way in range(2):
                for k in range(lengths[way]):
                    for q in range(2):
                        hop(k, way, q).wait_send()
            x_copy().wait_send()

        return push, push_for, step, cross, meet, drain

    push_q, push_q_for, step_q, cross_q, meet_q, drain_q = weight(0, anchor, (2, 5))
    push_kv, push_kv_for, step_kv, cross_kv, meet_kv, drain_kv = weight(1, projected, (4, 3))
    x_rows = remote(xout, xin, xg_s, xg_r, xp)
    sib_grad(0, 1).wait_recv()
    xout[...] = (mine[0, 1] + fromsib[0, 1].astype(F32)).astype(BF)
    x_rows.start()
    for h in range(2):
        grads[0, :, h * HD:(h + 1) * HD] = dq_t[:, h * TOK:(h + 1) * TOK].T.astype(BF)
    push_q_for(0)
    push_q_for(1)
    send_sum(1)
    step_q(0)
    for k in range(2, 5):
        push_q_for(k)
    push_q(z)
    step_q(1)
    sib_grad(0, 0).wait_recv()
    x_rows.wait_recv()
    mine[0, 0] += fromsib[0, 0].astype(F32) + xin[...].astype(F32)
    for k in (1, 0):
        for h, half in enumerate(halves):
            @pl.when(far_needs)
            def _():
                ring_in(4, k, h).wait_recv()
                mine[0, 0, half] += ringin[4, k, h].astype(F32)

            @pl.when(up_needs(0))
            def _():
                ring_in(0, k, h).wait_recv()
                mine[0, 0, half] += ringin[0, k, h].astype(F32)

    grads[1] = mine[0, 0].astype(BF)
    push_kv_for(0)
    step_kv(0)
    push_kv_for(1)
    push_kv_for(2)
    step_q(2)
    step_kv(1)
    push_kv_for(3)
    push_kv(z)
    step_q(3)
    step_kv(2)
    cross_kv()
    cross_q()
    step_kv(3)
    step_q(4)
    for half in range(2):
        pairs[pl.ds(half, TOK, stride=2), :] = grads[1, :, half * HD:(half + 1) * HD].astype(F32)
    rows_ref[...] = pairs[:2 * TOK, :].astype(BF)
    gq_ref[...] = meet_q()
    wacc[1, 0] = meet_kv()
    for half in range(2):
        gkv_ref[pl.ds(half, 144, stride=2), :] = wacc[1, 0, :, half * HD:(half + 1) * HD]

    for h in range(2):
        @pl.when(far_needs)
        def _():
            to_far(h).wait_send()

    x_rows.wait_send()
    drain_q()
    drain_kv()
    aug.drain()
    anc.drain()
    pros[0].drain()
    pros[1].drain()
    for k in range(5):
        step(k).wait_send()

    def drained(g, carry):
        @pl.when(needed(z - g, z))
        def _():
            for h in range(2):
                sib_grad(g, h).wait_send()
                to_xp(g, h).wait_send()
                for k in range(2):
                    to_sib(g, k, h).wait_send()

                @pl.when(up_needs(g))
                def _():
                    to_up(g, h).wait_send()

                @pl.when(g > 0)
                def _():
                    for k in range(2):
                        ring_out(g, k, h).wait_send()

        return carry

    lax.fori_loop(0, 6, drained, 0)


def step_call(aug_t, anc_t, pw_t, q_weight, kv_pairs, doc, d_out):
    dma = pltpu.SemaphoreType.DMA
    vmem = pl.BlockSpec(memory_space=pltpu.VMEM)
    hbm = pl.BlockSpec(memory_space=pl.ANY)
    two = lambda n: [dma(n), dma(n)]
    return pl.pallas_call(
        step_kernel,
        out_shape=[
            jax.ShapeDtypeStruct((TOK, 256), BF),
            jax.ShapeDtypeStruct((144, 256), F32),
            jax.ShapeDtypeStruct((288, HD), F32),
            jax.ShapeDtypeStruct((2 * TOK, HD), BF),
        ],
        in_specs=[vmem, vmem, hbm, hbm, hbm, vmem, vmem],
        out_specs=[vmem] * 4,
        scratch_shapes=[
            pltpu.VMEM((2304, TOK), BF), pltpu.VMEM((4608, TOK), BF), pltpu.VMEM((4608, TOK), BF),
            pltpu.VMEM((576, 2304), BF), pltpu.VMEM((4608, 256), BF), pltpu.VMEM((4608, 256), BF),
            pltpu.VMEM((9216, HD), BF), pltpu.VMEM((1152, HD), F32),
            pltpu.VMEM((TOK, 256), F32), pltpu.VMEM((TOK, 256), BF),
            pltpu.VMEM((6, 8, 128), jnp.int32), pltpu.VMEM((5, 8, 128), jnp.int32),
            pltpu.VMEM((32, TOK, 256), BF),
            pltpu.VMEM((512, HD), BF), pltpu.VMEM((HD, 512), BF),
            pltpu.VMEM((512, HD), BF), pltpu.VMEM((HD, 512), BF),
            pltpu.VMEM((HD, 512), F32), pltpu.VMEM((1, 512), F32),
            pltpu.VMEM((1, 512), jnp.int32), pltpu.VMEM((1, 512), jnp.int32),
            pltpu.VMEM((1, 512), F32), pltpu.VMEM((HD, 512), F32),
            pltpu.VMEM((6, 2, TOK, 256), F32), pltpu.VMEM((GROUP, 256), F32),
            pltpu.VMEM((6, 2, TOK, 256), BF), pltpu.VMEM((6, 2, TOK, 256), BF),
            pltpu.VMEM((5, 2, 2, HALF, 256), BF), pltpu.VMEM((5, 2, 2, HALF, 256), BF),
            pltpu.VMEM((TOK, 256), BF), pltpu.VMEM((TOK, 256), BF),
            pltpu.VMEM((2, TOK, 256), BF),
            pltpu.VMEM((2, 8, 2, 144, 256), BF), pltpu.VMEM((2, 8, 2, 144, 256), BF),
            pltpu.VMEM((2, 4, 2, 144, 256), BF), pltpu.VMEM((2, 4, 2, 144, 256), BF),
            pltpu.VMEM((2, 5, 2, 144, 256), BF), pltpu.VMEM((2, 5, 2, 144, 256), BF),
            pltpu.VMEM((2, 144, 256), BF), pltpu.VMEM((2, 144, 256), BF),
            pltpu.VMEM((2, 2, 144, 256), F32),
            dma((3,)), *two((13,)), *two((13,)), *two((2, 13)), *two((5,)),
            *two((5, 2)), *two((6, 2, 2)), *two((6, 2)), *two((6, 2)), *two((5, 2, 2)), *two(()),
            *two((2, 8)), *two((2, 4, 2)), *two((2, 5, 2)), *two((2,)),
        ],
        compiler_params=pltpu.CompilerParams(
            collective_id=1, has_side_effects=True, vmem_limit_bytes=60 * 1024 * 1024
        ),
    )(aug_t, anc_t, pw_t, q_weight, kv_pairs, doc, d_out)


def hand_over(*refs):
    n = len(refs) // 2
    for src, dst in zip(refs[:n], refs[n:]):
        dst[...] = src[...]


def body(anchor, augment, proj_weight, q_weight, kv_weight, doc_ids, d_out):
    results = step_call(
        augment.T, anchor.T, proj_weight.T, q_weight,
        kv_weight.reshape(-1, HD), doc_ids.reshape(1, -1), d_out,
    )
    attended, grad_q, grad_kv, rows = pl.pallas_call(
        hand_over,
        out_shape=[jax.ShapeDtypeStruct(r.shape, r.dtype) for r in results],
        in_specs=[pl.BlockSpec(memory_space=pltpu.VMEM)] * 4,
        out_specs=[pl.BlockSpec(memory_space=pltpu.VMEM)] * 4,
    )(*results)
    return attended, grad_q, grad_kv.reshape(144, 1, 2, HD), rows.reshape(TOK, 1, 2, HD)


def solution(mesh):
    placed = (
        P("seq", "mp"), P("seq", "mp"), P(None, "mp"), P(None, "mp"),
        P(None, "mp", None, None), P("seq"), P("seq", "mp"),
    )
    return jax.shard_map(
        body,
        mesh=mesh,
        in_specs=placed,
        out_specs=(
            P("seq", "mp"), P("seq", "mp"),
            P("seq", "mp", None, None), P("seq", "mp", None, None),
        ),
        check_vma=False,
    )
```

```python
import functools

import jax
import jax.numpy as jnp
from jax import lax
from jax.experimental import pallas as pl
from jax.experimental.pallas import tpu as pltpu
from jax.sharding import PartitionSpec as P

BF = jnp.bfloat16
F32 = jnp.float32
TOK = 256
HALF = 128
GROUP = 1024
HD = 128
MESH = pl.DeviceIdType.MESH
LOG2E = 1.4426950408889634
TN = (((0,), (0,)), ((), ()))


def remote(src, dst, send, recv, where):
    return pltpu.make_async_remote_copy(
        src_ref=src, dst_ref=dst, send_sem=send, recv_sem=recv, device_id=where, device_id_type=MESH
    )


def dot(a, b):
    return jnp.dot(a, b, preferred_element_type=F32)


def dot_tn(a, b):
    return lax.dot_general(a, b, TN, preferred_element_type=F32)


def rows_of(ref, start, size):
    return ref.at[pl.ds(pl.multiple_of(start, 16), size)]


def greet(partners):
    barrier = pltpu.get_barrier_semaphore()
    for where in partners:
        pl.semaphore_signal(barrier, inc=1, device_id=where, device_id_type=MESH)
    pl.semaphore_wait(barrier, len(partners))


class FeatureGather:
    def __init__(self, own, buf, rows, send, recv, m, lanes=pl.ds(0, TOK)):
        self.own, self.buf, self.rows, self.send, self.recv = own, buf, rows, send, recv
        self.lanes, self.m = lanes, m
        self.p = m + 1 - 2 * lax.rem(m, 2)
        self.up, self.dn = lax.rem(m + 2, 8), lax.rem(m + 6, 8)
        self.o = lax.rem(m + 4, 8)
        p = self.p
        self.p_up, self.p_dn, self.p_o = lax.rem(p + 2, 8), lax.rem(p + 6, 8), lax.rem(p + 4, 8)
        n = rows // 9
        whole, left, right = (0, 9 * n), (0, 5 * n), (5 * n, 4 * n)
        top, bottom = (0, rows // 2), (rows // 2, rows // 2)
        left0, left1 = (0, 5 * n // 2), (5 * n // 2, 5 * n // 2)
        m, p, up, dn = self.m, self.p, self.up, self.dn
        self.out = [
            (m, left, p), (m, whole, up), (m, whole, dn), (p, left, up), (p, left, dn),
            (dn, top, up), (up, bottom, dn), (self.p_dn, left0, up), (self.p_up, left1, dn),
            (m, right, p), (dn, right, p), (up, right, p), (self.o, right, p),
        ]
        self.into = [
            (p, left), (dn, whole), (up, whole), (self.p_dn, left), (self.p_up, left),
            (self.o, top), (self.o, bottom), (self.p_o, left0), (self.p_o, left1),
            (p, right), (self.p_dn, right), (self.p_up, right), (self.p_o, right),
        ]

    def part(self, block, rows):
        start = block * self.rows + rows[0]
        return self.buf.at[pl.ds(pl.multiple_of(start, 16), rows[1]), self.lanes]

    def sent(self, i):
        block, rows, to = self.out[i]
        dst = self.part(block, rows)
        src = self.own.at[pl.ds(*rows)] if i in (0, 1, 2, 9) else dst
        return remote(src, dst, self.send.at[i], self.recv.at[i], {"mp": to})

    def arrived(self, i):
        dst = self.part(*self.into[i])
        return remote(dst, dst, self.send.at[i], self.recv.at[i], {"mp": self.p})

    def start(self):
        for i in (0, 1, 2, 9):
            self.sent(i).start()

    def relay(self, stage):
        waits, sends = [
            ((0,), (3, 4)), ((1,), (5, 10)), ((2,), (6, 11)), ((3,), (7,)), ((4,), (8,)),
            ((6,), (12,)), ((5,), ()), ((9, 10, 11), ()), ((7, 8, 12), ()),
        ][stage]
        for i in waits:
            self.arrived(i).wait_recv()
        for i in sends:
            self.sent(i).start()

    def blocks(self, stage):
        return {
            1: [self.dn], 2: [self.up], 6: [self.o],
            7: [self.p, self.p_dn, self.p_up], 8: [self.p_o],
        }.get(stage, [])

    def drain(self):
        for i in range(13):
            self.sent(i).wait_send()


def needed(t, z):
    return (t >= 0) & (z <= 7) & ((t >= 2) | (z <= 5))


def step_kernel(
    aug_ref, anc_ref, pw_hbm, qw_hbm, kw_hbm, doc_ref, dout_ref,
    att_ref, gq_ref, gkv_ref, rows_ref,
    augment, anchor, projected, pw, qw, kw, kw_pairs, pairs, acc, kv_ref, cnt_out, cnt_in,
    kvs, q_n, q_t, do_n, do_t, num, den, first, place, delta, dq_t,
    mine, parts, tosib, fromsib, ringout, ringin, xout, xin, grads,
    wsib_out, wsib_in, wd_out, wd_in, wu_out, wu_in, wx_out, wx_in, wacc,
    wsem, asend, arecv, nsend, nrecv, psend, precv, csend, crecv,
    up_s, up_r, sb_s, sb_r, xp_s, xp_r, gs_s, gs_r, rg_s, rg_r, xg_s, xg_r,
    ws_s, ws_r, wd_s, wd_r, wu_s, wu_r, wx_s, wx_r,
):
    s, m = lax.axis_index("seq"), lax.axis_index("mp")
    z, xh, c = s // 4, lax.rem(s // 2, 2), lax.rem(s, 2)
    sib = {"seq": s + 1 - 2 * c}
    xp_id = s + 2 - 4 * xh
    xp = {"seq": xp_id}
    up, dn = {"seq": lax.rem(s + 4, 32)}, {"seq": lax.rem(s + 28, 32)}
    hyper = []
    for k in range(5):
        bit = lax.rem(s // (1 << k), 2)
        hyper.append(s + (1 << k) * (1 - 2 * bit))
    loads = [
        pltpu.make_async_copy(src, dst, wsem.at[i])
        for i, (src, dst) in enumerate([(pw_hbm, pw), (qw_hbm, qw), (kw_hbm, kw_pairs)])
    ]
    for load in loads:
        load.start()
    aug = FeatureGather(aug_ref, augment, 288, asend, arecv, m)
    anc = FeatureGather(anc_ref, anchor, 576, nsend, nrecv, m)
    own_projected = rows_of(projected, m * 576, 576)
    halves = [pl.ds(h * HALF, HALF) for h in range(2)]
    pros = [
        FeatureGather(own_projected.at[:, half], projected, 576, psend.at[h], precv.at[h], m, half)
        for h, half in enumerate(halves)
    ]
    far, near = {"seq": lax.rem(s + 20, 32)}, {"seq": lax.rem(s + 12, 32)}
    across = 2 - 4 * xh
    ring = [up, dn, far, near]
    greet(
        [{"mp": aug.p}, {"mp": aug.up}, {"mp": aug.dn}] + ring
        + [{"seq": one["seq"] + across} for one in ring] + [{"seq": h} for h in hyper]
    )

    aug.start()
    doc = doc_ref[...]
    zeros = jnp.sum((1 - doc).astype(F32), axis=1, keepdims=True)
    cnt_out[0] = jnp.broadcast_to(zeros, (8, 128)).astype(jnp.int32)

    def step(k):
        return remote(cnt_out.at[k], cnt_in.at[k], csend.at[k], crecv.at[k], {"seq": hyper[k]})

    def count(k):
        step(k).wait_recv()
        cnt_out[k + 1] = cnt_out[k] + cnt_in[k]
        if k < 4:
            step(k + 1).start()

    step(0).start()
    rows_of(augment, m * 288, 288)[...] = aug_ref[...]
    rows_of(anchor, m * 576, 576)[...] = anc_ref[...]
    loads[2].wait()

    def unpair(i, carry):
        pairs[...] = kw_pairs[pl.ds(pl.multiple_of(i * 1152, 1152), 1152), :].astype(F32)
        for half in range(2):
            out = pairs[pl.ds(half, 576, stride=2), :].astype(BF)
            kw[pl.ds(pl.multiple_of(i * 576, 576), 576), half * HD:(half + 1) * HD] = out
        return carry

    lax.fori_loop(0, 2, unpair, 0)
    lanes = lax.broadcasted_iota(jnp.int32, (1, 2 * TOK), 1)
    place[...] = lax.rem(lanes, TOK) + s * TOK
    for h in range(2):
        cut = slice(h * TOK, (h + 1) * TOK)
        head = slice(h * HD, (h + 1) * HD)
        do_n[cut, :] = dout_ref[:, head]
        do_t[:, cut] = dout_ref[:, head].T
    loads[0].wait()
    loads[1].wait()
    for stage in range(9):
        aug.relay(stage)
        if stage == 4:
            anc.start()
            lax.fori_loop(2, 6, unpair, 0)
    own_projected[...] = dot(pw[...], augment[...]).astype(BF)
    pros[0].start()
    count(0)
    for stage in range(3):
        anc.relay(stage)
    lax.fori_loop(6, 8, unpair, 0)

    def add(block):
        acc[...] += dot_tn(rows_of(anchor, block * 576, 576)[...], rows_of(qw, block * 576, 576)[...])

    def add_kv(h, block):
        piece = projected[pl.ds(pl.multiple_of(block * 576, 16), 576), halves[h]]
        acc[halves[h]] += dot_tn(piece, rows_of(kw, block * 576, 576)[...])

    def half_copy(src, block, h, send, recv, where):
        dst = kvs.at[block, halves[h]]
        return remote(dst if src is None else src.at[halves[h]], dst, send, recv, where)

    def lane(t, j):
        return 4 * t + 2 * j + c

    def piece(k):
        return lax.rem(xh + k, 2)

    def to_up(g, h, src=None):
        return half_copy(src, lane(z - g, xh), h, up_s.at[g, h], up_r.at[g, h], up)

    def to_far(h, src=None):
        return half_copy(src, lane(z, xh), h, up_s.at[4, h], up_r.at[4, h], far)

    def to_xp(g, h, src=None):
        return half_copy(src, lane(z - g, xh), h, xp_s.at[g, h], xp_r.at[g, h], xp)

    def to_sib(g, k, h, src=None):
        return half_copy(src, lane(z - g, piece(k)), h, sb_s.at[g, k, h], sb_r.at[g, k, h], sib)

    def from_sib(g, k, h):
        b = 4 * (z - g) + 2 * piece(k) + 1 - c
        return half_copy(None, b, h, sb_s.at[g, k, h], sb_r.at[g, k, h], sib)

    def from_dn(g, h):
        return half_copy(None, lane(z - g, xh), h, up_s.at[g - 1, h], up_r.at[g - 1, h], dn)

    def from_xp(g, h):
        return half_copy(None, lane(z - g, 1 - xh), h, xp_s.at[g, h], xp_r.at[g, h], xp)

    def up_needs(g):
        return (g < 4) & needed(z - g, z + 1)

    far_needs = needed(z, z + 5)

    def launch(h):
        kv_ref[halves[h]] = acc[halves[h]].astype(BF)

        @pl.when(up_needs(0))
        def _():
            to_up(0, h, kv_ref).start()

        to_xp(0, h, kv_ref).start()
        to_sib(0, 0, h, kv_ref).start()

        @pl.when(far_needs)
        def _():
            to_far(h, kv_ref).start()

        kvs[s, halves[h]] = kv_ref[halves[h]]

    def pass_on(g, h):
        @pl.when(needed(z - g, z))
        def _():
            from_dn(g, h).wait_recv()

            @pl.when(up_needs(g))
            def _():
                to_up(g, h).start()

            to_xp(g, h).start()
            to_sib(g, 0, h).start()

    def crossed(g, h):
        @pl.when(needed(z - g, z))
        def _():
            from_xp(g, h).wait_recv()
            to_sib(g, 1, h).start()

    acc[...] = jnp.zeros_like(acc)
    def gather(h, *stages):
        for stage in stages:
            pros[h].relay(stage)
            for block in pros[h].blocks(stage):
                add_kv(h, block)

    add_kv(0, m)
    gather(0, 0, 1, 2, 3, 4)
    pros[1].start()
    count(1)
    add_kv(1, m)
    gather(0, 5, 6, 7)
    pros[1].relay(0)
    gather(0, 8)
    launch(0)
    count(2)
    for stage in range(3, 6):
        anc.relay(stage)
    gather(1, 1, 2, 3, 4)
    pass_on(1, 0)
    count(3)
    gather(1, 5, 6)
    pass_on(2, 0)
    gather(1, 7, 8)
    launch(1)
    pass_on(3, 0)
    count(4)
    for h in range(2):
        first[:, h * TOK:(h + 1) * TOK] = doc * cnt_out[5, 0:1, 0:1]
    num[...] = jnp.zeros_like(num)
    den[...] = jnp.zeros_like(den)
    dq_t[...] = jnp.zeros_like(dq_t)
    crossed(0, 0)

    def scores(g):
        base = 4 * (z - g)
        kv = kvs[pl.ds(base, 4)].reshape(GROUP, 256)
        k, v = kv[:, :HD], kv[:, HD:]
        th = jnp.tanh(dot(k, q_t[...]) * (1.0 / 600.0))
        pos = lax.broadcasted_iota(jnp.int32, (GROUP, 2 * TOK), 0)
        allowed = (pos >= first[...] - base * TOK) & (pos <= place[...] - base * TOK)
        return k, v, th, jnp.where(allowed, jnp.exp2(th * (50.0 * LOG2E)), 0.0)

    def forward(g):
        _, v, _, w = scores(g)
        den[...] += jnp.sum(w, axis=0, keepdims=True)
        num[...] += dot_tn(v, w.astype(BF))

    acc[...] = jnp.zeros_like(acc)
    for block in (m, anc.dn, anc.up):
        add(block)
    for stage in range(6, 9):
        anc.relay(stage)
        for block in anc.blocks(stage):
            add(block)
    pass_on(1, 1)
    pass_on(4, 0)
    crossed(1, 0)
    crossed(0, 1)

    query = acc[...].astype(BF)
    for h in range(2):
        cut = slice(h * TOK, (h + 1) * TOK)
        head = slice(h * HD, (h + 1) * HD)
        q_n[cut, :] = query[:, head]
        q_t[:, cut] = query[:, head].T

    def forward_step(g):
        @pl.when(needed(z - g, z))
        def _():
            for h in range(2):
                for k in range(2):
                    from_sib(g, k, h).wait_recv()
            forward(g)

    pass_on(2, 1)
    crossed(1, 1)
    forward_step(0)
    pass_on(3, 1)
    crossed(2, 0)
    crossed(2, 1)
    forward_step(1)
    pass_on(4, 1)
    crossed(3, 0)
    crossed(3, 1)
    pass_on(5, 0)
    pass_on(5, 1)
    forward_step(2)
    for g in (4, 5):
        for h in range(2):
            crossed(g, h)
    forward_step(3)
    forward_step(5)
    forward_step(4)

    attended = (num[...] * (1.0 / den[...])).astype(BF)
    delta[...] = jnp.sum(do_t[...].astype(F32) * attended.astype(F32), axis=0, keepdims=True)
    den[...] = 1.0 / den[...]
    for h in range(2):
        att_ref[:, h * HD:(h + 1) * HD] = attended[:, h * TOK:(h + 1) * TOK].T

    def there(where, k):
        return {"seq": where["seq"] + k * across}

    def ring_out(g, k, h, last=False):
        where = there(near if g == 5 else dn, k) if last else dn
        return remote(
            ringout.at[g - 1, k, h], ringin.at[g - 1, k, h], rg_s.at[g - 1, k, h], rg_r.at[g - 1, k, h], where
        )

    def ring_in(g, k, h):
        return remote(ringout.at[g, k, h], ringin.at[g, k, h], rg_s.at[g, k, h], rg_r.at[g, k, h], up)

    def sib_grad(g, k):
        return remote(tosib.at[g, k], fromsib.at[g, k], gs_s.at[g, k], gs_r.at[g, k], sib)

    def contribute(g):
        @pl.when(needed(z - g, z))
        def _():
            k, v, th, w = scores(g)
            prob = w * den[...]
            soft = prob * (dot(v, do_t[...]) - delta[...])
            raw = (soft * ((1.0 - th * th) * (1.0 / 12.0))).astype(BF)
            parts[:, :HD] = dot(raw, q_n[...])
            parts[:, HD:] = dot(prob.astype(BF), do_n[...])
            for q in (1, 0):
                start = (2 * piece(q) + 1 - c) * TOK
                tosib[g, q] = parts[pl.ds(pl.multiple_of(start, TOK), TOK), :].astype(BF)
                sib_grad(g, q).start()
            for q in (1, 0):
                start = (2 * piece(q) + c) * TOK
                mine[g, q] = parts[pl.ds(pl.multiple_of(start, TOK), TOK), :]
            dq_t[...] += dot_tn(k, raw)

    def send_sum(g):
        @pl.when(needed(z - g, z))
        def _():
            for k in (1, 0):
                sib_grad(g, k).wait_recv()
                for h, half in enumerate(halves):
                    mine[g, k, half] += fromsib[g, k, half].astype(F32)

                    @pl.when(up_needs(g))
                    def _():
                        ring_in(g, k, h).wait_recv()
                        mine[g, k, half] += ringin[g, k, h].astype(F32)

                    ringout[g - 1, k, h] = mine[g, k, half].astype(BF)
                    ring_out(g, k, h, g in (1, 5)).start()

    contribute(4)
    send_sum(4)
    contribute(3)
    contribute(2)
    send_sum(3)
    contribute(1)
    contribute(5)
    send_sum(5)
    send_sum(2)
    contribute(0)

    def weight(n, act, lengths):
        grad = grads.at[n]

        def partial(t, j, core):
            return dot(rows_of(act, t * 576 + j * 288 + core * 144, 144)[...], grad[...])

        def sib_copy(t):
            return remote(wsib_out.at[n, t], wsib_in.at[n, t], ws_s.at[n, t], ws_r.at[n, t], sib)

        def target(k, way):
            return lax.rem(z + 8 - lengths[0] + k, 8) if way == 0 else lax.rem(z + 8 + lengths[1] - k, 8)

        def push(*targets):
            for t in targets:
                for j in range(2):
                    wsib_out[n, t, j] = partial(t, j, 1 - c).astype(BF)
                sib_copy(t).start()

        def push_for(k):
            push(*[target(k, way) for way in range(2) if k < lengths[way]])

        def hop(k, way, q):
            out, into = (wd_out, wd_in) if way == 0 else (wu_out, wu_in)
            ss, rr = (wd_s, wd_r) if way == 0 else (wu_s, wu_r)
            where = dn if way == 0 else up
            if k == lengths[way] - 1:
                where = there(where, q)
            return remote(out.at[n, k, q], into.at[n, k, q], ss.at[n, k, q], rr.at[n, k, q], where)

        def hop_step(k, way):
            out, into = (wd_out, wd_in) if way == 0 else (wu_out, wu_in)
            t = target(k, way)
            sib_copy(t).wait_recv()
            for q in (1, 0):
                total = partial(t, piece(q), c) + wsib_in[n, t, piece(q)].astype(F32)
                if k > 0:
                    hop(k - 1, way, q).wait_recv()
                    total += into[n, k - 1, q].astype(F32)
                out[n, k, q] = total.astype(BF)
                hop(k, way, q).start()

        def step(k):
            for way in range(2):
                if k < lengths[way]:
                    hop_step(k, way)

        def x_copy():
            return remote(wx_out.at[n], wx_in.at[n], wx_s.at[n], wx_r.at[n], xp)

        def cross():
            sib_copy(z).wait_recv()
            for q in (1, 0):
                wacc[n, q] = partial(z, piece(q), c) + wsib_in[n, z, piece(q)].astype(F32)
            wx_out[n] = wacc[n, 1].astype(BF)
            x_copy().start()

        def meet():
            x_copy().wait_recv()
            total = wacc[n, 0] + wx_in[n].astype(F32)
            for way, into in enumerate((wd_in, wu_in)):
                for q in range(2):
                    hop(lengths[way] - 1, way, q).wait_recv()
                    total += into[n, lengths[way] - 1, q].astype(F32)
            return total

        def drain():
            for t in range(8):
                sib_copy(t).wait_send()
            for way in range(2):
                for k in range(lengths[way]):
                    for q in range(2):
                        hop(k, way, q).wait_send()
            x_copy().wait_send()

        return push, push_for, step, cross, meet, drain

    push_q, push_q_for, step_q, cross_q, meet_q, drain_q = weight(0, anchor, (3, 4))
    push_kv, push_kv_for, step_kv, cross_kv, meet_kv, drain_kv = weight(1, projected, (4, 3))
    x_rows = remote(xout, xin, xg_s, xg_r, xp)
    sib_grad(0, 1).wait_recv()
    xout[...] = (mine[0, 1] + fromsib[0, 1].astype(F32)).astype(BF)
    x_rows.start()
    for h in range(2):
        grads[0, :, h * HD:(h + 1) * HD] = dq_t[:, h * TOK:(h + 1) * TOK].T.astype(BF)
    push_q_for(0)
    push_q_for(1)
    send_sum(1)
    step_q(0)
    push_q_for(2)
    push_q_for(3)
    push_q(z)
    step_q(1)
    step_q(2)
    sib_grad(0, 0).wait_recv()
    x_rows.wait_recv()
    mine[0, 0] += fromsib[0, 0].astype(F32) + xin[...].astype(F32)
    for k in (1, 0):
        for h, half in enumerate(halves):
            @pl.when(far_needs)
            def _():
                ring_in(4, k, h).wait_recv()
                mine[0, 0, half] += ringin[4, k, h].astype(F32)

            @pl.when(up_needs(0))
            def _():
                ring_in(0, k, h).wait_recv()
                mine[0, 0, half] += ringin[0, k, h].astype(F32)

    grads[1] = mine[0, 0].astype(BF)
    push_kv_for(0)
    step_kv(0)
    push_kv_for(1)
    push_kv_for(2)
    step_kv(1)
    push_kv_for(3)
    push_kv(z)
    step_q(3)
    step_kv(2)
    cross_kv()
    cross_q()
    step_kv(3)
    for half in range(2):
        pairs[pl.ds(half, TOK, stride=2), :] = grads[1, :, half * HD:(half + 1) * HD].astype(F32)
    rows_ref[...] = pairs[:2 * TOK, :].astype(BF)
    gq_ref[...] = meet_q()
    wacc[1, 0] = meet_kv()
    for half in range(2):
        gkv_ref[pl.ds(half, 144, stride=2), :] = wacc[1, 0, :, half * HD:(half + 1) * HD]

    for h in range(2):
        @pl.when(far_needs)
        def _():
            to_far(h).wait_send()

    x_rows.wait_send()
    drain_q()
    drain_kv()
    aug.drain()
    anc.drain()
    pros[0].drain()
    pros[1].drain()
    for k in range(5):
        step(k).wait_send()

    def drained(g, carry):
        @pl.when(needed(z - g, z))
        def _():
            for h in range(2):
                sib_grad(g, h).wait_send()
                to_xp(g, h).wait_send()
                for k in range(2):
                    to_sib(g, k, h).wait_send()

                @pl.when(up_needs(g))
                def _():
                    to_up(g, h).wait_send()

                @pl.when(g > 0)
                def _():
                    for k in range(2):
                        ring_out(g, k, h).wait_send()

        return carry

    lax.fori_loop(0, 6, drained, 0)


def step_call(aug_t, anc_t, pw_t, q_weight, kv_pairs, doc, d_out):
    dma = pltpu.SemaphoreType.DMA
    vmem = pl.BlockSpec(memory_space=pltpu.VMEM)
    hbm = pl.BlockSpec(memory_space=pl.ANY)
    two = lambda n: [dma(n), dma(n)]
    return pl.pallas_call(
        step_kernel,
        out_shape=[
            jax.ShapeDtypeStruct((TOK, 256), BF),
            jax.ShapeDtypeStruct((144, 256), F32),
            jax.ShapeDtypeStruct((288, HD), F32),
            jax.ShapeDtypeStruct((2 * TOK, HD), BF),
        ],
        in_specs=[vmem, vmem, hbm, hbm, hbm, vmem, vmem],
        out_specs=[vmem] * 4,
        scratch_shapes=[
            pltpu.VMEM((2304, TOK), BF), pltpu.VMEM((4608, TOK), BF), pltpu.VMEM((4608, TOK), BF),
            pltpu.VMEM((576, 2304), BF), pltpu.VMEM((4608, 256), BF), pltpu.VMEM((4608, 256), BF),
            pltpu.VMEM((9216, HD), BF), pltpu.VMEM((1152, HD), F32),
            pltpu.VMEM((TOK, 256), F32), pltpu.VMEM((TOK, 256), BF),
            pltpu.VMEM((6, 8, 128), jnp.int32), pltpu.VMEM((5, 8, 128), jnp.int32),
            pltpu.VMEM((32, TOK, 256), BF),
            pltpu.VMEM((512, HD), BF), pltpu.VMEM((HD, 512), BF),
            pltpu.VMEM((512, HD), BF), pltpu.VMEM((HD, 512), BF),
            pltpu.VMEM((HD, 512), F32), pltpu.VMEM((1, 512), F32),
            pltpu.VMEM((1, 512), jnp.int32), pltpu.VMEM((1, 512), jnp.int32),
            pltpu.VMEM((1, 512), F32), pltpu.VMEM((HD, 512), F32),
            pltpu.VMEM((6, 2, TOK, 256), F32), pltpu.VMEM((GROUP, 256), F32),
            pltpu.VMEM((6, 2, TOK, 256), BF), pltpu.VMEM((6, 2, TOK, 256), BF),
            pltpu.VMEM((5, 2, 2, HALF, 256), BF), pltpu.VMEM((5, 2, 2, HALF, 256), BF),
            pltpu.VMEM((TOK, 256), BF), pltpu.VMEM((TOK, 256), BF),
            pltpu.VMEM((2, TOK, 256), BF),
            pltpu.VMEM((2, 8, 2, 144, 256), BF), pltpu.VMEM((2, 8, 2, 144, 256), BF),
            pltpu.VMEM((2, 4, 2, 144, 256), BF), pltpu.VMEM((2, 4, 2, 144, 256), BF),
            pltpu.VMEM((2, 5, 2, 144, 256), BF), pltpu.VMEM((2, 5, 2, 144, 256), BF),
            pltpu.VMEM((2, 144, 256), BF), pltpu.VMEM((2, 144, 256), BF),
            pltpu.VMEM((2, 2, 144, 256), F32),
            dma((3,)), *two((13,)), *two((13,)), *two((2, 13)), *two((5,)),
            *two((5, 2)), *two((6, 2, 2)), *two((6, 2)), *two((6, 2)), *two((5, 2, 2)), *two(()),
            *two((2, 8)), *two((2, 4, 2)), *two((2, 5, 2)), *two((2,)),
        ],
        compiler_params=pltpu.CompilerParams(
            collective_id=1, has_side_effects=True, vmem_limit_bytes=60 * 1024 * 1024
        ),
    )(aug_t, anc_t, pw_t, q_weight, kv_pairs, doc, d_out)


def hand_over(*refs):
    n = len(refs) // 2
    for src, dst in zip(refs[:n], refs[n:]):
        dst[...] = src[...]


def body(anchor, augment, proj_weight, q_weight, kv_weight, doc_ids, d_out):
    results = step_call(
        augment.T, anchor.T, proj_weight.T, q_weight,
        kv_weight.reshape(-1, HD), doc_ids.reshape(1, -1), d_out,
    )
    attended, grad_q, grad_kv, rows = pl.pallas_call(
        hand_over,
        out_shape=[jax.ShapeDtypeStruct(r.shape, r.dtype) for r in results],
        in_specs=[pl.BlockSpec(memory_space=pltpu.VMEM)] * 4,
        out_specs=[pl.BlockSpec(memory_space=pltpu.VMEM)] * 4,
    )(*results)
    return attended, grad_q, grad_kv.reshape(144, 1, 2, HD), rows.reshape(TOK, 1, 2, HD)


def solution(mesh):
    placed = (
        P("seq", "mp"), P("seq", "mp"), P(None, "mp"), P(None, "mp"),
        P(None, "mp", None, None), P("seq"), P("seq", "mp"),
    )
    return jax.shard_map(
        body,
        mesh=mesh,
        in_specs=placed,
        out_specs=(
            P("seq", "mp"), P("seq", "mp"),
            P("seq", "mp", None, None), P("seq", "mp", None, None),
        ),
        check_vma=False,
    )
```

```python
import functools

import jax
import jax.numpy as jnp
from jax import lax
from jax.experimental import pallas as pl
from jax.experimental.pallas import tpu as pltpu
from jax.sharding import PartitionSpec as P

BF = jnp.bfloat16
F32 = jnp.float32
TOK = 256
HALF = 128
GROUP = 1024
HD = 128
MESH = pl.DeviceIdType.MESH
LOG2E = 1.4426950408889634
TN = (((0,), (0,)), ((), ()))


def remote(src, dst, send, recv, where):
    return pltpu.make_async_remote_copy(
        src_ref=src, dst_ref=dst, send_sem=send, recv_sem=recv, device_id=where, device_id_type=MESH
    )


def dot(a, b):
    return jnp.dot(a, b, preferred_element_type=F32)


def dot_tn(a, b):
    return lax.dot_general(a, b, TN, preferred_element_type=F32)


def rows_of(ref, start, size):
    return ref.at[pl.ds(pl.multiple_of(start, 16), size)]


def greet(partners):
    barrier = pltpu.get_barrier_semaphore()
    for where in partners:
        pl.semaphore_signal(barrier, inc=1, device_id=where, device_id_type=MESH)
    pl.semaphore_wait(barrier, len(partners))


class FeatureGather:
    def __init__(self, own, buf, rows, send, recv, m, lanes=pl.ds(0, TOK)):
        self.own, self.buf, self.rows, self.send, self.recv = own, buf, rows, send, recv
        self.lanes, self.m = lanes, m
        self.p = m + 1 - 2 * lax.rem(m, 2)
        self.up, self.dn = lax.rem(m + 2, 8), lax.rem(m + 6, 8)
        self.o = lax.rem(m + 4, 8)
        p = self.p
        self.p_up, self.p_dn, self.p_o = lax.rem(p + 2, 8), lax.rem(p + 6, 8), lax.rem(p + 4, 8)
        n = rows // 9
        whole, left, right = (0, 9 * n), (0, 5 * n), (5 * n, 4 * n)
        top, bottom = (0, rows // 2), (rows // 2, rows // 2)
        left0, left1 = (0, 5 * n // 2), (5 * n // 2, 5 * n // 2)
        m, p, up, dn = self.m, self.p, self.up, self.dn
        self.out = [
            (m, left, p), (m, whole, up), (m, whole, dn), (p, left, up), (p, left, dn),
            (dn, top, up), (up, bottom, dn), (self.p_dn, left0, up), (self.p_up, left1, dn),
            (m, right, p), (dn, right, p), (up, right, p), (self.o, right, p),
        ]
        self.into = [
            (p, left), (dn, whole), (up, whole), (self.p_dn, left), (self.p_up, left),
            (self.o, top), (self.o, bottom), (self.p_o, left0), (self.p_o, left1),
            (p, right), (self.p_dn, right), (self.p_up, right), (self.p_o, right),
        ]

    def part(self, block, rows):
        start = block * self.rows + rows[0]
        return self.buf.at[pl.ds(pl.multiple_of(start, 16), rows[1]), self.lanes]

    def sent(self, i):
        block, rows, to = self.out[i]
        dst = self.part(block, rows)
        src = self.own.at[pl.ds(*rows)] if i in (0, 1, 2, 9) else dst
        return remote(src, dst, self.send.at[i], self.recv.at[i], {"mp": to})

    def arrived(self, i):
        dst = self.part(*self.into[i])
        return remote(dst, dst, self.send.at[i], self.recv.at[i], {"mp": self.p})

    def start(self):
        for i in (0, 1, 2, 9):
            self.sent(i).start()

    def relay(self, stage):
        waits, sends = [
            ((0,), (3, 4)), ((1,), (5, 10)), ((2,), (6, 11)), ((3,), (7,)), ((4,), (8,)),
            ((6,), (12,)), ((5,), ()), ((9, 10, 11), ()), ((7, 8, 12), ()),
        ][stage]
        for i in waits:
            self.arrived(i).wait_recv()
        for i in sends:
            self.sent(i).start()

    def blocks(self, stage):
        return {
            1: [self.dn], 2: [self.up], 6: [self.o],
            7: [self.p, self.p_dn, self.p_up], 8: [self.p_o],
        }.get(stage, [])

    def drain(self):
        for i in range(13):
            self.sent(i).wait_send()


def needed(t, z):
    return (t >= 0) & (z <= 7) & ((t >= 2) | (z <= 5))


def step_kernel(
    aug_ref, anc_ref, pw_hbm, qw_hbm, kw_hbm, doc_ref, dout_ref,
    att_ref, gq_ref, gkv_ref, rows_ref,
    augment, anchor, projected, pw, qw, kw, kw_pairs, pairs, acc, kv_ref, cnt_out, cnt_in,
    kvs, q_n, q_t, do_n, do_t, num, den, first, place, delta, dq_t,
    mine, parts, tosib, fromsib, ringout, ringin, xout, xin, grads,
    wsib_out, wsib_in, wd_out, wd_in, wu_out, wu_in, wx_out, wx_in, wacc,
    wsem, asend, arecv, nsend, nrecv, psend, precv, csend, crecv,
    up_s, up_r, sb_s, sb_r, xp_s, xp_r, gs_s, gs_r, rg_s, rg_r, xg_s, xg_r,
    ws_s, ws_r, wd_s, wd_r, wu_s, wu_r, wx_s, wx_r,
):
    s, m = lax.axis_index("seq"), lax.axis_index("mp")
    z, xh, c = s // 4, lax.rem(s // 2, 2), lax.rem(s, 2)
    sib = {"seq": s + 1 - 2 * c}
    xp_id = s + 2 - 4 * xh
    xp = {"seq": xp_id}
    up, dn = {"seq": lax.rem(s + 4, 32)}, {"seq": lax.rem(s + 28, 32)}
    hyper = []
    for k in range(5):
        bit = lax.rem(s // (1 << k), 2)
        hyper.append(s + (1 << k) * (1 - 2 * bit))
    loads = [
        pltpu.make_async_copy(src, dst, wsem.at[i])
        for i, (src, dst) in enumerate([(pw_hbm, pw), (qw_hbm, qw), (kw_hbm, kw_pairs)])
    ]
    for load in loads:
        load.start()
    aug = FeatureGather(aug_ref, augment, 288, asend, arecv, m)
    anc = FeatureGather(anc_ref, anchor, 576, nsend, nrecv, m)
    own_projected = rows_of(projected, m * 576, 576)
    halves = [pl.ds(h * HALF, HALF) for h in range(2)]
    pros = [
        FeatureGather(own_projected.at[:, half], projected, 576, psend.at[h], precv.at[h], m, half)
        for h, half in enumerate(halves)
    ]
    far, near = {"seq": lax.rem(s + 20, 32)}, {"seq": lax.rem(s + 12, 32)}
    across = 2 - 4 * xh
    ring = [up, dn, far, near]
    greet(
        [{"mp": aug.p}, {"mp": aug.up}, {"mp": aug.dn}] + ring
        + [{"seq": one["seq"] + across} for one in ring] + [{"seq": h} for h in hyper]
    )

    aug.start()
    doc = doc_ref[...]
    zeros = jnp.sum((1 - doc).astype(F32), axis=1, keepdims=True)
    cnt_out[0] = jnp.broadcast_to(zeros, (8, 128)).astype(jnp.int32)

    def step(k):
        return remote(cnt_out.at[k], cnt_in.at[k], csend.at[k], crecv.at[k], {"seq": hyper[k]})

    def count(k):
        step(k).wait_recv()
        cnt_out[k + 1] = cnt_out[k] + cnt_in[k]
        if k < 4:
            step(k + 1).start()

    step(0).start()
    rows_of(augment, m * 288, 288)[...] = aug_ref[...]
    rows_of(anchor, m * 576, 576)[...] = anc_ref[...]
    loads[2].wait()

    def unpair(i, carry):
        pairs[...] = kw_pairs[pl.ds(pl.multiple_of(i * 1152, 1152), 1152), :].astype(F32)
        for half in range(2):
            out = pairs[pl.ds(half, 576, stride=2), :].astype(BF)
            kw[pl.ds(pl.multiple_of(i * 576, 576), 576), half * HD:(half + 1) * HD] = out
        return carry

    lax.fori_loop(0, 2, unpair, 0)
    lanes = lax.broadcasted_iota(jnp.int32, (1, 2 * TOK), 1)
    place[...] = lax.rem(lanes, TOK) + s * TOK
    for h in range(2):
        cut = slice(h * TOK, (h + 1) * TOK)
        head = slice(h * HD, (h + 1) * HD)
        do_n[cut, :] = dout_ref[:, head]
        do_t[:, cut] = dout_ref[:, head].T
    loads[0].wait()
    loads[1].wait()
    for stage in range(9):
        aug.relay(stage)
        if stage == 4:
            anc.start()
            lax.fori_loop(2, 6, unpair, 0)
    own_projected[...] = dot(pw[...], augment[...]).astype(BF)
    pros[0].start()
    count(0)
    lax.fori_loop(6, 8, unpair, 0)

    def add(block):
        acc[...] += dot_tn(rows_of(anchor, block * 576, 576)[...], rows_of(qw, block * 576, 576)[...])

    def add_kv(h, block):
        piece = projected[pl.ds(pl.multiple_of(block * 576, 16), 576), halves[h]]
        acc[halves[h]] += dot_tn(piece, rows_of(kw, block * 576, 576)[...])

    def half_copy(src, block, h, send, recv, where):
        dst = kvs.at[block, halves[h]]
        return remote(dst if src is None else src.at[halves[h]], dst, send, recv, where)

    def lane(t, j):
        return 4 * t + 2 * j + c

    def piece(k):
        return lax.rem(xh + k, 2)

    def to_up(g, h, src=None):
        return half_copy(src, lane(z - g, xh), h, up_s.at[g, h], up_r.at[g, h], up)

    def to_far(h, src=None):
        return half_copy(src, lane(z, xh), h, up_s.at[4, h], up_r.at[4, h], far)

    def to_xp(g, h, src=None):
        return half_copy(src, lane(z - g, xh), h, xp_s.at[g, h], xp_r.at[g, h], xp)

    def to_sib(g, k, h, src=None):
        return half_copy(src, lane(z - g, piece(k)), h, sb_s.at[g, k, h], sb_r.at[g, k, h], sib)

    def from_sib(g, k, h):
        b = 4 * (z - g) + 2 * piece(k) + 1 - c
        return half_copy(None, b, h, sb_s.at[g, k, h], sb_r.at[g, k, h], sib)

    def from_dn(g, h):
        return half_copy(None, lane(z - g, xh), h, up_s.at[g - 1, h], up_r.at[g - 1, h], dn)

    def from_xp(g, h):
        return half_copy(None, lane(z - g, 1 - xh), h, xp_s.at[g, h], xp_r.at[g, h], xp)

    def up_needs(g):
        return (g < 4) & needed(z - g, z + 1)

    far_needs = needed(z, z + 5)

    def launch(h):
        kv_ref[halves[h]] = acc[halves[h]].astype(BF)

        @pl.when(up_needs(0))
        def _():
            to_up(0, h, kv_ref).start()

        to_xp(0, h, kv_ref).start()
        to_sib(0, 0, h, kv_ref).start()

        @pl.when(far_needs)
        def _():
            to_far(h, kv_ref).start()

        kvs[s, halves[h]] = kv_ref[halves[h]]

    def pass_on(g, h):
        @pl.when(needed(z - g, z))
        def _():
            from_dn(g, h).wait_recv()

            @pl.when(up_needs(g))
            def _():
                to_up(g, h).start()

            to_xp(g, h).start()
            to_sib(g, 0, h).start()

    def crossed(g, h):
        @pl.when(needed(z - g, z))
        def _():
            from_xp(g, h).wait_recv()
            to_sib(g, 1, h).start()

    acc[...] = jnp.zeros_like(acc)
    def gather(h, *stages):
        for stage in stages:
            pros[h].relay(stage)
            for block in pros[h].blocks(stage):
                add_kv(h, block)

    add_kv(0, m)
    gather(0, 0, 1, 2, 3, 4)
    pros[1].start()
    for stage in range(3):
        anc.relay(stage)
    count(1)
    add_kv(1, m)
    gather(0, 5, 6, 7)
    pros[1].relay(0)
    gather(0, 8)
    launch(0)
    count(2)
    gather(1, 1, 2, 3, 4)
    pass_on(1, 0)
    for stage in range(3, 6):
        anc.relay(stage)
    count(3)
    gather(1, 5, 6)
    pass_on(2, 0)
    gather(1, 7, 8)
    launch(1)
    pass_on(3, 0)
    count(4)
    for h in range(2):
        first[:, h * TOK:(h + 1) * TOK] = doc * cnt_out[5, 0:1, 0:1]
    num[...] = jnp.zeros_like(num)
    den[...] = jnp.zeros_like(den)
    dq_t[...] = jnp.zeros_like(dq_t)
    crossed(0, 0)

    def scores(g):
        base = 4 * (z - g)
        kv = kvs[pl.ds(base, 4)].reshape(GROUP, 256)
        k, v = kv[:, :HD], kv[:, HD:]
        th = jnp.tanh(dot(k, q_t[...]) * (1.0 / 600.0))
        pos = lax.broadcasted_iota(jnp.int32, (GROUP, 2 * TOK), 0)
        allowed = (pos >= first[...] - base * TOK) & (pos <= place[...] - base * TOK)
        return k, v, th, jnp.where(allowed, jnp.exp2(th * (50.0 * LOG2E)), 0.0)

    def forward(g):
        _, v, _, w = scores(g)
        den[...] += jnp.sum(w, axis=0, keepdims=True)
        num[...] += dot_tn(v, w.astype(BF))

    acc[...] = jnp.zeros_like(acc)
    for block in (m, anc.dn, anc.up):
        add(block)
    for stage in range(6, 9):
        anc.relay(stage)
        for block in anc.blocks(stage):
            add(block)
    pass_on(1, 1)
    pass_on(4, 0)
    crossed(1, 0)
    crossed(0, 1)

    query = acc[...].astype(BF)
    for h in range(2):
        cut = slice(h * TOK, (h + 1) * TOK)
        head = slice(h * HD, (h + 1) * HD)
        q_n[cut, :] = query[:, head]
        q_t[:, cut] = query[:, head].T

    def forward_step(g):
        @pl.when(needed(z - g, z))
        def _():
            for h in range(2):
                for k in range(2):
                    from_sib(g, k, h).wait_recv()
            forward(g)

    pass_on(2, 1)
    crossed(1, 1)
    forward_step(0)
    pass_on(3, 1)
    crossed(2, 0)
    crossed(2, 1)
    forward_step(1)
    pass_on(4, 1)
    crossed(3, 0)
    crossed(3, 1)
    pass_on(5, 0)
    pass_on(5, 1)
    forward_step(2)
    for g in (4, 5):
        for h in range(2):
            crossed(g, h)
    forward_step(3)
    forward_step(5)
    forward_step(4)

    attended = (num[...] * (1.0 / den[...])).astype(BF)
    delta[...] = jnp.sum(do_t[...].astype(F32) * attended.astype(F32), axis=0, keepdims=True)
    den[...] = 1.0 / den[...]
    for h in range(2):
        att_ref[:, h * HD:(h + 1) * HD] = attended[:, h * TOK:(h + 1) * TOK].T

    def there(where, k):
        return {"seq": where["seq"] + k * across}

    def ring_out(g, k, h, last=False):
        where = there(near if g == 5 else dn, k) if last else dn
        return remote(
            ringout.at[g - 1, k, h], ringin.at[g - 1, k, h], rg_s.at[g - 1, k, h], rg_r.at[g - 1, k, h], where
        )

    def ring_in(g, k, h):
        return remote(ringout.at[g, k, h], ringin.at[g, k, h], rg_s.at[g, k, h], rg_r.at[g, k, h], up)

    def sib_grad(g, k):
        return remote(tosib.at[g, k], fromsib.at[g, k], gs_s.at[g, k], gs_r.at[g, k], sib)

    def contribute(g):
        @pl.when(needed(z - g, z))
        def _():
            k, v, th, w = scores(g)
            prob = w * den[...]
            soft = prob * (dot(v, do_t[...]) - delta[...])
            raw = (soft * ((1.0 - th * th) * (1.0 / 12.0))).astype(BF)
            parts[:, :HD] = dot(raw, q_n[...])
            parts[:, HD:] = dot(prob.astype(BF), do_n[...])
            for q in (1, 0):
                start = (2 * piece(q) + 1 - c) * TOK
                tosib[g, q] = parts[pl.ds(pl.multiple_of(start, TOK), TOK), :].astype(BF)
                sib_grad(g, q).start()
            for q in (1, 0):
                start = (2 * piece(q) + c) * TOK
                mine[g, q] = parts[pl.ds(pl.multiple_of(start, TOK), TOK), :]
            dq_t[...] += dot_tn(k, raw)

    def send_sum(g):
        @pl.when(needed(z - g, z))
        def _():
            for k in (1, 0):
                sib_grad(g, k).wait_recv()
                for h, half in enumerate(halves):
                    mine[g, k, half] += fromsib[g, k, half].astype(F32)

                    @pl.when(up_needs(g))
                    def _():
                        ring_in(g, k, h).wait_recv()
                        mine[g, k, half] += ringin[g, k, h].astype(F32)

                    ringout[g - 1, k, h] = mine[g, k, half].astype(BF)
                    ring_out(g, k, h, g in (1, 5)).start()

    contribute(4)
    send_sum(4)
    contribute(3)
    contribute(2)
    send_sum(3)
    contribute(1)
    contribute(5)
    send_sum(5)
    send_sum(2)
    contribute(0)

    def weight(n, act, lengths):
        grad = grads.at[n]

        def partial(t, j, core):
            return dot(rows_of(act, t * 576 + j * 288 + core * 144, 144)[...], grad[...])

        def sib_copy(t):
            return remote(wsib_out.at[n, t], wsib_in.at[n, t], ws_s.at[n, t], ws_r.at[n, t], sib)

        def target(k, way):
            return lax.rem(z + 8 - lengths[0] + k, 8) if way == 0 else lax.rem(z + 8 + lengths[1] - k, 8)

        def push(*targets):
            for t in targets:
                for j in range(2):
                    wsib_out[n, t, j] = partial(t, j, 1 - c).astype(BF)
                sib_copy(t).start()

        def push_for(k):
            push(*[target(k, way) for way in range(2) if k < lengths[way]])

        def hop(k, way, q):
            out, into = (wd_out, wd_in) if way == 0 else (wu_out, wu_in)
            ss, rr = (wd_s, wd_r) if way == 0 else (wu_s, wu_r)
            where = dn if way == 0 else up
            if k == lengths[way] - 1:
                where = there(where, q)
            return remote(out.at[n, k, q], into.at[n, k, q], ss.at[n, k, q], rr.at[n, k, q], where)

        def hop_step(k, way):
            out, into = (wd_out, wd_in) if way == 0 else (wu_out, wu_in)
            t = target(k, way)
            sib_copy(t).wait_recv()
            for q in (1, 0):
                total = partial(t, piece(q), c) + wsib_in[n, t, piece(q)].astype(F32)
                if k > 0:
                    hop(k - 1, way, q).wait_recv()
                    total += into[n, k - 1, q].astype(F32)
                out[n, k, q] = total.astype(BF)
                hop(k, way, q).start()

        def step(k):
            for way in range(2):
                if k < lengths[way]:
                    hop_step(k, way)

        def x_copy():
            return remote(wx_out.at[n], wx_in.at[n], wx_s.at[n], wx_r.at[n], xp)

        def cross():
            sib_copy(z).wait_recv()
            for q in (1, 0):
                wacc[n, q] = partial(z, piece(q), c) + wsib_in[n, z, piece(q)].astype(F32)
            wx_out[n] = wacc[n, 1].astype(BF)
            x_copy().start()

        def meet():
            x_copy().wait_recv()
            total = wacc[n, 0] + wx_in[n].astype(F32)
            for way, into in enumerate((wd_in, wu_in)):
                for q in range(2):
                    hop(lengths[way] - 1, way, q).wait_recv()
                    total += into[n, lengths[way] - 1, q].astype(F32)
            return total

        def drain():
            for t in range(8):
                sib_copy(t).wait_send()
            for way in range(2):
                for k in range(lengths[way]):
                    for q in range(2):
                        hop(k, way, q).wait_send()
            x_copy().wait_send()

        return push, push_for, step, cross, meet, drain

    push_q, push_q_for, step_q, cross_q, meet_q, drain_q = weight(0, anchor, (3, 4))
    push_kv, push_kv_for, step_kv, cross_kv, meet_kv, drain_kv = weight(1, projected, (4, 3))
    x_rows = remote(xout, xin, xg_s, xg_r, xp)
    sib_grad(0, 1).wait_recv()
    xout[...] = (mine[0, 1] + fromsib[0, 1].astype(F32)).astype(BF)
    x_rows.start()
    for h in range(2):
        grads[0, :, h * HD:(h + 1) * HD] = dq_t[:, h * TOK:(h + 1) * TOK].T.astype(BF)
    push_q_for(0)
    push_q_for(1)
    send_sum(1)
    step_q(0)
    push_q_for(2)
    push_q_for(3)
    push_q(z)
    step_q(1)
    sib_grad(0, 0).wait_recv()
    x_rows.wait_recv()
    mine[0, 0] += fromsib[0, 0].astype(F32) + xin[...].astype(F32)
    for k in (1, 0):
        for h, half in enumerate(halves):
            @pl.when(far_needs)
            def _():
                ring_in(4, k, h).wait_recv()
                mine[0, 0, half] += ringin[4, k, h].astype(F32)

            @pl.when(up_needs(0))
            def _():
                ring_in(0, k, h).wait_recv()
                mine[0, 0, half] += ringin[0, k, h].astype(F32)

    grads[1] = mine[0, 0].astype(BF)
    push_kv_for(0)
    step_kv(0)
    push_kv_for(1)
    push_kv_for(2)
    step_q(2)
    step_kv(1)
    push_kv_for(3)
    push_kv(z)
    step_q(3)
    step_kv(2)
    cross_kv()
    cross_q()
    step_kv(3)
    for half in range(2):
        pairs[pl.ds(half, TOK, stride=2), :] = grads[1, :, half * HD:(half + 1) * HD].astype(F32)
    rows_ref[...] = pairs[:2 * TOK, :].astype(BF)
    gq_ref[...] = meet_q()
    wacc[1, 0] = meet_kv()
    for half in range(2):
        gkv_ref[pl.ds(half, 144, stride=2), :] = wacc[1, 0, :, half * HD:(half + 1) * HD]

    for h in range(2):
        @pl.when(far_needs)
        def _():
            to_far(h).wait_send()

    x_rows.wait_send()
    drain_q()
    drain_kv()
    aug.drain()
    anc.drain()
    pros[0].drain()
    pros[1].drain()
    for k in range(5):
        step(k).wait_send()

    def drained(g, carry):
        @pl.when(needed(z - g, z))
        def _():
            for h in range(2):
                sib_grad(g, h).wait_send()
                to_xp(g, h).wait_send()
                for k in range(2):
                    to_sib(g, k, h).wait_send()

                @pl.when(up_needs(g))
                def _():
                    to_up(g, h).wait_send()

                @pl.when(g > 0)
                def _():
                    for k in range(2):
                        ring_out(g, k, h).wait_send()

        return carry

    lax.fori_loop(0, 6, drained, 0)


def step_call(aug_t, anc_t, pw_t, q_weight, kv_pairs, doc, d_out):
    dma = pltpu.SemaphoreType.DMA
    vmem = pl.BlockSpec(memory_space=pltpu.VMEM)
    hbm = pl.BlockSpec(memory_space=pl.ANY)
    two = lambda n: [dma(n), dma(n)]
    return pl.pallas_call(
        step_kernel,
        out_shape=[
            jax.ShapeDtypeStruct((TOK, 256), BF),
            jax.ShapeDtypeStruct((144, 256), F32),
            jax.ShapeDtypeStruct((288, HD), F32),
            jax.ShapeDtypeStruct((2 * TOK, HD), BF),
        ],
        in_specs=[vmem, vmem, hbm, hbm, hbm, vmem, vmem],
        out_specs=[vmem] * 4,
        scratch_shapes=[
            pltpu.VMEM((2304, TOK), BF), pltpu.VMEM((4608, TOK), BF), pltpu.VMEM((4608, TOK), BF),
            pltpu.VMEM((576, 2304), BF), pltpu.VMEM((4608, 256), BF), pltpu.VMEM((4608, 256), BF),
            pltpu.VMEM((9216, HD), BF), pltpu.VMEM((1152, HD), F32),
            pltpu.VMEM((TOK, 256), F32), pltpu.VMEM((TOK, 256), BF),
            pltpu.VMEM((6, 8, 128), jnp.int32), pltpu.VMEM((5, 8, 128), jnp.int32),
            pltpu.VMEM((32, TOK, 256), BF),
            pltpu.VMEM((512, HD), BF), pltpu.VMEM((HD, 512), BF),
            pltpu.VMEM((512, HD), BF), pltpu.VMEM((HD, 512), BF),
            pltpu.VMEM((HD, 512), F32), pltpu.VMEM((1, 512), F32),
            pltpu.VMEM((1, 512), jnp.int32), pltpu.VMEM((1, 512), jnp.int32),
            pltpu.VMEM((1, 512), F32), pltpu.VMEM((HD, 512), F32),
            pltpu.VMEM((6, 2, TOK, 256), F32), pltpu.VMEM((GROUP, 256), F32),
            pltpu.VMEM((6, 2, TOK, 256), BF), pltpu.VMEM((6, 2, TOK, 256), BF),
            pltpu.VMEM((5, 2, 2, HALF, 256), BF), pltpu.VMEM((5, 2, 2, HALF, 256), BF),
            pltpu.VMEM((TOK, 256), BF), pltpu.VMEM((TOK, 256), BF),
            pltpu.VMEM((2, TOK, 256), BF),
            pltpu.VMEM((2, 8, 2, 144, 256), BF), pltpu.VMEM((2, 8, 2, 144, 256), BF),
            pltpu.VMEM((2, 4, 2, 144, 256), BF), pltpu.VMEM((2, 4, 2, 144, 256), BF),
            pltpu.VMEM((2, 5, 2, 144, 256), BF), pltpu.VMEM((2, 5, 2, 144, 256), BF),
            pltpu.VMEM((2, 144, 256), BF), pltpu.VMEM((2, 144, 256), BF),
            pltpu.VMEM((2, 2, 144, 256), F32),
            dma((3,)), *two((13,)), *two((13,)), *two((2, 13)), *two((5,)),
            *two((5, 2)), *two((6, 2, 2)), *two((6, 2)), *two((6, 2)), *two((5, 2, 2)), *two(()),
            *two((2, 8)), *two((2, 4, 2)), *two((2, 5, 2)), *two((2,)),
        ],
        compiler_params=pltpu.CompilerParams(
            collective_id=1, has_side_effects=True, vmem_limit_bytes=60 * 1024 * 1024
        ),
    )(aug_t, anc_t, pw_t, q_weight, kv_pairs, doc, d_out)


def hand_over(*refs):
    n = len(refs) // 2
    for src, dst in zip(refs[:n], refs[n:]):
        dst[...] = src[...]


def body(anchor, augment, proj_weight, q_weight, kv_weight, doc_ids, d_out):
    results = step_call(
        augment.T, anchor.T, proj_weight.T, q_weight,
        kv_weight.reshape(-1, HD), doc_ids.reshape(1, -1), d_out,
    )
    attended, grad_q, grad_kv, rows = pl.pallas_call(
        hand_over,
        out_shape=[jax.ShapeDtypeStruct(r.shape, r.dtype) for r in results],
        in_specs=[pl.BlockSpec(memory_space=pltpu.VMEM)] * 4,
        out_specs=[pl.BlockSpec(memory_space=pltpu.VMEM)] * 4,
    )(*results)
    return attended, grad_q, grad_kv.reshape(144, 1, 2, HD), rows.reshape(TOK, 1, 2, HD)


def solution(mesh):
    placed = (
        P("seq", "mp"), P("seq", "mp"), P(None, "mp"), P(None, "mp"),
        P(None, "mp", None, None), P("seq"), P("seq", "mp"),
    )
    return jax.shard_map(
        body,
        mesh=mesh,
        in_specs=placed,
        out_specs=(
            P("seq", "mp"), P("seq", "mp"),
            P("seq", "mp", None, None), P("seq", "mp", None, None),
        ),
        check_vma=False,
    )
```
